256 devices in a mesh: lat: 64 (over x_lo, y, z), head: 4 (over x_hi, core).
Axes of the slice: x: 4 (x_hi: 2, x_lo: 2; x = x_hi * 2 + x_lo), y: 4, z: 8, core: 2. Of those that a mesh axis runs over, the one named last changes fastest.
Arguments:
- tokens: bfloat16 [384, 2, 48, 1024], P('lat', None, 'head'), may hold values from -6 to 6
- output_grad: bfloat16 [384, 2, 48, 1024], P('lat', None, 'head'), may hold values from -6 to 6
- region_labels: int32 [384, 2, 48], P('lat', None, 'head'), may hold values from 0 to 3
- qkv_weight: bfloat16 [3, 1024, 1024], P(None, None, 'head'), may hold values from -0.1875 to 0.1875
- out_weight: bfloat16 [1024, 1024], P('head'), may hold values from -0.1875 to 0.1875
- bias_table: float32 [759, 16], P(None, 'head'), may hold values from -5 to 326
- bias_index: int32 [144, 144], replicated, may hold values from 0 to 758
Outputs:
- input_grad: float32 [384, 2, 48, 1024], P('lat', None, 'head')
- qkv_weight_grad: float32 [3, 1024, 1024], P(None, 'lat', 'head')
- out_weight_grad: float32 [1024, 1024], P('head', 'lat')
- bias_grad: float32 [759, 16], P(None, 'head')
The draws below stay inside these ranges and needn't reach their ends.
All inputs are finite; a program needn't handle non-finite values.
Results may differ from the reference program's by a relative error of at most 0.0065.
Values may be sent and summed in bfloat16 or wider, within the bound.
No kernel may reach another device: no remote copies, remote signals or barrier semaphores. Data moves between devices by JAX's collectives and lax.ppermute only.
A program may use at most 64 MiB of HBM per device.

```python
import jax
import jax.numpy as jnp
from jax import lax

D = 1024
HEADS = 16
HD = 64
LON = 48
LEV = 2
WLAT = 6
WLEV = 2
WLON = 12
WT = 144
NB = 759
LAT = 384


def draw_bias_table(key, part):
    key = jax.random.fold_in(key, 7)
    first = jax.random.fold_in(key, 0)
    return jnp.clip(jax.random.normal(first, (NB, HEADS), jnp.float32), -5.0, 5.0)


def touch_ends(values, own_key, smallest, top_value):
    spot = [jax.random.randint(jax.random.fold_in(own_key, axis), (), 0, length) for axis, length in enumerate(values.shape)]
    longest = values.shape.index(max(values.shape))
    next_to = spot[:longest] + [(spot[longest] + 1) % values.shape[longest]] + spot[longest + 1:]
    return values.at[tuple(spot)].set(smallest).at[tuple(next_to)].set(top_value)


def shard_levels(key, extent, cuts, smallest, top_value):
    gain, own = 1.0, jax.random.fold_in(key, 6)
    for position, parts in cuts:
        heights = jnp.exp(jax.random.uniform(jax.random.fold_in(own, position), (parts,), jnp.float32, smallest / len(cuts), top_value / len(cuts)))
        gain = gain * jnp.repeat(heights, extent[position] // parts).reshape([-1 if axis == position else 1 for axis in range(len(extent))])
    return gain


def gaussian(rng, shape, width, reach, cuts=(), dtype=jnp.bfloat16):
    gain = shard_levels(rng, shape, cuts, -0.22, 0.18) if cuts else 1.0
    values = jax.random.normal(rng, shape, jnp.float32) * width * gain
    return jnp.minimum(jnp.maximum(values, -reach), reach).astype(dtype)


def setup_inputs(seed: int = 0) -> dict:
    arg_keys = jax.random.split(jax.random.key(seed), 8)
    tokens = gaussian(arg_keys[0], (LAT, LEV, LON, D), 1.0, 6.0, ((0, 64), (2, 4)))
    output_grad = gaussian(arg_keys[1], (LAT, LEV, LON, D), 1.0, 6.0, ((0, 64), (2, 4)))
    region_labels = touch_ends(jax.random.randint(arg_keys[2], (LAT, LEV, LON), 0, 4), jax.random.fold_in(arg_keys[2], 1), 0, 3).astype(jnp.int32)
    qkv_weight = gaussian(arg_keys[3], (3, D, D), D ** -0.5, 0.1875, ((2, 4),))
    out_weight = gaussian(arg_keys[4], (D, D), D ** -0.5, 0.1875, ((0, 4),))
    bias_table = draw_bias_table(jax.random.fold_in(arg_keys[7], 71), 0)
    bias_index = touch_ends(jax.random.randint(arg_keys[6], (WT, WT), 0, NB), jax.random.fold_in(arg_keys[6], 1), 0, NB - 1).astype(jnp.int32)
    return {"tokens": tokens, "output_grad": output_grad, "region_labels": region_labels, "qkv_weight": qkv_weight, "out_weight": out_weight, "bias_table": bias_table, "bias_index": bias_index}


def to_windows(source):
    channels = source.shape[-1]
    source = source.reshape(WLAT, LEV // WLEV, WLEV, LON // WLON, WLON, channels)
    source = source.transpose(1, 3, 0, 2, 4, 5)
    return source.reshape((LEV // WLEV) * (LON // WLON), WT, channels)


def from_windows(source, channels):
    source = source.reshape(LEV // WLEV, LON // WLON, WLAT, WLEV, WLON, channels)
    return source.transpose(2, 0, 3, 1, 4, 5).reshape(WLAT, LEV, LON, channels)


def band_backward(band_tokens, band_grads, band_labels, qkv_weight, out_weight, bias_table, bias_index):
    features = band_tokens.shape[-1]
    head_width = qkv_weight.shape[2]
    head_count = head_width // HD
    windows = (LEV // WLEV) * (LON // WLON)
    score_scale = HD ** -0.5
    token_rows = band_tokens.reshape(-1, features)
    grad_rows = band_grads.reshape(-1, features)

    def to_heads(source):
        return to_windows(source.reshape(WLAT, LEV, LON, -1)).reshape(windows, WT, head_count, HD).astype(jnp.float32)

    def from_heads(source):
        return from_windows(source.reshape(windows, WT, head_width), head_width).reshape(-1, head_width)

    projected = [jnp.dot(token_rows, qkv_weight[member], preferred_element_type=jnp.float32).astype(jnp.bfloat16) for member in range(3)]
    queries = to_heads(projected[0])
    key_win = to_heads(projected[1])
    values = to_heads(projected[2])
    bias_full = bias_table[bias_index].transpose(2, 0, 1)
    label_win = to_windows(band_labels.reshape(WLAT, LEV, LON, 1))[..., 0]
    same_label = label_win[:, :, None] == label_win[:, None, :]
    scores = jnp.einsum('wihe,wjhe->whij', queries, key_win) * score_scale + bias_full[None]
    scores = jnp.where(same_label[:, None], scores, -jnp.inf)
    row_max = jnp.max(scores, axis=-1, keepdims=True)
    weights_raw = jnp.exp(scores - row_max)
    probabilities = weights_raw / jnp.sum(weights_raw, axis=-1, keepdims=True)
    probs_low = probabilities.astype(jnp.bfloat16)
    attended = jnp.einsum('whij,wjhe->wihe', probs_low.astype(jnp.float32), values).astype(jnp.bfloat16)
    attended_rows = from_heads(attended)
    out_delta = jnp.dot(grad_rows, out_weight.T, preferred_element_type=jnp.float32).astype(jnp.bfloat16)
    grad_out = jnp.dot(attended_rows.T, grad_rows, preferred_element_type=jnp.float32)
    delta_win = to_heads(out_delta)
    prob_grad = jnp.einsum('wihe,wjhe->whij', delta_win, values)
    value_grad = jnp.einsum('whij,wihe->wjhe', probs_low.astype(jnp.float32), delta_win).astype(jnp.bfloat16)
    row_delta = jnp.sum(probabilities * prob_grad, axis=-1, keepdims=True)
    score_grad = probabilities * (prob_grad - row_delta)
    summed = jnp.sum(score_grad, axis=0).transpose(1, 2, 0).reshape(WT * WT, head_count)
    bias_grad = jax.ops.segment_sum(summed, bias_index.reshape(-1), num_segments=NB)
    score_low = score_grad.astype(jnp.bfloat16).astype(jnp.float32)
    query_grad = (jnp.einsum('whij,wjhe->wihe', score_low, key_win) * score_scale).astype(jnp.bfloat16)
    key_grad = (jnp.einsum('whij,wihe->wjhe', score_low, queries) * score_scale).astype(jnp.bfloat16)
    proj_grads = [from_heads(query_grad), from_heads(key_grad), from_heads(value_grad)]
    qkv_grad = jnp.stack([jnp.dot(token_rows.T, proj_grads[member], preferred_element_type=jnp.float32) for member in range(3)])
    return qkv_grad, grad_out, bias_grad, proj_grads


def reference(tokens, output_grad, region_labels, qkv_weight, out_weight, bias_table, bias_index):
    offsets = (-(WLAT // 2), -(WLEV // 2), -(WLON // 2))
    rolled_tokens = jnp.roll(tokens, offsets, axis=(0, 1, 2))
    rolled_grads = jnp.roll(output_grad, offsets, axis=(0, 1, 2))
    rolled_labels = jnp.roll(region_labels, offsets, axis=(0, 1, 2))
    bands = LAT // WLAT
    band_tokens = rolled_tokens.reshape(bands, WLAT, LEV, LON, D)
    band_grads = rolled_grads.reshape(bands, WLAT, LEV, LON, D)
    band_labels = rolled_labels.reshape(bands, WLAT, LEV, LON)

    def advance(totals, inputs):
        qkv_grad, grad_out, bias_grad, proj_grads = band_backward(inputs[0], inputs[1], inputs[2], qkv_weight, out_weight, bias_table, bias_index)
        terms = jnp.zeros((WLAT * LEV * LON, D), jnp.float32)
        for member in range(3):
            terms = terms + jnp.dot(proj_grads[member], qkv_weight[member].T, preferred_element_type=jnp.float32)
        return (totals[0] + qkv_grad, totals[1] + grad_out, totals[2] + bias_grad), terms.reshape(WLAT, LEV, LON, D)

    initial = (jnp.zeros((3, D, D), jnp.float32), jnp.zeros((D, D), jnp.float32), jnp.zeros((NB, HEADS), jnp.float32))
    totals, terms = lax.scan(advance, initial, (band_tokens, band_grads, band_labels))
    input_grad = jnp.roll(terms.reshape(LAT, LEV, LON, D), (WLAT // 2, WLEV // 2, WLON // 2), axis=(0, 1, 2))
    return input_grad, totals[0], totals[1], totals[2]
```

```python
import functools

import jax
import jax.numpy as jnp
import numpy as np
from jax import lax
from jax.experimental import pallas as pl
from jax.experimental.pallas import tpu as pltpu
from jax.sharding import PartitionSpec as P

D = 1024
HD = 64
HEADS = 4
WIDTH = 256
WT = 144
NB = 759
QUAD = 36
ROWS = 80
BLOCKS = 8
ALL = BLOCKS * ROWS
NY = 4
NZ = 8
F32 = jnp.float32
BF16 = jnp.bfloat16
NT = (((1,), (1,)), ((), ()))
TN = (((0,), (0,)), ((), ()))


def sent(x, axis, to):
    size = lax.axis_size(axis)
    return lax.ppermute(x, axis, [(i, to(i)) for i in range(size)])


def lat_of(x, y, z):
    return (x * NY + y % NY) * NZ + z % NZ


def moved(dx, dy, dz):
    def to(i):
        x, y, z = i // (NY * NZ), i // NZ % NY, i % NZ
        return lat_of(x ^ dx, y + dy, z + dz)

    return to


def call(kernel, out, args, flops, moved_bytes, vmem=32):
    return pl.pallas_call(
        kernel,
        out_shape=out,
        scratch_shapes=args,
        compiler_params=pltpu.CompilerParams(vmem_limit_bytes=vmem * 2**20),
        cost_estimate=pl.CostEstimate(flops=flops, bytes_accessed=moved_bytes, transcendentals=0),
    )


def shape(dims, dtype):
    return jax.ShapeDtypeStruct(dims, dtype)


def window_order():
    order = np.zeros((WT, WT), np.float32)
    n = 0
    for rows in range(2):
        for lons in range(2):
            for row in range(3):
                for lon in range(6):
                    for lev in range(2):
                        order[n, (rows * 3 + row) * 24 + (1 - lev) * 12 + lons * 6 + lon] = 1
                        n += 1
    return order


def bias_kernel(table, index, order, bias, places):
    idx = index[...].astype(F32)
    high = jnp.floor(idx * (1.0 / 32.0))
    low = idx - high * 32.0
    perm = order[...]

    def reordered(x):
        y = jnp.dot(perm, x.astype(BF16), preferred_element_type=F32).astype(BF16)
        return lax.dot_general(y, perm, NT, preferred_element_type=F32)

    own = (reordered(high) * 32.0 + reordered(low)).astype(jnp.int32)
    places[...] = own
    for start, stop in ((0, 128), (128, WT)):
        part = own[:, start:stop]
        if stop - start < 128:
            part = jnp.concatenate([part, jnp.zeros((WT, 128 - stop + start), jnp.int32)], axis=1)
        chunk = lax.shift_right_logical(part, 7)
        lane = lax.bitwise_and(part, 127)
        for head in range(HEADS):
            found = jnp.zeros((WT, 128), F32)
            for c in range(6):
                row = jnp.broadcast_to(table[head : head + 1, c * 128 : (c + 1) * 128], (WT, 128))
                got = jnp.take_along_axis(row, lane, axis=1, mode="promise_in_bounds")
                found = jnp.where(chunk == c, got, found)
            bias[head, :, start:stop] = found[:, : stop - start]


def to_windows(rows, wins, own):
    for p in range(4):
        shard = lax.bitwise_xor(own, p)
        before = lax.rem(shard + 3, 4)
        for r in range(2):
            start = (p * 2 + r) * ROWS
            wins[shard, pl.ds(r * 72, QUAD), :] = rows[pl.ds(start, QUAD), :]
            wins[before, pl.ds(r * 72 + QUAD, QUAD), :] = rows[pl.ds(start + QUAD, QUAD), :]


def from_windows(wins, rows, own):
    for p in range(4):
        shard = lax.bitwise_xor(own, p)
        before = lax.rem(shard + 3, 4)
        for r in range(2):
            start = (p * 2 + r) * ROWS
            rows[pl.ds(start, QUAD), :] = wins[shard, pl.ds(r * 72, QUAD), :]
            rows[pl.ds(start + QUAD, QUAD), :] = wins[before, pl.ds(r * 72 + QUAD, QUAD), :]
            rows[pl.ds(start + 72, 8), :] = jnp.zeros((8, rows.shape[1]), F32)


def head_mask(head, rows):
    lane = lax.broadcasted_iota(jnp.int32, (rows, WIDTH), 1)
    return lax.shift_right_logical(lane, 6) == head


def only(head, x):
    return jnp.where(head_mask(head, x.shape[0]), x, 0.0).astype(BF16)


def forward_kernel(t0, t1, t2, t3, t4, t5, t6, t7, weight, bias, tall, qkv, probs, att, rows, wins, labels):
    own = lax.axis_index("head")
    pieces = (t0, t1, t2, t3, t4, t5, t6, t7)
    labels[...] = jnp.zeros_like(labels)
    row = lax.broadcasted_iota(jnp.int32, (8, WIDTH), 0)
    for p in range(4):
        shard = lax.bitwise_xor(own, p)
        before = lax.rem(shard + 3, 4)
        for r in range(2):
            tall[pl.ds((p * 2 + r) * ROWS, ROWS), :] = pieces[p * 2 + r][...]
            marks = pieces[p * 2 + r][64:80, :WIDTH].astype(F32)[8:16]
            labels[shard] += jnp.where(row < 4, marks, 0.0)
            labels[before] += jnp.where(row < 4, pltpu.roll(marks, 4, 0), 0.0)
    for m in range(3):
        rows[...] = jnp.dot(tall[...], weight[m], preferred_element_type=F32).astype(BF16).astype(F32)
        to_windows(rows, wins, own)
        qkv[m] = wins[...].astype(BF16)

    def window(w, _):
        marks = labels[w].astype(BF16)
        same = lax.dot_general(marks, marks, TN, preferred_element_type=F32)[:WT, :WT] > 0.5
        q = qkv[0, w].astype(F32)
        k = qkv[1, w]
        v = qkv[2, w].astype(F32)
        total = jnp.zeros((WT, WIDTH), F32)
        for head in range(HEADS):
            s = lax.dot_general(only(head, q), k, NT, preferred_element_type=F32)
            s = s * 0.125 + bias[head]
            s = jnp.where(same, s, -jnp.inf)
            e = jnp.exp(s - jnp.max(s, axis=1, keepdims=True))
            pr = e / jnp.sum(e, axis=1, keepdims=True)
            probs[w, head] = pr
            total += jnp.dot(pr.astype(BF16), only(head, v), preferred_element_type=F32)
        wins[w] = total
        return 0

    lax.fori_loop(0, 4, window, 0)
    from_windows(wins, rows, own)
    att[...] = rows[...].astype(BF16)


def backward_kernel(g0, g1, g2, g3, g4, g5, g6, g7, wo, qkv, probs, gall, grads, sums, rows, wins, outs):
    own = lax.axis_index("head")
    pieces = (g0, g1, g2, g3, g4, g5, g6, g7)
    for b in range(BLOCKS):
        gall[pl.ds(b * ROWS, ROWS), :] = pieces[b][...]
    delta = lax.dot_general(gall[...], wo[...], NT, preferred_element_type=F32)
    rows[...] = delta.astype(BF16).astype(F32)
    to_windows(rows, wins, own)
    sums[...] = jnp.zeros_like(sums)

    def window(w, _):
        d = wins[w]
        q = qkv[0, w].astype(F32)
        k = qkv[1, w].astype(F32)
        v = qkv[2, w]
        dq = jnp.zeros((WT, WIDTH), F32)
        dk = jnp.zeros((WT, WIDTH), F32)
        dv = jnp.zeros((WT, WIDTH), F32)
        for head in range(HEADS):
            pr = probs[w, head]
            dh = only(head, d)
            dp = lax.dot_general(dh, v, NT, preferred_element_type=F32)
            ds = pr * (dp - jnp.sum(pr * dp, axis=1, keepdims=True))
            sums[head] += ds
            dsb = ds.astype(BF16)
            dv += lax.dot_general(pr.astype(BF16), dh, TN, preferred_element_type=F32)
            dq += jnp.dot(dsb, only(head, k), preferred_element_type=F32)
            dk += lax.dot_general(dsb, only(head, q), TN, preferred_element_type=F32)
        outs[0, w] = dq * 0.125
        outs[1, w] = dk * 0.125
        outs[2, w] = dv
        return 0

    lax.fori_loop(0, 4, window, 0)
    for m in range(3):
        from_windows(outs.at[m], rows, own)
        grads[:, m * WIDTH : (m + 1) * WIDTH] = rows[...].astype(BF16)


def weight_kernel(tall, gall, grads, att, r0, r1, r2, r3):
    y = lax.rem(lax.axis_index("lat") // NZ, NY)
    for d, out in enumerate((r0, r1, r2, r3)):
        to = lax.rem(y + d, NY)
        for x in range(2):
            lanes = pl.ds(pl.multiple_of(x * 512 + to * 128, 128), 128)
            out[x * 128 : (x + 1) * 128, : 3 * WIDTH] = lax.dot_general(
                tall[:, lanes], grads[...], TN, preferred_element_type=F32
            ).astype(BF16)
            out[x * 128 : (x + 1) * 128, 3 * WIDTH :] = lax.dot_general(
                gall[:, lanes], att[...], TN, preferred_element_type=F32
            ).astype(BF16)


def input_kernel(grads, weight, *outs):
    total = jnp.zeros((ALL, D), F32)
    for m in range(3):
        total += lax.dot_general(
            grads[:, m * WIDTH : (m + 1) * WIDTH], weight[m], NT, preferred_element_type=F32
        )
    for b in range(BLOCKS):
        outs[b][...] = total[b * ROWS : b * ROWS + 72].astype(BF16)


def y_sum_kernel(a, b, c, d, *outs):
    z = lax.rem(lax.axis_index("lat"), NZ)
    for step in range(NZ):
        to = lax.rem(z + step, NZ)
        for x in range(2):
            part = pl.ds(pl.multiple_of(x * 128 + to * 16, 16), 16)
            total = a[part, :].astype(F32) + b[part, :].astype(F32)
            total += c[part, :].astype(F32) + d[part, :].astype(F32)
            outs[step][x * 16 : (x + 1) * 16, :] = total.astype(outs[step].dtype)


def z_sum_kernel(a0, a1, a2, a3, a4, a5, a6, a7, kept, other):
    x = lax.axis_index("lat") // (NY * NZ)

    def total(part):
        rows = pl.ds(pl.multiple_of(part * 16, 16), 16)
        y = a0[rows, :]
        for a in (a1, a2, a3, a4, a5, a6, a7):
            y = y + a[rows, :].astype(F32)
        return y

    kept[...] = total(x)
    other[...] = total(1 - x).astype(BF16)


def segment_kernel(values, places, out):
    count = values.shape[1] // 2
    high_row = lax.broadcasted_iota(jnp.int32, (24, 256), 0)
    low_row = lax.broadcasted_iota(jnp.int32, (32, 256), 0)

    def pair(ref_rows):
        return jnp.concatenate([ref_rows[0:1], ref_rows[1:2]], axis=1)

    def step(i, acc):
        idx = pair(places[pl.ds(i * 2, 2), :])
        high = lax.shift_right_logical(idx, 5)
        low = lax.bitwise_and(idx, 31)
        pick = high_row == high
        terms = [jnp.where(pick, pair(values[head, pl.ds(i * 2, 2), :]), 0.0) for head in range(HEADS)]
        a = jnp.concatenate(terms, axis=0)
        top = a.astype(BF16)
        rest = (a - top.astype(F32)).astype(BF16)
        b = (low_row == low).astype(F32).astype(BF16)
        acc = acc + lax.dot_general(top, b, NT, preferred_element_type=F32)
        return acc + lax.dot_general(rest, b, NT, preferred_element_type=F32)

    out[...] = lax.fori_loop(0, count, step, jnp.zeros((96, 32), F32), unroll=3)


def halves(source):
    c = source.shape[-1]
    x = source.transpose(0, 2, 1, 3).reshape(2, 3, 2, 6, 2, c)
    x = x[:, :, ::-1].transpose(0, 2, 1, 3, 4, 5).reshape(2, 72, c)
    return x[0], x[1]


def label_rows(labels, first):
    row = lax.broadcasted_iota(jnp.int32, (8, 72), 0)
    col = lax.broadcasted_iota(jnp.int32, (8, 72), 1)
    hit = (row % 4 == labels[None]) & ((row >= 4) == (col >= QUAD))
    return jnp.pad(hit.astype(BF16), ((0, 0), (first, D - 72 - first)))


def shards(tokens, output_grad, region_labels, qkv_weight, out_weight, bias_table, bias_index):
    core = functools.partial(sent, axis="head", to=lambda i: i ^ 1)
    across = functools.partial(sent, axis="head", to=lambda i: i ^ 2)
    back = functools.partial(sent, axis="lat", to=lambda i: (i - 1) % 64)
    onward = functools.partial(sent, axis="lat", to=lambda i: (i + 1) % 64)

    t_low, t_high = halves(tokens)
    g_low, g_high = halves(output_grad)
    l_low, l_high = halves(region_labels[..., None])
    t_low = jnp.concatenate([t_low, label_rows(l_low[:, 0], 72)])
    t_high = jnp.concatenate([t_high, label_rows(l_high[:, 0], 0)])
    g_low = jnp.pad(g_low, ((0, 8), (0, 0)))
    g_high = jnp.pad(g_high, ((0, 8), (0, 0)))

    def spread(high, low):
        far_high, far_low = across(high), across(low)
        return (high, low, core(high), core(low), far_high, far_low, core(far_high), core(far_low))

    t_low, g_low = back(t_low), back(g_low)
    t_pieces = spread(t_high, t_low)
    g_pieces = spread(g_high, g_low)

    table = jnp.pad(bias_table.T, ((0, 0), (0, 9)))
    bias, places = call(
        bias_kernel, (shape((HEADS, WT, WT), F32), shape((WT, WT), jnp.int32)), (), 2 * 10**7, 10**6
    )(table, bias_index, jnp.asarray(window_order(), BF16))

    tall, qkv, probs, att = call(
        forward_kernel,
        (
            shape((ALL, D), BF16),
            shape((3, 4, WT, WIDTH), BF16),
            shape((4, HEADS, WT, WT), F32),
            shape((ALL, WIDTH), BF16),
        ),
        [pltpu.VMEM((ALL, WIDTH), F32), pltpu.VMEM((4, WT, WIDTH), F32), pltpu.VMEM((4, 8, WIDTH), F32)],
        2 * 10**9,
        10**7,
    )(*t_pieces, qkv_weight, bias)

    gall, grads, sums = call(
        backward_kernel,
        (shape((ALL, D), BF16), shape((ALL, 3 * WIDTH), BF16), shape((HEADS, WT, WT), F32)),
        [pltpu.VMEM((ALL, WIDTH), F32), pltpu.VMEM((4, WT, WIDTH), F32), pltpu.VMEM((3, 4, WT, WIDTH), F32)],
        2 * 10**9,
        10**7,
    )(*g_pieces, out_weight, qkv, probs)

    blocks = call(weight_kernel, (shape((256, D), BF16),) * NY, (), 14 * 10**8, 6 * 10**6)(tall, gall, grads, att)
    got = [blocks[0]] + [sent(blocks[d], "lat", moved(0, d, 0)) for d in range(1, NY)]

    terms = call(input_kernel, (shape((72, D), BF16),) * BLOCKS, (), 10**9, 5 * 10**6)(grads, qkv_weight)

    def add(a, b):
        return a.astype(F32) + b.astype(F32)

    def gathered(r):
        near = add(terms[r], core(terms[2 + r]))
        far = add(terms[4 + r], core(terms[6 + r])).astype(BF16)
        return near + across(far).astype(F32)

    low = onward(gathered(1).astype(BF16)).astype(F32)
    high = gathered(0)

    def rows_of(piece):
        x = piece.reshape(2, 3, 6, 2, D)[::-1].transpose(1, 0, 2, 3, 4).reshape(3, 12, 2, D)
        return x.transpose(0, 2, 1, 3)

    input_grad = jnp.concatenate([rows_of(low), rows_of(high)])

    parts = call(
        y_sum_kernel,
        (shape((32, D), F32),) + (shape((32, D), BF16),) * (NZ - 1),
        (),
        10**6,
        3 * 10**6,
    )(*got)
    got = [parts[0]] + [sent(parts[d], "lat", moved(0, 0, d)) for d in range(1, NZ)]
    kept, other = call(z_sum_kernel, (shape((16, D), F32), shape((16, D), BF16)), (), 10**6, 10**6)(*got)
    weights = kept + sent(other, "lat", moved(1, 0, 0)).astype(F32)
    qkv_grad = weights[:, : 3 * WIDTH].reshape(16, 3, WIDTH).transpose(1, 0, 2)
    out_grad = weights[:, 3 * WIDTH :].T

    values = jnp.concatenate([sums[:, :, :128], sums[:, :, 128:].reshape(HEADS, 18, 128)], axis=1)
    spots = jnp.concatenate([places[:, :128], places[:, 128:].reshape(18, 128)], axis=0)
    bias_sum = call(segment_kernel, shape((96, 32), F32), (), 10**8, 10**6)(values, spots)
    bias_sum = bias_sum.reshape(24, 128)
    bias_sum = sum([sent(bias_sum, "lat", moved(0, 0, d)) for d in range(1, NZ)], bias_sum)
    bias_sum = sum(
        [sent(bias_sum, "lat", moved(x, y, 0)) for x in range(2) for y in range(NY) if x or y], bias_sum
    )
    bias_grad = bias_sum.reshape(HEADS, 768)[:, :NB].T
    return input_grad, qkv_grad, out_grad, bias_grad


def solution(mesh):
    return jax.shard_map(
        shards,
        mesh=mesh,
        in_specs=(
            P("lat", None, "head", None),
            P("lat", None, "head", None),
            P("lat", None, "head"),
            P(None, None, "head"),
            P("head", None),
            P(None, "head"),
            P(),
        ),
        out_specs=(
            P("lat", None, "head", None),
            P(None, "lat", "head"),
            P("head", "lat"),
            P(None, "head"),
        ),
        check_vma=False,
    )
```

```python
import functools

import jax
import jax.numpy as jnp
import numpy as np
from jax import lax
from jax.experimental import pallas as pl
from jax.experimental.pallas import tpu as pltpu
from jax.sharding import PartitionSpec as P

D = 1024
HD = 64
HEADS = 4
WIDTH = 256
WT = 144
NB = 759
ROWS = 80
BLOCKS = 8
ALL = BLOCKS * ROWS
BAND = 576
NY = 4
NZ = 8
F32 = jnp.float32
BF16 = jnp.bfloat16
NT = (((1,), (1,)), ((), ()))
TN = (((0,), (0,)), ((), ()))


def sent(x, axis, to):
    size = lax.axis_size(axis)
    return lax.ppermute(x, axis, [(i, to(i)) for i in range(size)])


def lat_of(x, y, z):
    return (x * NY + y % NY) * NZ + z % NZ


def moved(dx, dy, dz):
    def to(i):
        x, y, z = i // (NY * NZ), i // NZ % NY, i % NZ
        return lat_of(x ^ dx, y + dy, z + dz)

    return to


def paired(dx, dz):
    def to(i):
        x, y, z = i // (NY * NZ), i // NZ % NY, i % NZ
        return lat_of(x ^ dx, y, z ^ dz)

    return to


def call(kernel, out, args, flops, moved_bytes, vmem=16):
    return pl.pallas_call(
        kernel,
        out_shape=out,
        scratch_shapes=args,
        compiler_params=pltpu.CompilerParams(vmem_limit_bytes=vmem * 2**20),
        cost_estimate=pl.CostEstimate(flops=flops, bytes_accessed=moved_bytes, transcendentals=0),
    )


def shape(dims, dtype):
    return jax.ShapeDtypeStruct(dims, dtype)


def window_order():
    order = np.zeros((WT, WT), np.float32)
    for row in range(6):
        for half in range(2):
            for lon in range(6):
                for lev in range(2):
                    n = row * 24 + half * 12 + lon * 2 + lev
                    order[n, row * 24 + (1 - lev) * 12 + (1 - half) * 6 + lon] = 1
    return order


def turned(x, fill):
    x = jnp.concatenate([x[:, 128:], jnp.full((WT, 112), fill, F32)], axis=1)
    x = jnp.concatenate([x, jnp.full((112, 128), fill, F32)], axis=0)
    return jnp.transpose(x)[:16]


def bias_kernel(table, index, order, bias, places, places_end):
    idx = index[...].astype(F32)
    high = jnp.floor(idx * (1.0 / 32.0))
    low = idx - high * 32.0
    perm = order[...]

    def reordered(x):
        y = jnp.dot(perm, x.astype(BF16), preferred_element_type=F32).astype(BF16)
        return lax.dot_general(y, perm, NT, preferred_element_type=F32)

    own_f = reordered(high) * 32.0 + reordered(low)
    own = own_f.astype(jnp.int32)
    places[...] = own[:, :128]
    places_end[...] = turned(own_f, -1.0).astype(jnp.int32)
    for start, stop in ((0, 128), (128, WT)):
        part = own[:, start:stop]
        if stop - start < 128:
            part = jnp.concatenate([part, jnp.zeros((WT, 128 - stop + start), jnp.int32)], axis=1)
        chunk = lax.shift_right_logical(part, 7)
        lane = lax.bitwise_and(part, 127)
        for head in range(HEADS):
            found = jnp.zeros((WT, 128), F32)
            for c in range(6):
                row = jnp.broadcast_to(table[head : head + 1, c * 128 : (c + 1) * 128], (WT, 128))
                got = jnp.take_along_axis(row, lane, axis=1, mode="promise_in_bounds")
                found = jnp.where(chunk == c, got, found)
            bias[head, :, start:stop] = found[:, : stop - start]


def eastern(width):
    row = lax.broadcasted_iota(jnp.int32, (72, width), 0)
    return lax.rem(row, 24) < 12


def to_windows(rows, wins, own, step):
    first = eastern(rows.shape[1])
    for w in range(4):
        near = lax.bitwise_xor(own, w) * (2 * step)
        east = lax.bitwise_xor(own, (w + 1) % 4) * (2 * step)
        for r in range(2):
            a = rows[pl.ds(pl.multiple_of(near + r * step, 8), 72), :]
            b = rows[pl.ds(pl.multiple_of(east + r * step, 8), 72), :]
            wins[w, r * 72 : (r + 1) * 72, :] = jnp.where(first, b, a)


def from_windows(wins, rows, own, step):
    first = eastern(rows.shape[1])
    for s in range(4):
        start = lax.bitwise_xor(own, s) * (2 * step)
        for r in range(2):
            a = wins[s, r * 72 : (r + 1) * 72, :]
            b = wins[(s + 3) % 4, r * 72 : (r + 1) * 72, :]
            at = pl.multiple_of(start + r * step, 8)
            rows[pl.ds(at, 72), :] = jnp.where(first, b, a)
            if step > 72:
                rows[pl.ds(pl.multiple_of(at + 72, 8), step - 72), :] = jnp.zeros((step - 72, rows.shape[1]), F32)


def head_mask(head, rows):
    lane = lax.broadcasted_iota(jnp.int32, (rows, WIDTH), 1)
    return lax.shift_right_logical(lane, 6) == head


def only(head, x):
    return jnp.where(head_mask(head, x.shape[0]), x, 0.0).astype(BF16)


def forward_kernel(t0, t1, t2, t3, t4, t5, t6, t7, weight, bias, tall, qkv, probs, att, rows, wins, labels):
    own = lax.axis_index("head")
    pieces = (t0, t1, t2, t3, t4, t5, t6, t7)
    labels[...] = jnp.zeros_like(labels)
    row = lax.broadcasted_iota(jnp.int32, (8, WIDTH), 0)
    for p in range(4):
        shard = lax.bitwise_xor(own, p)
        before = lax.rem(shard + 3, 4)
        for r in range(2):
            tall[pl.ds((p * 2 + r) * ROWS, ROWS), :] = pieces[p * 2 + r][...]
            marks = pieces[p * 2 + r][64:80, :WIDTH].astype(F32)[8:16]
            labels[shard] += jnp.where(row < 4, marks, 0.0)
            labels[before] += jnp.where(row < 4, pltpu.roll(marks, 4, 0), 0.0)
    for m in range(3):
        rows[...] = jnp.dot(tall[...], weight[m], preferred_element_type=F32).astype(BF16).astype(F32)
        to_windows(rows, wins, own, ROWS)
        qkv[m] = wins[...].astype(BF16)

    def window(w, _):
        marks = labels[w].astype(BF16)
        same = lax.dot_general(marks, marks, TN, preferred_element_type=F32)[:WT, :WT] > 0.5
        q = qkv[0, w].astype(F32)
        k = qkv[1, w]
        v = qkv[2, w].astype(F32)
        total = jnp.zeros((WT, WIDTH), F32)
        for head in range(HEADS):
            s = lax.dot_general(only(head, q), k, NT, preferred_element_type=F32)
            s = s * 0.125 + bias[head]
            s = jnp.where(same, s, -jnp.inf)
            e = jnp.exp(s - jnp.max(s, axis=1, keepdims=True))
            pr = e / jnp.sum(e, axis=1, keepdims=True)
            probs[w, head] = pr
            total += jnp.dot(pr.astype(BF16), only(head, v), preferred_element_type=F32)
        wins[w] = total
        return 0

    lax.fori_loop(0, 4, window, 0)
    band = rows.at[pl.ds(0, BAND), :]
    from_windows(wins, band, own, 72)
    att[...] = band[...].astype(BF16)


def segment_sums(sums, ends, places, places_end):
    low_row = lax.broadcasted_iota(jnp.int32, (128, 256), 0)

    def terms(idx, values):
        high = jnp.right_shift(idx, 7)
        low = lax.bitwise_and(idx, 127)
        a = jnp.concatenate([jnp.where(high == c, values, 0.0) for c in range(6)], axis=0)
        return a.astype(BF16), (low_row == low).astype(F32).astype(BF16)

    def added(acc, pairs):
        a = jnp.concatenate([p[0] for p in pairs], axis=1)
        b = jnp.concatenate([p[1] for p in pairs], axis=1)
        return acc + lax.dot_general(a, b, NT, preferred_element_type=F32)

    def split(block):
        top = block.astype(BF16).astype(F32)
        return top, block - top

    def rows_of(blocks, i):
        return jnp.concatenate([b[0][i : i + 1] for b in blocks] + [b[1][i : i + 1] for b in blocks], axis=0)

    def step(i, acc):
        at = pl.ds(pl.multiple_of(i * 8, 8), 8)
        idx = places[at, :]
        blocks = [split(sums[head, at, :128]) for head in range(HEADS)]
        pairs = []
        for j in range(0, 8, 2):
            both = jnp.concatenate([idx[j : j + 1], idx[j + 1 : j + 2]], axis=1)
            pairs.append(terms(both, jnp.concatenate([rows_of(blocks, j), rows_of(blocks, j + 1)], axis=1)))
        return added(acc, pairs)

    acc = lax.fori_loop(0, 18, step, jnp.zeros((48, 128), F32))

    def last(i, acc):
        at = pl.ds(pl.multiple_of(i * 8, 8), 8)
        idx = places_end[at, :]
        blocks = [split(ends[head, at, :]) for head in range(HEADS)]
        for j in range(0, 8, 4):
            acc = added(acc, [terms(idx[n : n + 1], rows_of(blocks, n)) for n in range(j, j + 4)])
        return acc

    acc = lax.fori_loop(0, 2, last, acc)
    return jnp.concatenate([acc[c * 8 : (c + 1) * 8] for c in range(6)], axis=1)


def bias_total(s):
    return s + pltpu.roll(s, 4, 0)


def bias_rows(total):
    top = total.astype(BF16).astype(F32)
    row = lax.broadcasted_iota(jnp.int32, total.shape, 0)
    both = jnp.where(row < 4, top, total - top)
    return jnp.concatenate([both, jnp.zeros_like(both)], axis=0).astype(BF16)


def backward_kernel(g0, g1, g2, g3, wo, qkv, probs, tall, att, places, places_end, grads, r0, r1, r2, r3, gall, rows, wins, outs, sums, ends):
    own = lax.axis_index("head")
    for p, piece in enumerate((g0, g1, g2, g3)):
        gall[p * WT : (p + 1) * WT, :] = piece[...]
    band = rows.at[pl.ds(0, BAND), :]
    delta = lax.dot_general(gall[...], wo[...], NT, preferred_element_type=F32)
    band[...] = delta.astype(BF16).astype(F32)
    to_windows(band, wins, own, 72)
    sums[...] = jnp.zeros_like(sums)

    def window(w, _):
        d = wins[w]
        q = qkv[0, w].astype(F32)
        k = qkv[1, w].astype(F32)
        v = qkv[2, w]
        dq = jnp.zeros((WT, WIDTH), F32)
        dk = jnp.zeros((WT, WIDTH), F32)
        dv = jnp.zeros((WT, WIDTH), F32)
        for head in range(HEADS):
            pr = probs[w, head]
            dh = only(head, d)
            dp = lax.dot_general(dh, v, NT, preferred_element_type=F32)
            ds = pr * (dp - jnp.sum(pr * dp, axis=1, keepdims=True))
            sums[head] += ds
            dsb = ds.astype(BF16)
            dv += lax.dot_general(pr.astype(BF16), dh, TN, preferred_element_type=F32)
            dq += jnp.dot(dsb, only(head, k), preferred_element_type=F32)
            dk += lax.dot_general(dsb, only(head, q), TN, preferred_element_type=F32)
        outs[0, w] = dq * 0.125
        outs[1, w] = dk * 0.125
        outs[2, w] = dv
        return 0

    lax.fori_loop(0, 4, window, 0)
    for m in range(3):
        from_windows(outs.at[m], rows, own, ROWS)
        grads[:, m * WIDTH : (m + 1) * WIDTH] = rows[...].astype(BF16)

    for head in range(HEADS):
        ends[head] = turned(sums[head], 0.0)
    found = bias_total(segment_sums(sums, ends, places, places_end))
    found = bias_rows(jnp.concatenate([found, jnp.zeros((8, 256), F32)], axis=1))

    y = lax.rem(lax.axis_index("lat") // NZ, NY)
    for d, out in enumerate((r0, r1, r2, r3)):
        to = lax.rem(y + d, NY)
        out[256:272, :] = found
        for x in range(2):
            lanes = pl.ds(pl.multiple_of(x * 512 + to * 128, 128), 128)
            out[x * 128 : (x + 1) * 128, : 3 * WIDTH] = lax.dot_general(
                tall[:, lanes], grads[...], TN, preferred_element_type=F32
            ).astype(BF16)
            out[x * 128 : (x + 1) * 128, 3 * WIDTH :] = lax.dot_general(
                gall[:, lanes], att[...], TN, preferred_element_type=F32
            ).astype(BF16)


def input_kernel(grads, weight, near, far, given):
    total = jnp.zeros((ALL, D), F32)
    for m in range(3):
        total += lax.dot_general(
            grads[:, m * WIDTH : (m + 1) * WIDTH], weight[m], NT, preferred_element_type=F32
        )
    for p, out in enumerate((near.at[...], given.at[:WT, :], far.at[...], given.at[WT:, :])):
        start = p * 2 * ROWS
        both = jnp.concatenate([total[start : start + 72], total[start + ROWS : start + ROWS + 72]], axis=0)
        out[...] = both.astype(BF16)


def stage_rows(parts, rows):
    total = parts[0][rows, :].astype(F32)
    for part in parts[1:]:
        total += part[rows, :].astype(F32)
    return total


def y_sum_kernel(a, b, c, d, *outs):
    parts = (a, b, c, d)
    lat = lax.axis_index("lat")
    x, z = lat // (NY * NZ), lax.rem(lat, 2)
    found = bias_rows(bias_total(stage_rows(parts, pl.ds(256, 16))[:8]))
    for dx in range(2):
        for dz in range(2):
            out = outs[dx * 2 + dz]
            start = lax.bitwise_xor(x, dx) * 128 + lax.bitwise_xor(z, dz) * 16
            for k in range(4):
                rows = pl.ds(pl.multiple_of(start + k * 32, 16), 16)
                out[k * 16 : (k + 1) * 16, :] = stage_rows(parts, rows).astype(BF16)
            out[64:80, :] = found


def pair_sum_kernel(a, b, c, d, *outs):
    parts = (a, b, c, d)
    z = lax.rem(lax.axis_index("lat"), NZ) // 2
    found = bias_rows(bias_total(stage_rows(parts, pl.ds(64, 16))[:8]))
    for e in range(4):
        rows = pl.ds(pl.multiple_of(lax.rem(z + e, 4) * 16, 16), 16)
        outs[e][:16, :] = stage_rows(parts, rows).astype(BF16)
        outs[e][16:, :] = found


def last_sum_kernel(a, b, c, d, qkv, out, bias):
    parts = (a, b, c, d)
    total = stage_rows(parts, pl.ds(0, 16))
    for m in range(3):
        qkv[m] = total[:, m * WIDTH : (m + 1) * WIDTH]
    out[...] = total[:, 3 * WIDTH :]
    bias[...] = bias_total(stage_rows(parts, pl.ds(16, 16))[:8])[:4, :NB]


def halves(source):
    x = source.transpose(0, 2, 1, 3).reshape(2, 72, source.shape[-1])
    return x[0], x[1]


def label_rows(labels, first):
    row = lax.broadcasted_iota(jnp.int32, (8, 72), 0)
    col = lax.broadcasted_iota(jnp.int32, (8, 72), 1)
    hit = (row % 4 == labels[None]) & ((row >= 4) == (col % 24 < 12))
    return jnp.pad(hit.astype(BF16), ((0, 0), (first, D - 72 - first)))


def shards(tokens, output_grad, region_labels, qkv_weight, out_weight, bias_table, bias_index):
    core = functools.partial(sent, axis="head", to=lambda i: i ^ 1)
    across = functools.partial(sent, axis="head", to=lambda i: i ^ 2)
    back = functools.partial(sent, axis="lat", to=lambda i: (i - 1) % 64)
    onward = functools.partial(sent, axis="lat", to=lambda i: (i + 1) % 64)

    t_low, t_high = halves(tokens)
    l_low, l_high = halves(region_labels[..., None])
    t_low = back(jnp.concatenate([t_low, label_rows(l_low[:, 0], 72)]))
    t_high = jnp.concatenate([t_high, label_rows(l_high[:, 0], 0)])
    g_low, g_high = halves(output_grad)
    g = jnp.concatenate([g_high, back(g_low)])

    far_high, far_low, far_g = across(t_high), across(t_low), across(g)
    t_pieces = (t_high, t_low, core(t_high), core(t_low), far_high, far_low, core(far_high), core(far_low))
    g_pieces = (g, core(g), far_g, core(far_g))

    table = jnp.pad(bias_table.T, ((0, 0), (0, 9)))
    bias, places, places_end = call(
        bias_kernel,
        (shape((HEADS, WT, WT), F32), shape((WT, 128), jnp.int32), shape((16, 256), jnp.int32)),
        (),
        2 * 10**7,
        10**6,
    )(table, bias_index, jnp.asarray(window_order(), BF16))

    tall, qkv, probs, att = call(
        forward_kernel,
        (
            shape((ALL, D), BF16),
            shape((3, 4, WT, WIDTH), BF16),
            shape((4, HEADS, WT, WT), F32),
            shape((BAND, WIDTH), BF16),
        ),
        [pltpu.VMEM((ALL, WIDTH), F32), pltpu.VMEM((4, WT, WIDTH), F32), pltpu.VMEM((4, 8, WIDTH), F32)],
        2 * 10**9,
        10**7,
    )(*t_pieces, qkv_weight, bias)

    grads, *blocks = call(
        backward_kernel,
        (shape((ALL, 3 * WIDTH), BF16),) + (shape((272, D), BF16),) * NY,
        [
            pltpu.VMEM((BAND, D), BF16),
            pltpu.VMEM((ALL, WIDTH), F32),
            pltpu.VMEM((4, WT, WIDTH), F32),
            pltpu.VMEM((3, 4, WT, WIDTH), F32),
            pltpu.VMEM((HEADS, WT, WT), F32),
            pltpu.VMEM((HEADS, 16, 256), F32),
        ],
        3 * 10**9,
        10**7,
    )(*g_pieces, out_weight, qkv, probs, tall, att, places, places_end)

    got = [blocks[0]] + [sent(blocks[d], "lat", moved(0, d, 0)) for d in range(1, NY)]
    parts = call(y_sum_kernel, (shape((80, D), BF16),) * 4, (), 10**6, 3 * 10**6, 8)(*got)
    got = [parts[0]] + [sent(parts[d], "lat", paired(d // 2, d % 2)) for d in range(1, 4)]
    parts = call(pair_sum_kernel, (shape((32, D), BF16),) * 4, (), 10**6, 10**6, 8)(*got)
    got = [parts[0]] + [sent(parts[e], "lat", moved(0, 0, 2 * e)) for e in range(1, 4)]
    qkv_grad, out_grad, bias_grad = call(
        last_sum_kernel,
        (shape((3, 16, WIDTH), F32), shape((16, WIDTH), F32), shape((HEADS, NB), F32)),
        (),
        10**6,
        10**6,
        8,
    )(*got)

    near, far, given = call(
        input_kernel, (shape((WT, D), BF16), shape((WT, D), BF16), shape((2 * WT, D), BF16)), (), 10**9, 5 * 10**6
    )(grads, qkv_weight)
    given = core(given)
    far = (far.astype(F32) + given[WT:].astype(F32)).astype(BF16)
    near = near.astype(F32) + given[:WT].astype(F32) + across(far).astype(F32)
    low = onward(near[72:].astype(BF16)).astype(F32)
    input_grad = jnp.concatenate([low, near[:72]]).reshape(6, 12, 2, D).transpose(0, 2, 1, 3)
    return input_grad, qkv_grad, out_grad.T, bias_grad.T


def solution(mesh):
    return jax.shard_map(
        shards,
        mesh=mesh,
        in_specs=(
            P("lat", None, "head", None),
            P("lat", None, "head", None),
            P("lat", None, "head"),
            P(None, None, "head"),
            P("head", None),
            P(None, "head"),
            P(),
        ),
        out_specs=(
            P("lat", None, "head", None),
            P(None, "lat", "head"),
            P("head", "lat"),
            P(None, "head"),
        ),
        check_vma=False,
    )
```

```python
import functools

import jax
import jax.numpy as jnp
import numpy as np
from jax import lax
from jax.experimental import pallas as pl
from jax.experimental.pallas import tpu as pltpu
from jax.sharding import PartitionSpec as P

D = 1024
HD = 64
HEADS = 4
WIDTH = 256
WT = 144
NB = 759
ROWS = 80
BLOCKS = 8
ALL = BLOCKS * ROWS
HALF = 320
NY = 4
NZ = 8
F32 = jnp.float32
BF16 = jnp.bfloat16
NT = (((1,), (1,)), ((), ()))
TN = (((0,), (0,)), ((), ()))


def sent(x, axis, to):
    size = lax.axis_size(axis)
    return lax.ppermute(x, axis, [(i, to(i)) for i in range(size)])


def lat_of(x, y, z):
    return (x * NY + y % NY) * NZ + z % NZ


def moved(dx, dy, dz):
    def to(i):
        x, y, z = i // (NY * NZ), i // NZ % NY, i % NZ
        return lat_of(x ^ dx, y + dy, z + dz)

    return to


def paired(dx, dz):
    def to(i):
        x, y, z = i // (NY * NZ), i // NZ % NY, i % NZ
        return lat_of(x ^ dx, y, z ^ dz)

    return to


def call(kernel, out, args, flops, moved_bytes, vmem=16):
    return pl.pallas_call(
        kernel,
        out_shape=out,
        scratch_shapes=args,
        compiler_params=pltpu.CompilerParams(vmem_limit_bytes=vmem * 2**20),
        cost_estimate=pl.CostEstimate(flops=flops, bytes_accessed=moved_bytes, transcendentals=0),
    )


def shape(dims, dtype):
    return jax.ShapeDtypeStruct(dims, dtype)


def window_order():
    order = np.zeros((WT, WT), np.float32)
    for row in range(6):
        for half in range(2):
            for lon in range(6):
                for lev in range(2):
                    n = row * 24 + half * 12 + lon * 2 + lev
                    order[n, row * 24 + (1 - lev) * 12 + (1 - half) * 6 + lon] = 1
    return order


def turned(x, fill):
    x = jnp.concatenate([x[:, 128:], jnp.full((WT, 112), fill, F32)], axis=1)
    x = jnp.concatenate([x, jnp.full((112, 128), fill, F32)], axis=0)
    return jnp.transpose(x)[:16]


def bias_kernel(table, index, order, bias, places, places_end):
    idx = index[...].astype(F32)
    high = jnp.floor(idx * (1.0 / 32.0))
    low = idx - high * 32.0
    perm = order[...]

    def reordered(x):
        y = jnp.dot(perm, x.astype(BF16), preferred_element_type=F32).astype(BF16)
        return lax.dot_general(y, perm, NT, preferred_element_type=F32)

    own_f = reordered(high) * 32.0 + reordered(low)
    own = own_f.astype(jnp.int32)
    places[...] = own[:, :128]
    places_end[...] = turned(own_f, -1.0).astype(jnp.int32)
    for start, stop in ((0, 128), (128, WT)):
        part = own[:, start:stop]
        if stop - start < 128:
            part = jnp.concatenate([part, jnp.zeros((WT, 128 - stop + start), jnp.int32)], axis=1)
        chunk = lax.shift_right_logical(part, 7)
        lane = lax.bitwise_and(part, 127)
        for head in range(HEADS):
            found = jnp.zeros((WT, 128), F32)
            for c in range(6):
                row = jnp.broadcast_to(table[head : head + 1, c * 128 : (c + 1) * 128], (WT, 128))
                got = jnp.take_along_axis(row, lane, axis=1, mode="promise_in_bounds")
                found = jnp.where(chunk == c, got, found)
            bias[head, :, start:stop] = found[:, : stop - start]


def eastern(width):
    row = lax.broadcasted_iota(jnp.int32, (72, width), 0)
    return lax.rem(row, 24) < 12


def to_windows(rows, wins, own):
    first = eastern(rows.shape[1])
    for w in range(4):
        near = lax.bitwise_xor(own, w) * ROWS
        east = lax.bitwise_xor(own, (w + 1) % 4) * ROWS
        for r in range(2):
            a = rows[pl.ds(pl.multiple_of(near + r * HALF, 8), 72), :]
            b = rows[pl.ds(pl.multiple_of(east + r * HALF, 8), 72), :]
            wins[w, r * 72 : (r + 1) * 72, :] = jnp.where(first, b, a)


def from_windows(wins, rows, own):
    first = eastern(rows.shape[1])
    for s in range(4):
        start = lax.bitwise_xor(own, s) * ROWS
        for r in range(2):
            a = wins[s, r * 72 : (r + 1) * 72, :]
            b = wins[(s + 3) % 4, r * 72 : (r + 1) * 72, :]
            at = pl.multiple_of(start + r * HALF, 8)
            rows[pl.ds(at, 72), :] = jnp.where(first, b, a)
            rows[pl.ds(pl.multiple_of(at + 72, 8), 8), :] = jnp.zeros((8, rows.shape[1]), F32)


def head_mask(head, rows):
    lane = lax.broadcasted_iota(jnp.int32, (rows, WIDTH), 1)
    return lax.shift_right_logical(lane, 6) == head


def only(head, x):
    return jnp.where(head_mask(head, x.shape[0]), x, 0.0).astype(BF16)


def stacked(pieces, tall, gall):
    for p, piece in enumerate(pieces):
        tall[p * ROWS : (p + 1) * ROWS, :] = piece[:ROWS, :]
        gall[p * ROWS : (p + 1) * ROWS, :] = piece[ROWS:, :]


def projected(m, tall, gall, weight, wo):
    if m < 3:
        y = jnp.dot(tall[...], weight[m], preferred_element_type=F32)
    else:
        y = lax.dot_general(gall[...], wo[...], NT, preferred_element_type=F32)
    return y.astype(BF16)


def early_kernel(m0, m1, m2, m3, weight, wo, proj, tall, gall):
    stacked((m0, m1, m2, m3), tall, gall)
    for m in range(4):
        proj[m] = projected(m, tall, gall, weight, wo)


def segment_sums(sums, ends, places, places_end):
    low_row = lax.broadcasted_iota(jnp.int32, (128, 256), 0)

    def terms(idx, values):
        high = jnp.right_shift(idx, 7)
        low = lax.bitwise_and(idx, 127)
        a = jnp.concatenate([jnp.where(high == c, values, 0.0) for c in range(6)], axis=0)
        return a.astype(BF16), (low_row == low).astype(F32).astype(BF16)

    def added(acc, pairs):
        a = jnp.concatenate([p[0] for p in pairs], axis=1)
        b = jnp.concatenate([p[1] for p in pairs], axis=1)
        return acc + lax.dot_general(a, b, NT, preferred_element_type=F32)

    def split(block):
        top = block.astype(BF16).astype(F32)
        return top, block - top

    def rows_of(blocks, i):
        return jnp.concatenate([b[0][i : i + 1] for b in blocks] + [b[1][i : i + 1] for b in blocks], axis=0)

    def step(i, acc):
        at = pl.ds(pl.multiple_of(i * 8, 8), 8)
        idx = places[at, :]
        blocks = [split(sums[head, at, :128]) for head in range(HEADS)]
        pairs = []
        for j in range(0, 8, 2):
            both = jnp.concatenate([idx[j : j + 1], idx[j + 1 : j + 2]], axis=1)
            pairs.append(terms(both, jnp.concatenate([rows_of(blocks, j), rows_of(blocks, j + 1)], axis=1)))
        return added(acc, pairs)

    acc = lax.fori_loop(0, 18, step, jnp.zeros((48, 128), F32))

    def last(i, acc):
        at = pl.ds(pl.multiple_of(i * 8, 8), 8)
        idx = places_end[at, :]
        blocks = [split(ends[head, at, :]) for head in range(HEADS)]
        for j in range(0, 8, 4):
            acc = added(acc, [terms(idx[n : n + 1], rows_of(blocks, n)) for n in range(j, j + 4)])
        return acc

    acc = lax.fori_loop(0, 2, last, acc)
    return jnp.concatenate([acc[c * 8 : (c + 1) * 8] for c in range(6)], axis=1)


def bias_rows(x):
    top = x.astype(BF16).astype(F32)
    return jnp.concatenate([top, x - top], axis=0).astype(BF16)


def band_kernel(*refs):
    highs, lows = refs[:4], refs[4:8]
    weight, wo, bias, early, places, places_end, grads = refs[8:15]
    ways, pairs = refs[15:19], refs[19:23]
    tall, gall, qkv, rows, wins, outs, sums, ends, att, labels, full = refs[23:]
    own = lax.axis_index("head")
    labels[...] = jnp.zeros_like(labels)
    row = lax.broadcasted_iota(jnp.int32, (8, WIDTH), 0)
    for p in range(4):
        shard = lax.bitwise_xor(own, p)
        before = lax.rem(shard + 3, 4)
        marks = highs[p][64:80, :WIDTH].astype(F32)[8:16] + lows[p][64:80, :WIDTH].astype(F32)[8:16]
        labels[shard] += jnp.where(row < 4, marks, 0.0)
        labels[before] += jnp.where(row < 4, pltpu.roll(marks, 4, 0), 0.0)
    stacked(highs, tall.at[:HALF, :], gall.at[:HALF, :])
    stacked(lows, tall.at[HALF:, :], gall.at[HALF:, :])
    for m in range(4):
        rows[:HALF, :] = early[m].astype(F32)
        rows[HALF:, :] = projected(m, tall.at[HALF:, :], gall.at[HALF:, :], weight, wo).astype(F32)
        to_windows(rows, wins, own)
        if m < 3:
            qkv[m] = wins[...].astype(BF16)
    sums[...] = jnp.zeros_like(sums)

    def window(w, _):
        marks = labels[w].astype(BF16)
        same = lax.dot_general(marks, marks, TN, preferred_element_type=F32)[:WT, :WT] > 0.5
        q = qkv[0, w].astype(F32)
        k = qkv[1, w]
        v = qkv[2, w]
        d = wins[w]
        k_f = k.astype(F32)
        v_f = v.astype(F32)
        total = jnp.zeros((WT, WIDTH), F32)
        dq = jnp.zeros((WT, WIDTH), F32)
        dk = jnp.zeros((WT, WIDTH), F32)
        dv = jnp.zeros((WT, WIDTH), F32)
        for head in range(HEADS):
            qh = only(head, q)
            dh = only(head, d)
            s = lax.dot_general(qh, k, NT, preferred_element_type=F32)
            dp = lax.dot_general(dh, v, NT, preferred_element_type=F32)
            s = s * 0.125 + bias[head]
            s = jnp.where(same, s, -jnp.inf)
            e = jnp.exp(s - jnp.max(s, axis=1, keepdims=True))
            pr = e / jnp.sum(e, axis=1, keepdims=True)
            prb = pr.astype(BF16)
            total += jnp.dot(prb, only(head, v_f), preferred_element_type=F32)
            dv += lax.dot_general(prb, dh, TN, preferred_element_type=F32)
            ds = pr * (dp - jnp.sum(pr * dp, axis=1, keepdims=True))
            sums[head] += ds
            dsb = ds.astype(BF16)
            dq += jnp.dot(dsb, only(head, k_f), preferred_element_type=F32)
            dk += lax.dot_general(dsb, qh, TN, preferred_element_type=F32)
        outs[0, w] = dq * 0.125
        outs[1, w] = dk * 0.125
        outs[2, w] = dv
        outs[3, w] = total
        return 0

    lax.fori_loop(0, 4, window, 0)
    for m in range(4):
        from_windows(outs.at[m], rows, own)
        if m < 3:
            grads[:, m * WIDTH : (m + 1) * WIDTH] = rows[...].astype(BF16)
    att[...] = rows[...].astype(BF16)

    for head in range(HEADS):
        ends[head] = turned(sums[head], 0.0)
    found = segment_sums(sums, ends, places, places_end)
    found = found + pltpu.roll(found, 4, 0)
    rest = jnp.concatenate([found[:, 512:], jnp.zeros((8, 256), F32)], axis=1)
    found = bias_rows(jnp.where(lax.broadcasted_iota(jnp.int32, (8, 512), 0) < 4, found[:, :512], rest))

    full[:, : 3 * WIDTH] = lax.dot_general(tall[...], grads[...], TN, preferred_element_type=F32).astype(BF16)
    full[:, 3 * WIDTH :] = lax.dot_general(gall[...], att[...], TN, preferred_element_type=F32).astype(BF16)
    lat = lax.axis_index("lat")
    x, y, z = lat // (NY * NZ), lax.rem(lat // NZ, NY), lax.rem(lat, 2)
    for d, out in enumerate(ways):
        out[256:272, :] = found
        for half in range(2):
            at = pl.ds(pl.multiple_of(half * 512 + lax.rem(y + d, NY) * 128, 128), 128)
            out[half * 128 : (half + 1) * 128, :] = full[at, :512]
    for i, out in enumerate(pairs):
        start = lax.bitwise_xor(x, i // 2) * 512 + lax.bitwise_xor(z, i % 2) * 16
        for b in range(16):
            at = pl.ds(pl.multiple_of(start + (b // 4) * 128 + (b % 4) * 32, 16), 16)
            out[b * 16 : (b + 1) * 16, :] = full[at, 512:]


def input_kernel(grads, weight, near, far, given):
    total = jnp.zeros((ALL, D), F32)
    for m in range(3):
        total += lax.dot_general(
            grads[:, m * WIDTH : (m + 1) * WIDTH], weight[m], NT, preferred_element_type=F32
        )
    for p, out in enumerate((near.at[...], given.at[:WT, :], far.at[...], given.at[WT:, :])):
        start = p * ROWS
        both = jnp.concatenate([total[start : start + 72], total[start + HALF : start + HALF + 72]], axis=0)
        out[...] = both.astype(BF16)


def stage_rows(parts, rows):
    total = parts[0][rows, :].astype(F32)
    for part in parts[1:]:
        total += part[rows, :].astype(F32)
    return total


def second_kernel(*refs):
    ways, pairs, to_pairs, to_ways = refs[:4], refs[4:8], refs[8:12], refs[12:]
    lat = lax.axis_index("lat")
    x, y, z = lat // (NY * NZ), lax.rem(lat // NZ, NY), lax.rem(lat, 2)
    found = stage_rows(ways, pl.ds(256, 16))
    found = bias_rows(found[:8] + found[8:])
    for i, out in enumerate(to_pairs):
        start = lax.bitwise_xor(x, i // 2) * 128 + lax.bitwise_xor(z, i % 2) * 16
        for k in range(4):
            rows = pl.ds(pl.multiple_of(start + k * 32, 16), 16)
            out[k * 16 : (k + 1) * 16, :] = stage_rows(ways, rows).astype(BF16)
        out[64:80, :] = found
    for d, out in enumerate(to_ways):
        rows = pl.ds(pl.multiple_of(lax.rem(y + d, NY) * 64, 64), 64)
        out[...] = stage_rows(pairs, rows).astype(BF16)


def third_kernel(*refs):
    pairs, ways, outs = refs[:4], refs[4:8], refs[8:]
    z = lax.rem(lax.axis_index("lat"), NZ) // 2
    found = stage_rows(pairs, pl.ds(64, 16))
    found = bias_rows(found[:8] + found[8:])
    for e, out in enumerate(outs):
        rows = pl.ds(pl.multiple_of(lax.rem(z + e, 4) * 16, 16), 16)
        out[:16, :512] = stage_rows(pairs, rows).astype(BF16)
        out[:16, 512:] = stage_rows(ways, rows).astype(BF16)
        out[16:, :512] = found
        out[16:, 512:] = jnp.zeros_like(found)


def last_kernel(a, b, c, d, qkv, out, bias):
    parts = (a, b, c, d)
    total = stage_rows(parts, pl.ds(0, 16))
    for m in range(3):
        qkv[m] = total[:, m * WIDTH : (m + 1) * WIDTH]
    out[...] = total[:, 3 * WIDTH :]
    found = stage_rows(parts, pl.ds(16, 16))
    found = found[:8, :512] + found[8:, :512]
    bias[...] = jnp.concatenate([found[:4], found[4:]], axis=1)[:, :NB]


def label_rows(labels, first):
    row = lax.broadcasted_iota(jnp.int32, (8, 72), 0)
    col = lax.broadcasted_iota(jnp.int32, (8, 72), 1)
    labels = labels.transpose(0, 2, 1).reshape(1, 72)
    hit = (row % 4 == labels) & ((row >= 4) == (col % 24 < 12))
    return jnp.pad(hit.astype(BF16), ((0, 0), (first, D - 72 - first)))


def shards(tokens, output_grad, region_labels, qkv_weight, out_weight, bias_table, bias_index):
    core = functools.partial(sent, axis="head", to=lambda i: i ^ 1)
    across = functools.partial(sent, axis="head", to=lambda i: i ^ 2)
    back = functools.partial(sent, axis="lat", to=lambda i: (i - 1) % 64)
    onward = functools.partial(sent, axis="lat", to=lambda i: (i + 1) % 64)

    def message(r):
        rows = slice(3 - 3 * r, 6 - 3 * r)
        t, g = (x[rows].transpose(0, 2, 1, 3).reshape(72, D) for x in (tokens, output_grad))
        marks = label_rows(region_labels[rows], 72 * r)
        return jnp.concatenate([t, marks, g, jnp.zeros((8, D), BF16)])

    high = message(0)
    low = back(message(1))
    far_high = across(high)
    highs = (high, core(high), far_high, core(far_high))

    table = jnp.pad(bias_table.T, ((0, 0), (0, 9)))
    bias, places, places_end = call(
        bias_kernel,
        (shape((HEADS, WT, WT), F32), shape((WT, 128), jnp.int32), shape((16, 256), jnp.int32)),
        (),
        2 * 10**7,
        10**6,
    )(table, bias_index, jnp.asarray(window_order(), BF16))

    low, bias, places, places_end = lax.optimization_barrier((low, bias, places, places_end))
    far_low = across(low)
    early = call(
        early_kernel,
        shape((4, HALF, WIDTH), BF16),
        [pltpu.VMEM((HALF, D), BF16), pltpu.VMEM((HALF, D), BF16)],
        10**9,
        5 * 10**6,
        8,
    )(*highs, qkv_weight, out_weight)
    far_low, early = lax.optimization_barrier((far_low, early))
    lows = (low, core(low), far_low, core(far_low))

    grads, *blocks = call(
        band_kernel,
        (shape((ALL, 3 * WIDTH), BF16),) + (shape((272, 512), BF16),) * 4 + (shape((256, 512), BF16),) * 4,
        [
            pltpu.VMEM((ALL, D), BF16),
            pltpu.VMEM((ALL, D), BF16),
            pltpu.VMEM((3, 4, WT, WIDTH), BF16),
            pltpu.VMEM((ALL, WIDTH), F32),
            pltpu.VMEM((4, WT, WIDTH), F32),
            pltpu.VMEM((4, 4, WT, WIDTH), F32),
            pltpu.VMEM((HEADS, WT, WT), F32),
            pltpu.VMEM((HEADS, 16, 256), F32),
            pltpu.VMEM((ALL, WIDTH), BF16),
            pltpu.VMEM((4, 8, WIDTH), F32),
            pltpu.VMEM((D, D), BF16),
        ],
        3 * 10**9,
        10**7,
        24,
    )(*highs, *lows, qkv_weight, out_weight, bias, early, places, places_end)

    def by_y(parts):
        return [parts[0]] + [sent(parts[d], "lat", moved(0, d, 0)) for d in range(1, 4)]

    def by_pair(parts):
        return [parts[0]] + [sent(parts[d], "lat", paired(d // 2, d % 2)) for d in range(1, 4)]

    ways, pairs = by_y(blocks[:4]), by_pair(blocks[4:])

    near, far, given = call(
        input_kernel, (shape((WT, D), BF16), shape((WT, D), BF16), shape((2 * WT, D), BF16)), (), 10**9, 5 * 10**6
    )(grads, qkv_weight)
    given = core(given)
    far = (far.astype(F32) + given[WT:].astype(F32)).astype(BF16)
    parts = call(
        second_kernel, (shape((80, 512), BF16),) * 4 + (shape((64, 512), BF16),) * 4, (), 10**6, 3 * 10**6, 8
    )(*ways, *pairs)
    far, parts = lax.optimization_barrier((far, parts))
    more = across(far)
    pairs, ways = by_pair(parts[:4]), by_y(parts[4:])
    pairs, ways, more = lax.optimization_barrier((pairs, ways, more))
    parts = call(third_kernel, (shape((32, D), BF16),) * 4, (), 10**6, 10**6, 8)(*pairs, *ways)
    got = [parts[0]] + [sent(parts[e], "lat", moved(0, 0, 2 * e)) for e in range(1, 4)]
    near = near.astype(F32) + given[:WT].astype(F32) + more.astype(F32)
    low = onward(near[72:].astype(BF16)).astype(F32)
    input_grad = jnp.concatenate([low, near[:72]]).reshape(6, 12, 2, D).transpose(0, 2, 1, 3)
    got, input_grad = lax.optimization_barrier((got, input_grad))
    qkv_grad, out_grad, bias_grad = call(
        last_kernel,
        (shape((3, 16, WIDTH), F32), shape((16, WIDTH), F32), shape((HEADS, NB), F32)),
        (),
        10**6,
        10**6,
        8,
    )(*got)
    return input_grad, qkv_grad, out_grad.T, bias_grad.T


def solution(mesh):
    return jax.shard_map(
        shards,
        mesh=mesh,
        in_specs=(
            P("lat", None, "head", None),
            P("lat", None, "head", None),
            P("lat", None, "head"),
            P(None, None, "head"),
            P("head", None),
            P(None, "head"),
            P(),
        ),
        out_specs=(
            P("lat", None, "head", None),
            P(None, "lat", "head"),
            P("head", "lat"),
            P(None, "head"),
        ),
        check_vma=False,
    )
```

```python
import functools

import jax
import jax.numpy as jnp
import numpy as np
from jax import lax
from jax.experimental import pallas as pl
from jax.experimental.pallas import tpu as pltpu
from jax.sharding import PartitionSpec as P

D = 1024
HD = 64
HEADS = 4
WIDTH = 256
WT = 144
NB = 759
ROWS = 80
BLOCKS = 8
ALL = BLOCKS * ROWS
HALF = 320
NY = 4
NZ = 8
F32 = jnp.float32
BF16 = jnp.bfloat16
NT = (((1,), (1,)), ((), ()))
TN = (((0,), (0,)), ((), ()))


def sent(x, axis, to):
    size = lax.axis_size(axis)
    return lax.ppermute(x, axis, [(i, to(i)) for i in range(size)])


def lat_of(x, y, z):
    return (x * NY + y % NY) * NZ + z % NZ


def moved(dx, dy, dz):
    def to(i):
        x, y, z = i // (NY * NZ), i // NZ % NY, i % NZ
        return lat_of(x ^ dx, y + dy, z + dz)

    return to


def paired(dx, dz):
    def to(i):
        x, y, z = i // (NY * NZ), i // NZ % NY, i % NZ
        return lat_of(x ^ dx, y, z ^ dz)

    return to


def call(kernel, out, args, flops, moved_bytes, vmem=16):
    return pl.pallas_call(
        kernel,
        out_shape=out,
        scratch_shapes=args,
        compiler_params=pltpu.CompilerParams(vmem_limit_bytes=vmem * 2**20),
        cost_estimate=pl.CostEstimate(flops=flops, bytes_accessed=moved_bytes, transcendentals=0),
    )


def shape(dims, dtype):
    return jax.ShapeDtypeStruct(dims, dtype)


def window_order():
    order = np.zeros((WT, WT), np.float32)
    for row in range(6):
        for half in range(2):
            for lon in range(6):
                for lev in range(2):
                    n = row * 24 + half * 12 + lon * 2 + lev
                    order[n, row * 24 + (1 - lev) * 12 + (1 - half) * 6 + lon] = 1
    return order


def turned(x, fill):
    x = jnp.concatenate([x[:, 128:], jnp.full((WT, 112), fill, F32)], axis=1)
    x = jnp.concatenate([x, jnp.full((112, 128), fill, F32)], axis=0)
    return jnp.transpose(x)[:16]


def bias_kernel(table, index, order, bias, highs, lows):
    idx = index[...].astype(F32)
    high = jnp.floor(idx * (1.0 / 32.0))
    low = idx - high * 32.0
    perm = order[...]

    def reordered(x):
        y = jnp.dot(perm, x.astype(BF16), preferred_element_type=F32).astype(BF16)
        return lax.dot_general(y, perm, NT, preferred_element_type=F32)

    own_f = reordered(high) * 32.0 + reordered(low)
    own = own_f.astype(jnp.int32)
    ends = turned(own_f, -1.0).astype(jnp.int32)

    def found(head, places):
        chunk = lax.shift_right_logical(places, 7)
        lane = lax.bitwise_and(places, 127)
        total = jnp.zeros(places.shape, F32)
        for c in range(6):
            row = jnp.broadcast_to(table[head : head + 1, c * 128 : (c + 1) * 128], places.shape)
            got = jnp.take_along_axis(row, lane, axis=1, mode="promise_in_bounds")
            total = jnp.where(chunk == c, got, total)
        return total

    for head in range(HEADS):
        bias[head, :, :128] = found(head, own[:, :128])
        rest = jnp.concatenate([found(head, ends[:, :128]), found(head, ends[:, 128:])], axis=1)
        rest = jnp.transpose(jnp.concatenate([rest, jnp.zeros((112, 256), F32)], axis=0))
        bias[head, :, 128:] = rest[:WT, :16]

    high_row = lax.broadcasted_iota(jnp.int32, (16, 256), 0)
    low_row = lax.broadcasted_iota(jnp.int32, (48, 256), 0)
    for n in range(88):
        if n < 72:
            places = jnp.concatenate([own[2 * n : 2 * n + 1, :128], own[2 * n + 1 : 2 * n + 2, :128]], axis=1)
        else:
            places = ends[n - 72 : n - 71]
        upper = jnp.floor(places.astype(F32) * (1.0 / 48.0) + 0.01).astype(jnp.int32)
        highs[n] = (high_row == upper).astype(F32).astype(BF16)
        lows[n] = (low_row == places - upper * 48).astype(F32).astype(BF16)


def eastern(width):
    row = lax.broadcasted_iota(jnp.int32, (72, width), 0)
    return lax.rem(row, 24) < 12


def to_windows(rows, wins, own):
    first = eastern(rows.shape[1])
    for w in range(4):
        near = lax.bitwise_xor(own, w) * ROWS
        east = lax.bitwise_xor(own, (w + 1) % 4) * ROWS
        for r in range(2):
            a = rows[pl.ds(pl.multiple_of(near + r * HALF, 8), 72), :]
            b = rows[pl.ds(pl.multiple_of(east + r * HALF, 8), 72), :]
            wins[w, r * 72 : (r + 1) * 72, :] = jnp.where(first, b, a)


def from_windows(wins, rows, own):
    first = eastern(rows.shape[1])
    for s in range(4):
        start = lax.bitwise_xor(own, s) * ROWS
        for r in range(2):
            a = wins[s, r * 72 : (r + 1) * 72, :]
            b = wins[(s + 3) % 4, r * 72 : (r + 1) * 72, :]
            at = pl.multiple_of(start + r * HALF, 8)
            rows[pl.ds(at, 72), :] = jnp.where(first, b, a)
            rows[pl.ds(pl.multiple_of(at + 72, 8), 8), :] = jnp.zeros((8, rows.shape[1]), F32)


def by_head(x):
    lane = lax.shift_right_logical(lax.broadcasted_iota(jnp.int32, (1, WIDTH), 1), 6)
    return jnp.concatenate([x * (lane == head).astype(F32).astype(BF16) for head in range(HEADS)], axis=0)


def own_columns(x):
    first = lax.broadcasted_iota(jnp.int32, (WT, 128), 1) < HD
    part = [x[head * WT : (head + 1) * WT, head // 2 * 128 : head // 2 * 128 + 128] for head in range(HEADS)]
    return jnp.concatenate([jnp.where(first, part[0], part[1]), jnp.where(first, part[2], part[3])], axis=1)


def stacked(pieces, tall, gall):
    for p, piece in enumerate(pieces):
        tall[p * ROWS : (p + 1) * ROWS, :] = piece[:ROWS, :]
        gall[p * ROWS : (p + 1) * ROWS, :] = piece[ROWS:, :]


def projected(m, tall, gall, weight, wo):
    if m < 3:
        y = jnp.dot(tall[...], weight[m], preferred_element_type=F32)
    else:
        y = lax.dot_general(gall[...], wo[...], NT, preferred_element_type=F32)
    return y.astype(BF16)


def early_kernel(m0, m1, m2, m3, weight, wo, proj, tall, gall):
    stacked((m0, m1, m2, m3), tall, gall)
    for m in range(4):
        proj[m] = projected(m, tall, gall, weight, wo)


def segment_sums(sums, highs, lows):
    total = jnp.zeros((64, 48), F32)
    ends = [turned(sums[head], 0.0) for head in range(HEADS)]
    for n in range(88):
        rows = []
        for head in range(HEADS):
            if n < 72:
                row = jnp.concatenate([sums[head, 2 * n : 2 * n + 1, :128], sums[head, 2 * n + 1 : 2 * n + 2, :128]], axis=1)
            else:
                row = ends[head][n - 72 : n - 71]
            rows.append(jnp.broadcast_to(row, (16, 256)).astype(BF16) * highs[n])
        total += lax.dot_general(jnp.concatenate(rows, axis=0), lows[n], NT, preferred_element_type=F32)
    return total


def bias_rows(x):
    top = x.astype(BF16).astype(F32)
    x = top + pltpu.roll(x - top, 64, 1)
    return jnp.concatenate([x[head * 16 : (head + 1) * 16] for head in range(HEADS)], axis=1).astype(BF16)


def bias_sum(s):
    x = jnp.concatenate([s[:, head * 128 : (head + 1) * 128] for head in range(HEADS)], axis=0)
    lane = lax.broadcasted_iota(jnp.int32, x.shape, 1)
    return jnp.where(lane < 64, x + pltpu.roll(x, 64, 1), 0.0)


def band_kernel(*refs):
    highs, lows = refs[:4], refs[4:8]
    weight, wo, bias, early, high_rows, low_rows, grads = refs[8:15]
    ways, pairs = refs[15:19], refs[19:23]
    tall, gall, qkv, rows, wins, outs, sums, att, labels, full = refs[23:]
    own = lax.axis_index("head")
    labels[...] = jnp.zeros_like(labels)
    row = lax.broadcasted_iota(jnp.int32, (8, WIDTH), 0)
    for p in range(4):
        shard = lax.bitwise_xor(own, p)
        before = lax.rem(shard + 3, 4)
        marks = highs[p][64:80, :WIDTH].astype(F32)[8:16] + lows[p][64:80, :WIDTH].astype(F32)[8:16]
        labels[shard] += jnp.where(row < 4, marks, 0.0)
        labels[before] += jnp.where(row < 4, pltpu.roll(marks, 4, 0), 0.0)
    stacked(highs, tall.at[:HALF, :], gall.at[:HALF, :])
    stacked(lows, tall.at[HALF:, :], gall.at[HALF:, :])
    for m in range(4):
        rows[:HALF, :] = early[m].astype(F32)
        rows[HALF:, :] = projected(m, tall.at[HALF:, :], gall.at[HALF:, :], weight, wo).astype(F32)
        to_windows(rows, wins, own)
        if m < 3:
            qkv[m] = wins[...].astype(BF16)
    for w in range(4):
        marks = labels[w].astype(BF16)
        same = lax.dot_general(marks, marks, TN, preferred_element_type=F32)[:WT, :WT] > 0.5
        same = jnp.where(same, 0.0, -jnp.inf)
        q = by_head(qkv[0, w] * jnp.asarray(0.125, BF16))
        k = qkv[1, w]
        v = qkv[2, w]
        d = by_head(wins[w].astype(BF16))
        s = lax.dot_general(q, k, NT, preferred_element_type=F32).reshape(HEADS, WT, WT)
        dp = lax.dot_general(d, v, NT, preferred_element_type=F32).reshape(HEADS, WT, WT)
        s = s + bias[...] + same[None]
        e = jnp.exp(s - jnp.max(s, axis=2, keepdims=True))
        pr = e * (1.0 / jnp.sum(e, axis=2, keepdims=True))
        ds = pr * (dp - jnp.sum(pr * dp, axis=2, keepdims=True))
        sums[...] = ds if w == 0 else sums[...] + ds
        prb = pr.astype(BF16).reshape(HEADS * WT, WT)
        dsb = ds.astype(BF16).reshape(HEADS * WT, WT)
        outs[0, w] = own_columns(jnp.dot(dsb, k, preferred_element_type=F32)) * 0.125
        outs[1, w] = lax.dot_general(dsb, q, TN, preferred_element_type=F32)
        outs[2, w] = lax.dot_general(prb, d, TN, preferred_element_type=F32)
        outs[3, w] = own_columns(jnp.dot(prb, v, preferred_element_type=F32))
    for m in range(4):
        from_windows(outs.at[m], rows, own)
        if m < 3:
            grads[:, m * WIDTH : (m + 1) * WIDTH] = rows[...].astype(BF16)
    att[...] = rows[...].astype(BF16)

    found = segment_sums(sums, high_rows, low_rows)
    found = bias_rows(jnp.concatenate([found, jnp.zeros((64, 80), F32)], axis=1))

    full[:, : 3 * WIDTH] = lax.dot_general(tall[...], grads[...], TN, preferred_element_type=F32).astype(BF16)
    full[:, 3 * WIDTH :] = lax.dot_general(gall[...], att[...], TN, preferred_element_type=F32).astype(BF16)
    lat = lax.axis_index("lat")
    x, y, z = lat // (NY * NZ), lax.rem(lat // NZ, NY), lax.rem(lat, 2)
    for d, out in enumerate(ways):
        out[256:272, :] = found
        for half in range(2):
            at = pl.ds(pl.multiple_of(half * 512 + lax.rem(y + d, NY) * 128, 128), 128)
            out[half * 128 : (half + 1) * 128, :] = full[at, :512]
    for i, out in enumerate(pairs):
        start = lax.bitwise_xor(x, i // 2) * 512 + lax.bitwise_xor(z, i % 2) * 16
        for b in range(16):
            at = pl.ds(pl.multiple_of(start + (b // 4) * 128 + (b % 4) * 32, 16), 16)
            out[b * 16 : (b + 1) * 16, :] = full[at, 512:]


def input_kernel(grads, weight, near, far, given):
    total = jnp.zeros((ALL, D), F32)
    for m in range(3):
        total += lax.dot_general(
            grads[:, m * WIDTH : (m + 1) * WIDTH], weight[m], NT, preferred_element_type=F32
        )
    for p, out in enumerate((near.at[...], given.at[:WT, :], far.at[...], given.at[WT:, :])):
        start = p * ROWS
        both = jnp.concatenate([total[start : start + 72], total[start + HALF : start + HALF + 72]], axis=0)
        out[...] = both.astype(BF16)


def stage_rows(parts, rows):
    total = parts[0][rows, :].astype(F32)
    for part in parts[1:]:
        total += part[rows, :].astype(F32)
    return total


def second_kernel(*refs):
    ways, pairs, to_pairs, to_ways = refs[:4], refs[4:8], refs[8:12], refs[12:]
    lat = lax.axis_index("lat")
    x, y, z = lat // (NY * NZ), lax.rem(lat // NZ, NY), lax.rem(lat, 2)
    found = stage_rows(ways, pl.ds(256, 16))
    found = bias_rows(bias_sum(found))
    for i, out in enumerate(to_pairs):
        start = lax.bitwise_xor(x, i // 2) * 128 + lax.bitwise_xor(z, i % 2) * 16
        for k in range(4):
            rows = pl.ds(pl.multiple_of(start + k * 32, 16), 16)
            out[k * 16 : (k + 1) * 16, :] = stage_rows(ways, rows).astype(BF16)
        out[64:80, :] = found
    for d, out in enumerate(to_ways):
        rows = pl.ds(pl.multiple_of(lax.rem(y + d, NY) * 64, 64), 64)
        out[...] = stage_rows(pairs, rows).astype(BF16)


def third_kernel(*refs):
    pairs, ways, outs = refs[:4], refs[4:8], refs[8:]
    z = lax.rem(lax.axis_index("lat"), NZ) // 2
    found = stage_rows(pairs, pl.ds(64, 16))
    found = bias_rows(bias_sum(found))
    for e, out in enumerate(outs):
        rows = pl.ds(pl.multiple_of(lax.rem(z + e, 4) * 16, 16), 16)
        out[:16, :512] = stage_rows(pairs, rows).astype(BF16)
        out[:16, 512:] = stage_rows(ways, rows).astype(BF16)
        out[16:, :512] = found
        out[16:, 512:] = jnp.zeros_like(found)


def last_kernel(a, b, c, d, qkv, out, bias):
    parts = (a, b, c, d)
    total = stage_rows(parts, pl.ds(0, 16))
    for m in range(3):
        qkv[m] = total[:, m * WIDTH : (m + 1) * WIDTH]
    out[...] = total[:, 3 * WIDTH :]
    found = bias_sum(stage_rows(parts, pl.ds(16, 16))[:, :512])
    for head in range(HEADS):
        for c in range(16):
            stop = min(c * 48 + 48, NB)
            bias[head : head + 1, c * 48 : stop] = found[head * 16 + c : head * 16 + c + 1, : stop - c * 48]


def label_rows(labels, first):
    row = lax.broadcasted_iota(jnp.int32, (8, 72), 0)
    col = lax.broadcasted_iota(jnp.int32, (8, 72), 1)
    labels = labels.transpose(0, 2, 1).reshape(1, 72)
    hit = (row % 4 == labels) & ((row >= 4) == (col % 24 < 12))
    return jnp.pad(hit.astype(BF16), ((0, 0), (first, D - 72 - first)))


def shards(tokens, output_grad, region_labels, qkv_weight, out_weight, bias_table, bias_index):
    core = functools.partial(sent, axis="head", to=lambda i: i ^ 1)
    across = functools.partial(sent, axis="head", to=lambda i: i ^ 2)
    back = functools.partial(sent, axis="lat", to=lambda i: (i - 1) % 64)
    onward = functools.partial(sent, axis="lat", to=lambda i: (i + 1) % 64)

    def message(r):
        rows = slice(3 - 3 * r, 6 - 3 * r)
        t, g = (x[rows].transpose(0, 2, 1, 3).reshape(72, D) for x in (tokens, output_grad))
        marks = label_rows(region_labels[rows], 72 * r)
        return jnp.concatenate([t, marks, g, jnp.zeros((8, D), BF16)])

    high = message(0)
    low = back(message(1))
    far_high = across(high)
    table = jnp.pad(bias_table.T, ((0, 0), (0, 9)))
    bias, high_rows, low_rows = call(
        bias_kernel,
        (shape((HEADS, WT, WT), F32), shape((88, 16, 256), BF16), shape((88, 48, 256), BF16)),
        (),
        10**8,
        4 * 10**6,
    )(table, bias_index, jnp.asarray(window_order(), BF16))
    high, bias, high_rows, low_rows = lax.optimization_barrier((high, bias, high_rows, low_rows))
    near_high = core(high)
    far_low = across(low)
    far_high, low = lax.optimization_barrier((far_high, low))
    highs = (high, near_high, far_high, core(far_high))

    early = call(
        early_kernel,
        shape((4, HALF, WIDTH), BF16),
        [pltpu.VMEM((HALF, D), BF16), pltpu.VMEM((HALF, D), BF16)],
        10**9,
        5 * 10**6,
        8,
    )(*highs, qkv_weight, out_weight)
    far_low, early = lax.optimization_barrier((far_low, early))
    lows = (low, core(low), far_low, core(far_low))

    grads, *blocks = call(
        band_kernel,
        (shape((ALL, 3 * WIDTH), BF16),) + (shape((272, 512), BF16),) * 4 + (shape((256, 512), BF16),) * 4,
        [
            pltpu.VMEM((ALL, D), BF16),
            pltpu.VMEM((ALL, D), BF16),
            pltpu.VMEM((3, 4, WT, WIDTH), BF16),
            pltpu.VMEM((ALL, WIDTH), F32),
            pltpu.VMEM((4, WT, WIDTH), F32),
            pltpu.VMEM((4, 4, WT, WIDTH), F32),
            pltpu.VMEM((HEADS, WT, WT), F32),
            pltpu.VMEM((ALL, WIDTH), BF16),
            pltpu.VMEM((4, 8, WIDTH), F32),
            pltpu.VMEM((D, D), BF16),
        ],
        3 * 10**9,
        10**7,
        24,
    )(*highs, *lows, qkv_weight, out_weight, bias, early, high_rows, low_rows)

    def by_y(parts):
        return [parts[0]] + [sent(parts[d], "lat", moved(0, d, 0)) for d in range(1, 4)]

    def by_pair(parts):
        return [parts[0]] + [sent(parts[d], "lat", paired(d // 2, d % 2)) for d in range(1, 4)]

    ways, pairs = by_y(blocks[:4]), by_pair(blocks[4:])

    grads, near_pair = lax.optimization_barrier((grads, pairs[1]))
    pairs[1] = near_pair
    near, far, given = call(
        input_kernel, (shape((WT, D), BF16), shape((WT, D), BF16), shape((2 * WT, D), BF16)), (), 10**9, 5 * 10**6
    )(grads, qkv_weight)
    given = core(given)
    far = (far.astype(F32) + given[WT:].astype(F32)).astype(BF16)
    parts = call(
        second_kernel, (shape((80, 512), BF16),) * 4 + (shape((64, 512), BF16),) * 4, (), 10**6, 3 * 10**6, 8
    )(*ways, *pairs)
    far, parts = lax.optimization_barrier((far, parts))
    more = across(far)
    pairs, ways = by_pair(parts[:4]), by_y(parts[4:])
    pairs, ways, more = lax.optimization_barrier((pairs, ways, more))
    parts = call(third_kernel, (shape((32, D), BF16),) * 4, (), 10**6, 10**6, 8)(*pairs, *ways)
    got = [parts[0]] + [sent(parts[e], "lat", moved(0, 0, 2 * e)) for e in range(1, 4)]
    near = near.astype(F32) + given[:WT].astype(F32) + more.astype(F32)
    low = onward(near[72:].astype(BF16)).astype(F32)
    input_grad = jnp.concatenate([low, near[:72]]).reshape(6, 12, 2, D).transpose(0, 2, 1, 3)
    got, input_grad = lax.optimization_barrier((got, input_grad))
    qkv_grad, out_grad, bias_grad = call(
        last_kernel,
        (shape((3, 16, WIDTH), F32), shape((16, WIDTH), F32), shape((HEADS, NB), F32)),
        (),
        10**6,
        10**6,
        8,
    )(*got)
    return input_grad, qkv_grad, out_grad.T, bias_grad.T


def solution(mesh):
    return jax.shard_map(
        shards,
        mesh=mesh,
        in_specs=(
            P("lat", None, "head", None),
            P("lat", None, "head", None),
            P("lat", None, "head"),
            P(None, None, "head"),
            P("head", None),
            P(None, "head"),
            P(),
        ),
        out_specs=(
            P("lat", None, "head", None),
            P(None, "lat", "head"),
            P("head", "lat"),
            P(None, "head"),
        ),
        check_vma=False,
    )
```

```python
import functools

import jax
import jax.numpy as jnp
import numpy as np
from jax import lax
from jax.experimental import pallas as pl
from jax.experimental.pallas import tpu as pltpu
from jax.sharding import PartitionSpec as P

D = 1024
HD = 64
HEADS = 4
WIDTH = 256
WT = 144
NB = 759
ROWS = 80
BLOCKS = 8
ALL = BLOCKS * ROWS
HALF = 320
NY = 4
NZ = 8
F32 = jnp.float32
BF16 = jnp.bfloat16
NT = (((1,), (1,)), ((), ()))
TN = (((0,), (0,)), ((), ()))


def sent(x, axis, to):
    size = lax.axis_size(axis)
    return lax.ppermute(x, axis, [(i, to(i)) for i in range(size)])


def lat_of(x, y, z):
    return (x * NY + y % NY) * NZ + z % NZ


def moved(dx, dy, dz):
    def to(i):
        x, y, z = i // (NY * NZ), i // NZ % NY, i % NZ
        return lat_of(x ^ dx, y + dy, z + dz)

    return to


def paired(dx, dz):
    def to(i):
        x, y, z = i // (NY * NZ), i // NZ % NY, i % NZ
        return lat_of(x ^ dx, y, z ^ dz)

    return to


def call(kernel, out, args, flops, moved_bytes, vmem=16):
    return pl.pallas_call(
        kernel,
        out_shape=out,
        scratch_shapes=args,
        compiler_params=pltpu.CompilerParams(vmem_limit_bytes=vmem * 2**20),
        cost_estimate=pl.CostEstimate(flops=flops, bytes_accessed=moved_bytes, transcendentals=0),
    )


def shape(dims, dtype):
    return jax.ShapeDtypeStruct(dims, dtype)


def window_order():
    order = np.zeros((WT, WT), np.float32)
    for row in range(6):
        for half in range(2):
            for lon in range(6):
                for lev in range(2):
                    n = row * 24 + half * 12 + lon * 2 + lev
                    order[n, row * 24 + (1 - lev) * 12 + (1 - half) * 6 + lon] = 1
    return order


def turned(x, fill):
    x = jnp.concatenate([x[:, 128:], jnp.full((WT, 112), fill, F32)], axis=1)
    x = jnp.concatenate([x, jnp.full((112, 128), fill, F32)], axis=0)
    return jnp.transpose(x)[:16]


def bias_kernel(table, index, order, bias, highs, lows):
    idx = index[...].astype(F32)
    high = jnp.floor(idx * (1.0 / 32.0))
    low = idx - high * 32.0
    perm = order[...]

    def reordered(x):
        y = jnp.dot(perm, x.astype(BF16), preferred_element_type=F32).astype(BF16)
        return lax.dot_general(y, perm, NT, preferred_element_type=F32)

    own_f = reordered(high) * 32.0 + reordered(low)
    own = own_f.astype(jnp.int32)
    ends = turned(own_f, -1.0).astype(jnp.int32)

    def found(head, places):
        chunk = lax.shift_right_logical(places, 7)
        lane = lax.bitwise_and(places, 127)
        total = jnp.zeros(places.shape, F32)
        for c in range(6):
            row = jnp.broadcast_to(table[head : head + 1, c * 128 : (c + 1) * 128], places.shape)
            got = jnp.take_along_axis(row, lane, axis=1, mode="promise_in_bounds")
            total = jnp.where(chunk == c, got, total)
        return total

    for head in range(HEADS):
        bias[head, :, :128] = found(head, own[:, :128])
        rest = jnp.concatenate([found(head, ends[:, :128]), found(head, ends[:, 128:])], axis=1)
        rest = jnp.transpose(jnp.concatenate([rest, jnp.zeros((112, 256), F32)], axis=0))
        bias[head, :, 128:] = rest[:WT, :16]

    high_row = lax.broadcasted_iota(jnp.int32, (16, 256), 0)
    low_row = lax.broadcasted_iota(jnp.int32, (48, 256), 0)
    for n in range(88):
        if n < 72:
            places = jnp.concatenate([own[2 * n : 2 * n + 1, :128], own[2 * n + 1 : 2 * n + 2, :128]], axis=1)
        else:
            places = ends[n - 72 : n - 71]
        upper = jnp.floor(places.astype(F32) * (1.0 / 48.0) + 0.01).astype(jnp.int32)
        highs[n] = (high_row == upper).astype(F32).astype(BF16)
        lows[n] = (low_row == places - upper * 48).astype(F32).astype(BF16)


def eastern(width):
    row = lax.broadcasted_iota(jnp.int32, (72, width), 0)
    return lax.rem(row, 24) < 12


def to_windows(rows, wins, own):
    first = eastern(rows.shape[1])
    for w in range(4):
        near = lax.bitwise_xor(own, w) * 2 * ROWS
        east = lax.bitwise_xor(own, (w + 1) % 4) * 2 * ROWS
        for r in range(2):
            a = rows[pl.ds(pl.multiple_of(near + r * ROWS, 8), 72), :]
            b = rows[pl.ds(pl.multiple_of(east + r * ROWS, 8), 72), :]
            wins[w, r * 72 : (r + 1) * 72, :] = jnp.where(first, b, a)


def from_windows(wins, rows, own):
    first = eastern(rows.shape[1])
    for s in range(4):
        start = lax.bitwise_xor(own, s) * 2 * ROWS
        for r in range(2):
            a = wins[s, r * 72 : (r + 1) * 72, :]
            b = wins[(s + 3) % 4, r * 72 : (r + 1) * 72, :]
            at = pl.multiple_of(start + r * ROWS, 8)
            rows[pl.ds(at, 72), :] = jnp.where(first, b, a)
            rows[pl.ds(pl.multiple_of(at + 72, 8), 8), :] = jnp.zeros((8, rows.shape[1]), F32)


def by_head(x):
    lane = lax.shift_right_logical(lax.broadcasted_iota(jnp.int32, (1, WIDTH), 1), 6)
    return jnp.concatenate([x * (lane == head).astype(F32).astype(BF16) for head in range(HEADS)], axis=0)


def own_columns(x):
    first = lax.broadcasted_iota(jnp.int32, (WT, 128), 1) < HD
    part = [x[head * WT : (head + 1) * WT, head // 2 * 128 : head // 2 * 128 + 128] for head in range(HEADS)]
    return jnp.concatenate([jnp.where(first, part[0], part[1]), jnp.where(first, part[2], part[3])], axis=1)


def stacked(pieces, tall, gall):
    for p, piece in enumerate(pieces):
        tall[p * ROWS : (p + 1) * ROWS, :] = piece[:ROWS, :]
        rows = jnp.concatenate([piece[ROWS:, :].astype(F32), jnp.zeros((8, D), F32)], axis=0)
        gall[p * ROWS : (p + 1) * ROWS, :] = rows.astype(BF16)


def projected(m, tall, gall, weight, wo):
    if m < 3:
        y = jnp.dot(tall[...], weight[m], preferred_element_type=F32)
    else:
        y = lax.dot_general(gall[...], wo[...], NT, preferred_element_type=F32)
    return y.astype(BF16)


def early_kernel(m0, m1, m2, m3, weight, wo, proj, tall, gall):
    stacked((m0, m1, m2, m3), tall, gall)
    for m in range(4):
        proj[m] = projected(m, tall, gall, weight, wo)


def segment_sums(sums, highs, lows):
    total = jnp.zeros((64, 48), F32)
    ends = [turned(sums[head], 0.0) for head in range(HEADS)]
    for n in range(88):
        rows = []
        for head in range(HEADS):
            if n < 72:
                row = jnp.concatenate([sums[head, 2 * n : 2 * n + 1, :128], sums[head, 2 * n + 1 : 2 * n + 2, :128]], axis=1)
            else:
                row = ends[head][n - 72 : n - 71]
            rows.append(jnp.broadcast_to(row, (16, 256)).astype(BF16) * highs[n])
        total += lax.dot_general(jnp.concatenate(rows, axis=0), lows[n], NT, preferred_element_type=F32)
    return total


def bias_rows(x):
    top = x.astype(BF16).astype(F32)
    x = top + pltpu.roll(x - top, 64, 1)
    return jnp.concatenate([x[head * 16 : (head + 1) * 16] for head in range(HEADS)], axis=1).astype(BF16)


def bias_sum(s):
    x = jnp.concatenate([s[:, head * 128 : (head + 1) * 128] for head in range(HEADS)], axis=0)
    lane = lax.broadcasted_iota(jnp.int32, x.shape, 1)
    return jnp.where(lane < 64, x + pltpu.roll(x, 64, 1), 0.0)


def folded(rows):
    rest = jnp.concatenate([rows[:, 384:], jnp.zeros((16, 256), BF16)], axis=1)
    return jnp.concatenate([rows[:, :384], rest], axis=0)


def unfolded(rows):
    return jnp.concatenate([rows[:16], rows[16:, :128]], axis=1)


def band_kernel(*refs):
    pieces = refs[:8]
    weight, wo, bias, early, high_rows, low_rows, grads = refs[8:15]
    ways, sides, pairs = refs[15:19], refs[19:21], refs[21:23]
    tall, gall, qkv, rows, wins, outs, sums, att, labels, full = refs[23:]
    own = lax.axis_index("head")
    labels[...] = jnp.zeros_like(labels)
    row = lax.broadcasted_iota(jnp.int32, (8, WIDTH), 0)
    for p in range(4):
        shard = lax.bitwise_xor(own, p)
        before = lax.rem(shard + 3, 4)
        marks = sum(pieces[2 * p + r][64:80, :WIDTH].astype(F32)[8:16] for r in range(2))
        labels[shard] += jnp.where(row < 4, marks, 0.0)
        labels[before] += jnp.where(row < 4, pltpu.roll(marks, 4, 0), 0.0)
    stacked(pieces[:4], tall.at[:HALF, :], gall.at[:HALF, :])
    stacked(pieces[4:], tall.at[HALF:, :], gall.at[HALF:, :])
    for m in range(4):
        rows[:HALF, :] = early[m].astype(F32)
        rows[HALF:, :] = projected(m, tall.at[HALF:, :], gall.at[HALF:, :], weight, wo).astype(F32)
        to_windows(rows, wins, own)
        if m < 3:
            qkv[m] = wins[...].astype(BF16)
    for w in range(4):
        marks = labels[w].astype(BF16)
        same = lax.dot_general(marks, marks, TN, preferred_element_type=F32)[:WT, :WT] > 0.5
        same = jnp.where(same, 0.0, -jnp.inf)
        q = by_head(qkv[0, w] * jnp.asarray(0.125, BF16))
        k = qkv[1, w]
        v = qkv[2, w]
        d = by_head(wins[w].astype(BF16))
        s = lax.dot_general(q, k, NT, preferred_element_type=F32).reshape(HEADS, WT, WT)
        dp = lax.dot_general(d, v, NT, preferred_element_type=F32).reshape(HEADS, WT, WT)
        s = s + bias[...] + same[None]
        e = jnp.exp(s - jnp.max(s, axis=2, keepdims=True))
        pr = e * (1.0 / jnp.sum(e, axis=2, keepdims=True))
        ds = pr * (dp - jnp.sum(pr * dp, axis=2, keepdims=True))
        sums[...] = ds if w == 0 else sums[...] + ds
        prb = pr.astype(BF16).reshape(HEADS * WT, WT)
        dsb = ds.astype(BF16).reshape(HEADS * WT, WT)
        outs[0, w] = own_columns(jnp.dot(dsb, k, preferred_element_type=F32)) * 0.125
        outs[1, w] = lax.dot_general(dsb, q, TN, preferred_element_type=F32)
        outs[2, w] = lax.dot_general(prb, d, TN, preferred_element_type=F32)
        outs[3, w] = own_columns(jnp.dot(prb, v, preferred_element_type=F32))
    for m in range(4):
        from_windows(outs.at[m], rows, own)
        if m < 3:
            grads[:, m * WIDTH : (m + 1) * WIDTH] = rows[...].astype(BF16)
    att[...] = rows[...].astype(BF16)

    found = segment_sums(sums, high_rows, low_rows)
    found = bias_rows(jnp.concatenate([found, jnp.zeros((64, 80), F32)], axis=1))

    full[:, : 3 * WIDTH] = lax.dot_general(tall[...], grads[...], TN, preferred_element_type=F32).astype(BF16)
    full[:, 3 * WIDTH :] = lax.dot_general(gall[...], att[...], TN, preferred_element_type=F32).astype(BF16)
    lat = lax.axis_index("lat")
    x, y, z = lat // (NY * NZ), lax.rem(lat // NZ, NY), lax.rem(lat, 2)
    for d, out in enumerate(ways):
        for half in range(2):
            at = pl.ds(pl.multiple_of(half * 512 + lax.rem(y + d, NY) * 128, 128), 128)
            out[half * 128 : (half + 1) * 128, :] = full[at, :384]
    for i, out in enumerate(sides):
        out[:512, :] = full[pl.ds(pl.multiple_of(lax.bitwise_xor(x, i) * 512, 512), 512), 384:768]
        out[512:, :] = folded(found)
    for i, out in enumerate(pairs):
        for b in range(32):
            at = pl.ds(pl.multiple_of(lax.bitwise_xor(z, i) * 16 + (b // 4) * 128 + (b % 4) * 32, 16), 16)
            out[b * 16 : (b + 1) * 16, :] = full[at, 768:]


def input_kernel(grads, weight, near, far, given):
    total = jnp.zeros((ALL, D), F32)
    for m in range(3):
        total += lax.dot_general(
            grads[:, m * WIDTH : (m + 1) * WIDTH], weight[m], NT, preferred_element_type=F32
        )
    for p, out in enumerate((near.at[...], given.at[:WT, :], far.at[...], given.at[WT:, :])):
        start = p * 2 * ROWS
        both = jnp.concatenate([total[start : start + 72], total[start + ROWS : start + ROWS + 72]], axis=0)
        out[...] = both.astype(BF16)


def stage_rows(parts, rows, columns=slice(None)):
    total = parts[0][rows, columns].astype(F32)
    for part in parts[1:]:
        total += part[rows, columns].astype(F32)
    return total


def place():
    lat = lax.axis_index("lat")
    return lat // (NY * NZ), lax.rem(lat // NZ, NY), lax.rem(lat, NZ)


def second_kernel(*refs):
    ways, sides, pairs, mixed, to_ways = refs[:4], refs[4:6], refs[6:8], refs[8:10], refs[10:]
    x, y, _ = place()
    for i, out in enumerate(mixed):
        to = lax.bitwise_xor(x, i)
        first = stage_rows(ways, pl.ds(pl.multiple_of(to * 128, 128), 128)).astype(BF16)
        out[:, :256] = stage_rows(pairs, pl.ds(pl.multiple_of(to * 256, 256), 256)).astype(BF16)
        out[:128, 256:] = first[:, :256]
        out[128:, 256:384] = first[:, 256:]
        out[128:, 384:] = jnp.zeros((128, 128), BF16)
    found = folded(bias_rows(bias_sum(unfolded(stage_rows(sides, pl.ds(512, 32))))))
    for d, out in enumerate(to_ways):
        out[:128, :] = stage_rows(sides, pl.ds(pl.multiple_of(lax.rem(y + d, NY) * 128, 128), 128)).astype(BF16)
        out[128:, :] = found


def third_kernel(*refs):
    mixed, ways, to_pairs, to_ways = refs[:2], refs[2:6], refs[6:8], refs[8:]
    _, y, z = place()
    found = bias_rows(bias_sum(unfolded(stage_rows(ways, pl.ds(128, 32)))))
    for i, out in enumerate(to_pairs):
        start = lax.bitwise_xor(lax.rem(z, 2), i) * 16
        for k in range(4):
            rows = pl.ds(pl.multiple_of(start + k * 32, 16), 16)
            late = pl.ds(pl.multiple_of(start + k * 32 + 128, 16), 16)
            here = slice(k * 16, (k + 1) * 16)
            out[here, :256] = stage_rows(mixed, rows, slice(256, 512)).astype(BF16)
            out[here, 256:384] = stage_rows(mixed, late, slice(256, 384)).astype(BF16)
            out[here, 384:] = stage_rows(ways, rows).astype(BF16)
        out[64:, :512] = found
        out[64:, 512:] = jnp.zeros((16, 256), BF16)
    for d, out in enumerate(to_ways):
        rows = pl.ds(pl.multiple_of(lax.rem(y + d, NY) * 64, 64), 64)
        out[...] = stage_rows(mixed, rows, slice(0, 256)).astype(BF16)


def fourth_kernel(*refs):
    pairs, ways, outs = refs[:2], refs[2:6], refs[6:]
    z = place()[2] // 2
    found = bias_rows(bias_sum(stage_rows(pairs, pl.ds(64, 16), slice(0, 512))))
    for e, out in enumerate(outs):
        rows = pl.ds(pl.multiple_of(lax.rem(z + e, 4) * 16, 16), 16)
        out[:16, :768] = stage_rows(pairs, rows).astype(BF16)
        out[:16, 768:] = stage_rows(ways, rows).astype(BF16)
        out[16:, :512] = found
        out[16:, 512:] = jnp.zeros_like(found)


def last_kernel(a, b, c, d, qkv, out, bias):
    parts = (a, b, c, d)
    total = stage_rows(parts, pl.ds(0, 16))
    for m in range(3):
        qkv[m] = total[:, m * WIDTH : (m + 1) * WIDTH]
    out[...] = total[:, 3 * WIDTH :]
    found = bias_sum(stage_rows(parts, pl.ds(16, 16))[:, :512])
    for head in range(HEADS):
        for c in range(16):
            stop = min(c * 48 + 48, NB)
            bias[head : head + 1, c * 48 : stop] = found[head * 16 + c : head * 16 + c + 1, : stop - c * 48]


def load_kernel(*refs):
    sources, targets, arrived = refs[:3], refs[3:6], refs[6]
    copies = [pltpu.make_async_copy(a, b, arrived.at[i]) for i, (a, b) in enumerate(zip(sources, targets))]
    for copy in copies:
        copy.start()
    for copy in copies:
        copy.wait()


def label_rows(labels, first):
    row = lax.broadcasted_iota(jnp.int32, (8, 72), 0)
    col = lax.broadcasted_iota(jnp.int32, (8, 72), 1)
    labels = labels.transpose(0, 2, 1).reshape(1, 72)
    hit = (row % 4 == labels) & ((row >= 4) == (col % 24 < 12))
    return jnp.pad(hit.astype(BF16), ((0, 0), (first, D - 72 - first)))


def shards(tokens, output_grad, region_labels, qkv_weight, out_weight, bias_table, bias_index):
    core = functools.partial(sent, axis="head", to=lambda i: i ^ 1)
    across = functools.partial(sent, axis="head", to=lambda i: i ^ 2)
    back = functools.partial(sent, axis="lat", to=lambda i: (i - 1) % 64)
    onward = functools.partial(sent, axis="lat", to=lambda i: (i + 1) % 64)

    inputs = tokens.transpose(0, 2, 1, 3), output_grad.transpose(0, 2, 1, 3), region_labels
    loaded = pl.pallas_call(
        load_kernel,
        out_shape=[shape(x.shape, x.dtype) for x in inputs],
        in_specs=[pl.BlockSpec(memory_space=pl.ANY)] * 3,
        out_specs=[pl.BlockSpec(memory_space=pltpu.VMEM)] * 3,
        scratch_shapes=[pltpu.SemaphoreType.DMA((3,))],
        compiler_params=pltpu.CompilerParams(vmem_limit_bytes=8 * 2**20),
    )(*inputs)

    def message(r):
        rows = slice(3 - 3 * r, 6 - 3 * r)
        t, g = (x[rows].reshape(72, D) for x in loaded[:2])
        return jnp.concatenate([t, label_rows(loaded[2][rows], 72 * r), g])

    high = message(0)
    low = back(message(1))
    far_high = across(high)

    table = jnp.pad(bias_table.T, ((0, 0), (0, 9)))
    bias, high_rows, low_rows = call(
        bias_kernel,
        (shape((HEADS, WT, WT), F32), shape((88, 16, 256), BF16), shape((88, 48, 256), BF16)),
        (),
        10**8,
        4 * 10**6,
    )(table, bias_index, jnp.asarray(window_order(), BF16))
    low, far_high, bias, high_rows, low_rows = lax.optimization_barrier((low, far_high, bias, high_rows, low_rows))
    far_low = across(low)
    near = (high, low, core(high), core(low))

    early = call(
        early_kernel,
        shape((4, HALF, WIDTH), BF16),
        [pltpu.VMEM((HALF, D), BF16), pltpu.VMEM((HALF, D), BF16)],
        10**9,
        5 * 10**6,
        8,
    )(*near, qkv_weight, out_weight)
    far_high, far_low, early = lax.optimization_barrier((far_high, far_low, early))
    far = (far_high, far_low, core(far_high), core(far_low))

    grads, *blocks = call(
        band_kernel,
        (shape((ALL, 3 * WIDTH), BF16),)
        + (shape((256, 384), BF16),) * 4
        + (shape((544, 384), BF16),) * 2
        + (shape((512, 256), BF16),) * 2,
        [
            pltpu.VMEM((ALL, D), BF16),
            pltpu.VMEM((ALL, D), BF16),
            pltpu.VMEM((3, 4, WT, WIDTH), BF16),
            pltpu.VMEM((ALL, WIDTH), F32),
            pltpu.VMEM((4, WT, WIDTH), F32),
            pltpu.VMEM((4, 4, WT, WIDTH), F32),
            pltpu.VMEM((HEADS, WT, WT), F32),
            pltpu.VMEM((ALL, WIDTH), BF16),
            pltpu.VMEM((4, 8, WIDTH), F32),
            pltpu.VMEM((D, D), BF16),
        ],
        3 * 10**9,
        10**7,
        24,
    )(*near, *far, qkv_weight, out_weight, bias, early, high_rows, low_rows)

    def by_y(parts):
        return [parts[0]] + [sent(parts[d], "lat", moved(0, d, 0)) for d in range(1, 4)]

    def swapped(parts, dx, dz):
        return [parts[0], sent(parts[1], "lat", paired(dx, dz))]

    ways, sides, pairs = by_y(blocks[:4]), swapped(blocks[4:6], 1, 0), swapped(blocks[6:], 0, 1)

    near, far, given = call(
        input_kernel, (shape((WT, D), BF16), shape((WT, D), BF16), shape((2 * WT, D), BF16)), (), 10**9, 5 * 10**6
    )(grads, qkv_weight)
    given = core(given)
    far = (far.astype(F32) + given[WT:].astype(F32)).astype(BF16)
    ways, sides, pairs, far = lax.optimization_barrier((ways, sides, pairs, far))
    parts = call(
        second_kernel, (shape((256, 512), BF16),) * 2 + (shape((160, 384), BF16),) * 4, (), 10**6, 3 * 10**6, 8
    )(*ways, *sides, *pairs)
    more = across(far)
    mixed, ways = swapped(parts[:2], 1, 0), by_y(parts[2:])
    parts = call(
        third_kernel, (shape((80, 768), BF16),) * 2 + (shape((64, 256), BF16),) * 4, (), 10**6, 10**6, 8
    )(*mixed, *ways)
    pairs, ways = swapped(parts[:2], 0, 1), by_y(parts[2:])
    near = near.astype(F32) + given[:WT].astype(F32) + more.astype(F32)
    pairs, ways, near = lax.optimization_barrier((pairs, ways, near))
    parts = call(fourth_kernel, (shape((32, D), BF16),) * 4, (), 10**6, 10**6, 8)(*pairs, *ways)
    got = [parts[0]] + [sent(parts[e], "lat", moved(0, 0, 2 * e)) for e in range(1, 4)]
    low = onward(near[72:].astype(BF16)).astype(F32)
    input_grad = jnp.concatenate([low, near[:72]]).reshape(6, 12, 2, D).transpose(0, 2, 1, 3)
    got, input_grad = lax.optimization_barrier((got, input_grad))
    qkv_grad, out_grad, bias_grad = call(
        last_kernel,
        (shape((3, 16, WIDTH), F32), shape((16, WIDTH), F32), shape((HEADS, NB), F32)),
        (),
        10**6,
        10**6,
        8,
    )(*got)
    return input_grad, qkv_grad, out_grad.T, bias_grad.T


def solution(mesh):
    return jax.shard_map(
        shards,
        mesh=mesh,
        in_specs=(
            P("lat", None, "head", None),
            P("lat", None, "head", None),
            P("lat", None, "head"),
            P(None, None, "head"),
            P("head", None),
            P(None, "head"),
            P(),
        ),
        out_specs=(
            P("lat", None, "head", None),
            P(None, "lat", "head"),
            P("head", "lat"),
            P(None, "head"),
        ),
        check_vma=False,
    )
```

```python
import functools

import jax
import jax.numpy as jnp
import numpy as np
from jax import lax
from jax.experimental import pallas as pl
from jax.experimental.pallas import tpu as pltpu
from jax.sharding import PartitionSpec as P

D = 1024
HD = 64
HEADS = 4
WIDTH = 256
WT = 144
NB = 759
ROWS = 80
BLOCKS = 8
ALL = BLOCKS * ROWS
HALF = 320
NY = 4
NZ = 8
F32 = jnp.float32
BF16 = jnp.bfloat16
NT = (((1,), (1,)), ((), ()))
TN = (((0,), (0,)), ((), ()))


def sent(x, axis, to):
    size = lax.axis_size(axis)
    return lax.ppermute(x, axis, [(i, to(i)) for i in range(size)])


def lat_of(x, y, z):
    return (x * NY + y % NY) * NZ + z % NZ


def moved(dx, dy, dz):
    def to(i):
        x, y, z = i // (NY * NZ), i // NZ % NY, i % NZ
        return lat_of(x ^ dx, y + dy, z + dz)

    return to


def paired(dx, dz):
    def to(i):
        x, y, z = i // (NY * NZ), i // NZ % NY, i % NZ
        return lat_of(x ^ dx, y, z ^ dz)

    return to


def call(kernel, out, args, flops, moved_bytes, vmem=16):
    return pl.pallas_call(
        kernel,
        out_shape=out,
        scratch_shapes=args,
        compiler_params=pltpu.CompilerParams(vmem_limit_bytes=vmem * 2**20),
        cost_estimate=pl.CostEstimate(flops=flops, bytes_accessed=moved_bytes, transcendentals=0),
    )


def shape(dims, dtype):
    return jax.ShapeDtypeStruct(dims, dtype)


def window_order():
    order = np.zeros((WT, WT), np.float32)
    for row in range(6):
        for half in range(2):
            for lon in range(6):
                for lev in range(2):
                    n = row * 24 + half * 12 + lon * 2 + lev
                    order[n, row * 24 + (1 - lev) * 12 + (1 - half) * 6 + lon] = 1
    return order


def turned(x, fill):
    x = jnp.concatenate([x[:, 128:], jnp.full((WT, 112), fill, F32)], axis=1)
    x = jnp.concatenate([x, jnp.full((112, 128), fill, F32)], axis=0)
    return jnp.transpose(x)[:16]


def bias_kernel(table, index, order, bias, highs, lows):
    idx = index[...].astype(F32)
    high = jnp.floor(idx * (1.0 / 32.0))
    low = idx - high * 32.0
    perm = order[...]

    def reordered(x):
        y = jnp.dot(perm, x.astype(BF16), preferred_element_type=F32).astype(BF16)
        return lax.dot_general(y, perm, NT, preferred_element_type=F32)

    own_f = reordered(high) * 32.0 + reordered(low)
    own = own_f.astype(jnp.int32)
    ends = turned(own_f, -1.0).astype(jnp.int32)

    def found(head, places):
        chunk = lax.shift_right_logical(places, 7)
        lane = lax.bitwise_and(places, 127)
        total = jnp.zeros(places.shape, F32)
        for c in range(6):
            row = jnp.broadcast_to(table[head : head + 1, c * 128 : (c + 1) * 128], places.shape)
            got = jnp.take_along_axis(row, lane, axis=1, mode="promise_in_bounds")
            total = jnp.where(chunk == c, got, total)
        return total

    for head in range(HEADS):
        bias[head, :, :128] = found(head, own[:, :128])
        rest = jnp.concatenate([found(head, ends[:, :128]), found(head, ends[:, 128:])], axis=1)
        rest = jnp.transpose(jnp.concatenate([rest, jnp.zeros((112, 256), F32)], axis=0))
        bias[head, :, 128:] = rest[:WT, :16]

    high_row = lax.broadcasted_iota(jnp.int32, (16, 256), 0)
    low_row = lax.broadcasted_iota(jnp.int32, (48, 256), 0)
    for n in range(88):
        if n < 72:
            places = jnp.concatenate([own[2 * n : 2 * n + 1, :128], own[2 * n + 1 : 2 * n + 2, :128]], axis=1)
        else:
            places = ends[n - 72 : n - 71]
        upper = jnp.floor(places.astype(F32) * (1.0 / 48.0) + 0.01).astype(jnp.int32)
        highs[n] = (high_row == upper).astype(F32).astype(BF16)
        lows[n] = (low_row == places - upper * 48).astype(F32).astype(BF16)


def eastern(width):
    row = lax.broadcasted_iota(jnp.int32, (72, width), 0)
    return lax.rem(row, 24) < 12


def to_windows(rows, wins, own):
    first = eastern(rows.shape[1])
    for w in range(4):
        near = lax.bitwise_xor(own, w) * 2 * ROWS
        east = lax.bitwise_xor(own, (w + 1) % 4) * 2 * ROWS
        for r in range(2):
            a = rows[pl.ds(pl.multiple_of(near + r * ROWS, 8), 72), :]
            b = rows[pl.ds(pl.multiple_of(east + r * ROWS, 8), 72), :]
            wins[w, r * 72 : (r + 1) * 72, :] = jnp.where(first, b, a)


def from_windows(wins, rows, own):
    first = eastern(rows.shape[1])
    for s in range(4):
        start = lax.bitwise_xor(own, s) * 2 * ROWS
        for r in range(2):
            a = wins[s, r * 72 : (r + 1) * 72, :]
            b = wins[(s + 3) % 4, r * 72 : (r + 1) * 72, :]
            at = pl.multiple_of(start + r * ROWS, 8)
            rows[pl.ds(at, 72), :] = jnp.where(first, b, a)
            rows[pl.ds(pl.multiple_of(at + 72, 8), 8), :] = jnp.zeros((8, rows.shape[1]), F32)


def by_head(x):
    lane = lax.shift_right_logical(lax.broadcasted_iota(jnp.int32, (1, WIDTH), 1), 6)
    return jnp.concatenate([x * (lane == head).astype(F32).astype(BF16) for head in range(HEADS)], axis=0)


def own_columns(x):
    first = lax.broadcasted_iota(jnp.int32, (WT, 128), 1) < HD
    part = [x[head * WT : (head + 1) * WT, head // 2 * 128 : head // 2 * 128 + 128] for head in range(HEADS)]
    return jnp.concatenate([jnp.where(first, part[0], part[1]), jnp.where(first, part[2], part[3])], axis=1)


def stacked(pieces, tall, gall):
    for p, piece in enumerate(pieces):
        tall[p * ROWS : (p + 1) * ROWS, :] = piece[:ROWS, :]
        rows = jnp.concatenate([piece[ROWS:, :].astype(F32), jnp.zeros((8, D), F32)], axis=0)
        gall[p * ROWS : (p + 1) * ROWS, :] = rows.astype(BF16)


def projected(m, tall, gall, weight, wo):
    if m < 3:
        y = jnp.dot(tall[...], weight[m], preferred_element_type=F32)
    else:
        y = lax.dot_general(gall[...], wo[...], NT, preferred_element_type=F32)
    return y.astype(BF16)


def early_kernel(m0, m1, m2, m3, weight, wo, proj, tall, gall):
    stacked((m0, m1, m2, m3), tall, gall)
    for m in range(4):
        proj[m] = projected(m, tall, gall, weight, wo)


def segment_sums(sums, highs, lows):
    total = jnp.zeros((64, 48), F32)
    ends = [turned(sums[head], 0.0) for head in range(HEADS)]
    for n in range(88):
        rows = []
        for head in range(HEADS):
            if n < 72:
                row = jnp.concatenate([sums[head, 2 * n : 2 * n + 1, :128], sums[head, 2 * n + 1 : 2 * n + 2, :128]], axis=1)
            else:
                row = ends[head][n - 72 : n - 71]
            rows.append(jnp.broadcast_to(row, (16, 256)).astype(BF16) * highs[n])
        total += lax.dot_general(jnp.concatenate(rows, axis=0), lows[n], NT, preferred_element_type=F32)
    return total


def bias_rows(x):
    top = x.astype(BF16).astype(F32)
    x = top + pltpu.roll(x - top, 64, 1)
    return jnp.concatenate([x[head * 16 : (head + 1) * 16] for head in range(HEADS)], axis=1).astype(BF16)


def bias_sum(s):
    x = jnp.concatenate([s[:, head * 128 : (head + 1) * 128] for head in range(HEADS)], axis=0)
    lane = lax.broadcasted_iota(jnp.int32, x.shape, 1)
    return jnp.where(lane < 64, x + pltpu.roll(x, 64, 1), 0.0)


def band_kernel(*refs):
    pieces = refs[:8]
    weight, wo, bias, early, high_rows, low_rows, grads = refs[8:15]
    ways, pairs = refs[15:19], refs[19:23]
    tall, gall, qkv, rows, wins, outs, sums, att, labels, full = refs[23:]
    own = lax.axis_index("head")
    labels[...] = jnp.zeros_like(labels)
    row = lax.broadcasted_iota(jnp.int32, (8, WIDTH), 0)
    for p in range(4):
        shard = lax.bitwise_xor(own, p)
        before = lax.rem(shard + 3, 4)
        marks = sum(pieces[2 * p + r][64:80, :WIDTH].astype(F32)[8:16] for r in range(2))
        labels[shard] += jnp.where(row < 4, marks, 0.0)
        labels[before] += jnp.where(row < 4, pltpu.roll(marks, 4, 0), 0.0)
    stacked(pieces[:4], tall.at[:HALF, :], gall.at[:HALF, :])
    stacked(pieces[4:], tall.at[HALF:, :], gall.at[HALF:, :])
    for m in range(4):
        rows[:HALF, :] = early[m].astype(F32)
        rows[HALF:, :] = projected(m, tall.at[HALF:, :], gall.at[HALF:, :], weight, wo).astype(F32)
        to_windows(rows, wins, own)
        if m < 3:
            qkv[m] = wins[...].astype(BF16)
    for w in range(4):
        marks = labels[w].astype(BF16)
        same = lax.dot_general(marks, marks, TN, preferred_element_type=F32)[:WT, :WT] > 0.5
        same = jnp.where(same, 0.0, -jnp.inf)
        q = by_head(qkv[0, w] * jnp.asarray(0.125, BF16))
        k = qkv[1, w]
        v = qkv[2, w]
        d = by_head(wins[w].astype(BF16))
        s = lax.dot_general(q, k, NT, preferred_element_type=F32).reshape(HEADS, WT, WT)
        dp = lax.dot_general(d, v, NT, preferred_element_type=F32).reshape(HEADS, WT, WT)
        s = s + bias[...] + same[None]
        e = jnp.exp(s - jnp.max(s, axis=2, keepdims=True))
        pr = e * (1.0 / jnp.sum(e, axis=2, keepdims=True))
        ds = pr * (dp - jnp.sum(pr * dp, axis=2, keepdims=True))
        sums[...] = ds if w == 0 else sums[...] + ds
        prb = pr.astype(BF16).reshape(HEADS * WT, WT)
        dsb = ds.astype(BF16).reshape(HEADS * WT, WT)
        outs[0, w] = own_columns(jnp.dot(dsb, k, preferred_element_type=F32)) * 0.125
        outs[1, w] = lax.dot_general(dsb, q, TN, preferred_element_type=F32)
        outs[2, w] = lax.dot_general(prb, d, TN, preferred_element_type=F32)
        outs[3, w] = own_columns(jnp.dot(prb, v, preferred_element_type=F32))
    for m in range(4):
        from_windows(outs.at[m], rows, own)
        if m < 3:
            grads[:, m * WIDTH : (m + 1) * WIDTH] = rows[...].astype(BF16)
    att[...] = rows[...].astype(BF16)

    found = segment_sums(sums, high_rows, low_rows)
    found = bias_rows(jnp.concatenate([found, jnp.zeros((64, 80), F32)], axis=1))

    full[:, : 3 * WIDTH] = lax.dot_general(tall[...], grads[...], TN, preferred_element_type=F32).astype(BF16)
    full[:, 3 * WIDTH :] = lax.dot_general(gall[...], att[...], TN, preferred_element_type=F32).astype(BF16)
    lat = lax.axis_index("lat")
    x, y, z = lat // (NY * NZ), lax.rem(lat // NZ, NY), lax.rem(lat, 2)
    for d, out in enumerate(ways):
        out[256:272, :512] = found
        out[256:272, 512:] = jnp.zeros((16, 128), BF16)
        for half in range(2):
            at = pl.ds(pl.multiple_of(half * 512 + lax.rem(y + d, NY) * 128, 128), 128)
            out[half * 128 : (half + 1) * 128, :] = full[at, :640]
    for i, out in enumerate(pairs):
        start = lax.bitwise_xor(x, i // 2) * 512 + lax.bitwise_xor(z, i % 2) * 16
        for b in range(16):
            at = pl.ds(pl.multiple_of(start + (b // 4) * 128 + (b % 4) * 32, 16), 16)
            out[b * 16 : (b + 1) * 16, :] = full[at, 640:]


def input_kernel(grads, weight, near, far, given):
    total = jnp.zeros((ALL, D), F32)
    for m in range(3):
        total += lax.dot_general(
            grads[:, m * WIDTH : (m + 1) * WIDTH], weight[m], NT, preferred_element_type=F32
        )
    for p, out in enumerate((near.at[...], given.at[:WT, :], far.at[...], given.at[WT:, :])):
        start = p * 2 * ROWS
        both = jnp.concatenate([total[start : start + 72], total[start + ROWS : start + ROWS + 72]], axis=0)
        out[...] = both.astype(BF16)


def stage_rows(parts, rows, columns=slice(None)):
    total = parts[0][rows, columns].astype(F32)
    for part in parts[1:]:
        total += part[rows, columns].astype(F32)
    return total


def place():
    lat = lax.axis_index("lat")
    return lat // (NY * NZ), lax.rem(lat // NZ, NY), lax.rem(lat, NZ)


def after_ways_kernel(*refs):
    ways, outs = refs[:4], refs[4:]
    x, _, z = place()
    found = bias_rows(bias_sum(stage_rows(ways, pl.ds(256, 16), slice(0, 512))))
    for i, out in enumerate(outs):
        start = lax.bitwise_xor(x, i // 2) * 128 + lax.bitwise_xor(lax.rem(z, 2), i % 2) * 16
        for k in range(4):
            rows = pl.ds(pl.multiple_of(start + k * 32, 16), 16)
            out[k * 16 : (k + 1) * 16, :] = stage_rows(ways, rows).astype(BF16)
        out[64:80, :512] = found
        out[64:80, 512:] = jnp.zeros((16, 128), BF16)


def after_pairs_kernel(*refs):
    pairs, outs = refs[:4], refs[4:]
    y = place()[1]
    for d, out in enumerate(outs):
        rows = pl.ds(pl.multiple_of(lax.rem(y + d, NY) * 64, 64), 64)
        out[...] = stage_rows(pairs, rows).astype(BF16)


def third_kernel(*refs):
    pairs, ways, outs = refs[:4], refs[4:8], refs[8:]
    z = place()[2] // 2
    found = bias_rows(bias_sum(stage_rows(pairs, pl.ds(64, 16), slice(0, 512))))
    for e, out in enumerate(outs):
        rows = pl.ds(pl.multiple_of(lax.rem(z + e, 4) * 16, 16), 16)
        out[:16, :640] = stage_rows(pairs, rows).astype(BF16)
        out[:16, 640:] = stage_rows(ways, rows).astype(BF16)
        out[16:, :512] = found
        out[16:, 512:] = jnp.zeros_like(found)


def last_kernel(a, b, c, d, qkv, out, bias):
    parts = (a, b, c, d)
    total = stage_rows(parts, pl.ds(0, 16))
    for m in range(3):
        qkv[m] = total[:, m * WIDTH : (m + 1) * WIDTH]
    out[...] = total[:, 3 * WIDTH :]
    found = bias_sum(stage_rows(parts, pl.ds(16, 16))[:, :512])
    for head in range(HEADS):
        for c in range(16):
            stop = min(c * 48 + 48, NB)
            bias[head : head + 1, c * 48 : stop] = found[head * 16 + c : head * 16 + c + 1, : stop - c * 48]


def load_kernel(*refs):
    sources, targets, arrived = refs[:3], refs[3:6], refs[6]
    copies = [pltpu.make_async_copy(a, b, arrived.at[i]) for i, (a, b) in enumerate(zip(sources, targets))]
    for copy in copies:
        copy.start()
    for copy in copies:
        copy.wait()


def label_rows(labels, first):
    row = lax.broadcasted_iota(jnp.int32, (8, 72), 0)
    col = lax.broadcasted_iota(jnp.int32, (8, 72), 1)
    labels = labels.transpose(0, 2, 1).reshape(1, 72)
    hit = (row % 4 == labels) & ((row >= 4) == (col % 24 < 12))
    return jnp.pad(hit.astype(BF16), ((0, 0), (first, D - 72 - first)))


def shards(tokens, output_grad, region_labels, qkv_weight, out_weight, bias_table, bias_index):
    core = functools.partial(sent, axis="head", to=lambda i: i ^ 1)
    across = functools.partial(sent, axis="head", to=lambda i: i ^ 2)
    back = functools.partial(sent, axis="lat", to=lambda i: (i - 1) % 64)
    onward = functools.partial(sent, axis="lat", to=lambda i: (i + 1) % 64)

    inputs = tokens.transpose(0, 2, 1, 3), output_grad.transpose(0, 2, 1, 3), region_labels
    loaded = pl.pallas_call(
        load_kernel,
        out_shape=[shape(x.shape, x.dtype) for x in inputs],
        in_specs=[pl.BlockSpec(memory_space=pl.ANY)] * 3,
        out_specs=[pl.BlockSpec(memory_space=pltpu.VMEM)] * 3,
        scratch_shapes=[pltpu.SemaphoreType.DMA((3,))],
        compiler_params=pltpu.CompilerParams(vmem_limit_bytes=8 * 2**20),
    )(*inputs)

    def message(r):
        rows = slice(3 - 3 * r, 6 - 3 * r)
        t, g = (x[rows].reshape(72, D) for x in loaded[:2])
        return jnp.concatenate([t, label_rows(loaded[2][rows], 72 * r), g])

    high = message(0)
    low = back(message(1))
    far_high = across(high)

    table = jnp.pad(bias_table.T, ((0, 0), (0, 9)))
    bias, high_rows, low_rows = call(
        bias_kernel,
        (shape((HEADS, WT, WT), F32), shape((88, 16, 256), BF16), shape((88, 48, 256), BF16)),
        (),
        10**8,
        4 * 10**6,
    )(table, bias_index, jnp.asarray(window_order(), BF16))
    low, far_high, bias, high_rows, low_rows = lax.optimization_barrier((low, far_high, bias, high_rows, low_rows))
    far_low = across(low)
    near = (high, low, core(high), core(low))

    early = call(
        early_kernel,
        shape((4, HALF, WIDTH), BF16),
        [pltpu.VMEM((HALF, D), BF16), pltpu.VMEM((HALF, D), BF16)],
        10**9,
        5 * 10**6,
        8,
    )(*near, qkv_weight, out_weight)
    far_high, far_low, early = lax.optimization_barrier((far_high, far_low, early))
    far = (far_high, far_low, core(far_high), core(far_low))

    grads, *blocks = call(
        band_kernel,
        (shape((ALL, 3 * WIDTH), BF16),)
        + (shape((272, 640), BF16),) * 4
        + (shape((256, 384), BF16),) * 4,
        [
            pltpu.VMEM((ALL, D), BF16),
            pltpu.VMEM((ALL, D), BF16),
            pltpu.VMEM((3, 4, WT, WIDTH), BF16),
            pltpu.VMEM((ALL, WIDTH), F32),
            pltpu.VMEM((4, WT, WIDTH), F32),
            pltpu.VMEM((4, 4, WT, WIDTH), F32),
            pltpu.VMEM((HEADS, WT, WT), F32),
            pltpu.VMEM((ALL, WIDTH), BF16),
            pltpu.VMEM((4, 8, WIDTH), F32),
            pltpu.VMEM((D, D), BF16),
        ],
        3 * 10**9,
        10**7,
        24,
    )(*near, *far, qkv_weight, out_weight, bias, early, high_rows, low_rows)

    def by_y(parts):
        far = sent(parts[2], "lat", moved(0, 2, 0))
        return [parts[0], sent(parts[1], "lat", moved(0, 1, 0)), far, sent(parts[3], "lat", moved(0, 3, 0))]

    def by_pair(parts):
        return [parts[0]] + [sent(parts[d], "lat", paired(d // 2, d % 2)) for d in range(1, 4)]

    ways, pairs = by_y(blocks[:4]), by_pair(blocks[4:])

    near, far, given = call(
        input_kernel, (shape((WT, D), BF16), shape((WT, D), BF16), shape((2 * WT, D), BF16)), (), 10**9, 5 * 10**6
    )(grads, qkv_weight)
    given = core(given)
    far = (far.astype(F32) + given[WT:].astype(F32)).astype(BF16)
    more = across(far)
    parts = call(after_pairs_kernel, (shape((64, 384), BF16),) * 4, (), 10**6, 10**6, 8)(*pairs)
    late = by_y(parts)
    ways, more = lax.optimization_barrier((ways, more))
    near = near.astype(F32) + given[:WT].astype(F32) + more.astype(F32)
    low = onward(near[72:].astype(BF16))
    parts = call(after_ways_kernel, (shape((80, 640), BF16),) * 4, (), 10**6, 2 * 10**6, 8)(*ways)
    pairs = by_pair(parts)
    pairs, late, low = lax.optimization_barrier((pairs, late, low))
    input_grad = jnp.concatenate([low.astype(F32), near[:72]]).reshape(6, 12, 2, D).transpose(0, 2, 1, 3)
    parts = call(third_kernel, (shape((32, D), BF16),) * 4, (), 10**6, 10**6, 8)(*pairs, *late)
    far = sent(parts[2], "lat", moved(0, 0, 4))
    got = [parts[0], sent(parts[1], "lat", moved(0, 0, 2)), far, sent(parts[3], "lat", moved(0, 0, 6))]
    got, input_grad = lax.optimization_barrier((got, input_grad))
    qkv_grad, out_grad, bias_grad = call(
        last_kernel,
        (shape((3, 16, WIDTH), F32), shape((16, WIDTH), F32), shape((HEADS, NB), F32)),
        (),
        10**6,
        10**6,
        8,
    )(*got)
    return input_grad, qkv_grad, out_grad.T, bias_grad.T


def solution(mesh):
    return jax.shard_map(
        shards,
        mesh=mesh,
        in_specs=(
            P("lat", None, "head", None),
            P("lat", None, "head", None),
            P("lat", None, "head"),
            P(None, None, "head"),
            P("head", None),
            P(None, "head"),
            P(),
        ),
        out_specs=(
            P("lat", None, "head", None),
            P(None, "lat", "head"),
            P("head", "lat"),
            P(None, "head"),
        ),
        check_vma=False,
    )
```

```python
import functools

import jax
import jax.numpy as jnp
import numpy as np
from jax import lax
from jax.experimental import pallas as pl
from jax.experimental.pallas import tpu as pltpu
from jax.sharding import PartitionSpec as P

D = 1024
HD = 64
HEADS = 4
WIDTH = 256
WT = 144
NB = 759
ROWS = 80
BLOCKS = 8
ALL = BLOCKS * ROWS
HALF = 320
NY = 4
NZ = 8
F32 = jnp.float32
BF16 = jnp.bfloat16
NT = (((1,), (1,)), ((), ()))
TN = (((0,), (0,)), ((), ()))


def sent(x, axis, to):
    size = lax.axis_size(axis)
    return lax.ppermute(x, axis, [(i, to(i)) for i in range(size)])


def lat_of(x, y, z):
    return (x * NY + y % NY) * NZ + z % NZ


def moved(dx, dy, dz):
    def to(i):
        x, y, z = i // (NY * NZ), i // NZ % NY, i % NZ
        return lat_of(x ^ dx, y + dy, z + dz)

    return to


def paired(dx, dz):
    def to(i):
        x, y, z = i // (NY * NZ), i // NZ % NY, i % NZ
        return lat_of(x ^ dx, y, z ^ dz)

    return to


def call(kernel, out, args, flops, moved_bytes, vmem=16):
    return pl.pallas_call(
        kernel,
        out_shape=out,
        scratch_shapes=args,
        compiler_params=pltpu.CompilerParams(vmem_limit_bytes=vmem * 2**20),
        cost_estimate=pl.CostEstimate(flops=flops, bytes_accessed=moved_bytes, transcendentals=0),
    )


def shape(dims, dtype):
    return jax.ShapeDtypeStruct(dims, dtype)


def window_order():
    order = np.zeros((WT, WT), np.float32)
    for row in range(6):
        for half in range(2):
            for lon in range(6):
                for lev in range(2):
                    n = row * 24 + half * 12 + lon * 2 + lev
                    order[n, row * 24 + (1 - lev) * 12 + (1 - half) * 6 + lon] = 1
    return order


def turned(x, fill):
    x = jnp.concatenate([x[:, 128:], jnp.full((WT, 112), fill, F32)], axis=1)
    x = jnp.concatenate([x, jnp.full((112, 128), fill, F32)], axis=0)
    return jnp.transpose(x)[:16]


def bias_kernel(table, index, order, bias, highs, lows):
    idx = index[...].astype(F32)
    high = jnp.floor(idx * (1.0 / 32.0))
    low = idx - high * 32.0
    perm = order[...]

    def reordered(x):
        y = jnp.dot(perm, x.astype(BF16), preferred_element_type=F32).astype(BF16)
        return lax.dot_general(y, perm, NT, preferred_element_type=F32)

    own_f = reordered(high) * 32.0 + reordered(low)
    own = own_f.astype(jnp.int32)
    ends = turned(own_f, -1.0).astype(jnp.int32)

    def found(head, places):
        chunk = lax.shift_right_logical(places, 7)
        lane = lax.bitwise_and(places, 127)
        total = jnp.zeros(places.shape, F32)
        for c in range(6):
            row = jnp.broadcast_to(table[head : head + 1, c * 128 : (c + 1) * 128], places.shape)
            got = jnp.take_along_axis(row, lane, axis=1, mode="promise_in_bounds")
            total = jnp.where(chunk == c, got, total)
        return total

    for head in range(HEADS):
        bias[head, :, :128] = found(head, own[:, :128])
        rest = jnp.concatenate([found(head, ends[:, :128]), found(head, ends[:, 128:])], axis=1)
        rest = jnp.transpose(jnp.concatenate([rest, jnp.zeros((112, 256), F32)], axis=0))
        bias[head, :, 128:] = rest[:WT, :16]

    high_row = lax.broadcasted_iota(jnp.int32, (16, 256), 0)
    low_row = lax.broadcasted_iota(jnp.int32, (48, 256), 0)
    for n in range(88):
        if n < 72:
            places = jnp.concatenate([own[2 * n : 2 * n + 1, :128], own[2 * n + 1 : 2 * n + 2, :128]], axis=1)
        else:
            places = ends[n - 72 : n - 71]
        upper = jnp.floor(places.astype(F32) * (1.0 / 48.0) + 0.01).astype(jnp.int32)
        highs[n] = (high_row == upper).astype(F32).astype(BF16)
        lows[n] = (low_row == places - upper * 48).astype(F32).astype(BF16)


def eastern(width):
    row = lax.broadcasted_iota(jnp.int32, (72, width), 0)
    return lax.rem(row, 24) < 12


def to_windows(rows, wins, own):
    first = eastern(rows.shape[1])
    for w in range(4):
        near = lax.bitwise_xor(own, w) * 2 * ROWS
        east = lax.bitwise_xor(own, (w + 1) % 4) * 2 * ROWS
        for r in range(2):
            a = rows[pl.ds(pl.multiple_of(near + r * ROWS, 8), 72), :]
            b = rows[pl.ds(pl.multiple_of(east + r * ROWS, 8), 72), :]
            wins[w, r * 72 : (r + 1) * 72, :] = jnp.where(first, b, a)


def from_windows(wins, rows, own):
    first = eastern(rows.shape[1])
    for s in range(4):
        start = lax.bitwise_xor(own, s) * 2 * ROWS
        for r in range(2):
            a = wins[s, r * 72 : (r + 1) * 72, :]
            b = wins[(s + 3) % 4, r * 72 : (r + 1) * 72, :]
            at = pl.multiple_of(start + r * ROWS, 8)
            rows[pl.ds(at, 72), :] = jnp.where(first, b, a)
            rows[pl.ds(pl.multiple_of(at + 72, 8), 8), :] = jnp.zeros((8, rows.shape[1]), F32)


def by_head(x):
    lane = lax.shift_right_logical(lax.broadcasted_iota(jnp.int32, (1, WIDTH), 1), 6)
    return jnp.concatenate([x * (lane == head).astype(F32).astype(BF16) for head in range(HEADS)], axis=0)


def own_columns(x):
    first = lax.broadcasted_iota(jnp.int32, (WT, 128), 1) < HD
    part = [x[head * WT : (head + 1) * WT, head // 2 * 128 : head // 2 * 128 + 128] for head in range(HEADS)]
    return jnp.concatenate([jnp.where(first, part[0], part[1]), jnp.where(first, part[2], part[3])], axis=1)


def stacked(pieces, tall, gall):
    for p, piece in enumerate(pieces):
        tall[p * ROWS : (p + 1) * ROWS, :] = piece[:ROWS, :]
        rows = jnp.concatenate([piece[ROWS:, :].astype(F32), jnp.zeros((8, D), F32)], axis=0)
        gall[p * ROWS : (p + 1) * ROWS, :] = rows.astype(BF16)


def projected(m, tall, gall, weight, wo):
    if m < 3:
        y = jnp.dot(tall[...], weight[m], preferred_element_type=F32)
    else:
        y = lax.dot_general(gall[...], wo[...], NT, preferred_element_type=F32)
    return y.astype(BF16)


def early_kernel(m0, m1, m2, m3, weight, wo, proj, tall, gall):
    stacked((m0, m1, m2, m3), tall, gall)
    for m in range(4):
        proj[m] = projected(m, tall, gall, weight, wo)


def segment_sums(sums, highs, lows):
    total = jnp.zeros((64, 48), F32)
    ends = [turned(sums[head], 0.0) for head in range(HEADS)]
    for n in range(88):
        rows = []
        for head in range(HEADS):
            if n < 72:
                row = jnp.concatenate([sums[head, 2 * n : 2 * n + 1, :128], sums[head, 2 * n + 1 : 2 * n + 2, :128]], axis=1)
            else:
                row = ends[head][n - 72 : n - 71]
            rows.append(jnp.broadcast_to(row, (16, 256)).astype(BF16) * highs[n])
        total += lax.dot_general(jnp.concatenate(rows, axis=0), lows[n], NT, preferred_element_type=F32)
    return total


def bias_rows(x):
    top = x.astype(BF16).astype(F32)
    x = top + pltpu.roll(x - top, 64, 1)
    return jnp.concatenate([x[head * 16 : (head + 1) * 16] for head in range(HEADS)], axis=1).astype(BF16)


def bias_sum(s):
    x = jnp.concatenate([s[:, head * 128 : (head + 1) * 128] for head in range(HEADS)], axis=0)
    lane = lax.broadcasted_iota(jnp.int32, x.shape, 1)
    return jnp.where(lane < 64, x + pltpu.roll(x, 64, 1), 0.0)


def band_kernel(*refs):
    pieces = refs[:8]
    weight, wo, bias, early, high_rows, low_rows, grads = refs[8:15]
    ways, pairs = refs[15:19], refs[19:21]
    tall, gall, qkv, rows, wins, outs, sums, att, labels, full = refs[21:]
    own = lax.axis_index("head")
    labels[...] = jnp.zeros_like(labels)
    row = lax.broadcasted_iota(jnp.int32, (8, WIDTH), 0)
    for p in range(4):
        shard = lax.bitwise_xor(own, p)
        before = lax.rem(shard + 3, 4)
        marks = sum(pieces[2 * p + r][64:80, :WIDTH].astype(F32)[8:16] for r in range(2))
        labels[shard] += jnp.where(row < 4, marks, 0.0)
        labels[before] += jnp.where(row < 4, pltpu.roll(marks, 4, 0), 0.0)
    stacked(pieces[:4], tall.at[:HALF, :], gall.at[:HALF, :])
    stacked(pieces[4:], tall.at[HALF:, :], gall.at[HALF:, :])
    for m in range(4):
        rows[:HALF, :] = early[m].astype(F32)
        rows[HALF:, :] = projected(m, tall.at[HALF:, :], gall.at[HALF:, :], weight, wo).astype(F32)
        to_windows(rows, wins, own)
        if m < 3:
            qkv[m] = wins[...].astype(BF16)
    for w in range(4):
        marks = labels[w].astype(BF16)
        same = lax.dot_general(marks, marks, TN, preferred_element_type=F32)[:WT, :WT] > 0.5
        same = jnp.where(same, 0.0, -jnp.inf)
        q = by_head(qkv[0, w] * jnp.asarray(0.125, BF16))
        k = qkv[1, w]
        v = qkv[2, w]
        d = by_head(wins[w].astype(BF16))
        s = lax.dot_general(q, k, NT, preferred_element_type=F32).reshape(HEADS, WT, WT)
        dp = lax.dot_general(d, v, NT, preferred_element_type=F32).reshape(HEADS, WT, WT)
        s = s + bias[...] + same[None]
        e = jnp.exp(s - jnp.max(s, axis=2, keepdims=True))
        pr = e * (1.0 / jnp.sum(e, axis=2, keepdims=True))
        ds = pr * (dp - jnp.sum(pr * dp, axis=2, keepdims=True))
        sums[...] = ds if w == 0 else sums[...] + ds
        prb = pr.astype(BF16).reshape(HEADS * WT, WT)
        dsb = ds.astype(BF16).reshape(HEADS * WT, WT)
        outs[0, w] = own_columns(jnp.dot(dsb, k, preferred_element_type=F32)) * 0.125
        outs[1, w] = lax.dot_general(dsb, q, TN, preferred_element_type=F32)
        outs[2, w] = lax.dot_general(prb, d, TN, preferred_element_type=F32)
        outs[3, w] = own_columns(jnp.dot(prb, v, preferred_element_type=F32))
    for m in range(4):
        from_windows(outs.at[m], rows, own)
        if m < 3:
            grads[:, m * WIDTH : (m + 1) * WIDTH] = rows[...].astype(BF16)
    att[...] = rows[...].astype(BF16)

    found = segment_sums(sums, high_rows, low_rows)
    found = bias_rows(jnp.concatenate([found, jnp.zeros((64, 80), F32)], axis=1))

    full[:, : 3 * WIDTH] = lax.dot_general(tall[...], grads[...], TN, preferred_element_type=F32).astype(BF16)
    full[:, 3 * WIDTH :] = lax.dot_general(gall[...], att[...], TN, preferred_element_type=F32).astype(BF16)
    lat = lax.axis_index("lat")
    y, z = lax.rem(lat // NZ, NY), lax.rem(lat, 2)
    for d, out in enumerate(ways):
        out[256:272, :512] = found
        out[256:272, 512:] = jnp.zeros((16, 128), BF16)
        for half in range(2):
            at = pl.ds(pl.multiple_of(half * 512 + lax.rem(y + d, NY) * 128, 128), 128)
            out[half * 128 : (half + 1) * 128, :] = full[at, :640]
    for i, out in enumerate(pairs):
        start = lax.bitwise_xor(z, i) * 16
        for b in range(32):
            at = pl.ds(pl.multiple_of(start + (b // 4) * 128 + (b % 4) * 32, 16), 16)
            out[b * 16 : (b + 1) * 16, :] = full[at, 640:]


def input_kernel(grads, weight, near, far, given):
    total = jnp.zeros((ALL, D), F32)
    for m in range(3):
        total += lax.dot_general(
            grads[:, m * WIDTH : (m + 1) * WIDTH], weight[m], NT, preferred_element_type=F32
        )
    for p, out in enumerate((near.at[...], given.at[:WT, :], far.at[...], given.at[WT:, :])):
        start = p * 2 * ROWS
        both = jnp.concatenate([total[start : start + 72], total[start + ROWS : start + ROWS + 72]], axis=0)
        out[...] = both.astype(BF16)


def stage_rows(parts, rows, columns=slice(None)):
    total = parts[0][rows, columns].astype(F32)
    for part in parts[1:]:
        total += part[rows, columns].astype(F32)
    return total


def place():
    lat = lax.axis_index("lat")
    return lat // (NY * NZ), lax.rem(lat // NZ, NY), lax.rem(lat, NZ)


def after_pairs_kernel(*refs):
    pairs, outs = refs[:2], refs[2:]
    y = place()[1]
    for d, out in enumerate(outs):
        to = lax.rem(y + d, NY) * 64
        for half in range(2):
            rows = pl.ds(pl.multiple_of(half * 256 + to, 64), 64)
            out[half * 64 : (half + 1) * 64, :] = stage_rows(pairs, rows).astype(BF16)


def second_kernel(*refs):
    ways, late, (near, given, more), outs, (high, low) = refs[:4], refs[4:8], refs[8:11], refs[11:15], refs[15:]
    total = near[...].astype(F32) + given[...].astype(F32) + more[...].astype(F32)
    high[...] = total[:72]
    low[...] = total[72:].astype(BF16)
    x, _, z = place()
    found = bias_rows(bias_sum(stage_rows(ways, pl.ds(256, 16), slice(0, 512))))
    for i, out in enumerate(outs):
        to = lax.bitwise_xor(x, i // 2)
        start = to * 128 + lax.bitwise_xor(lax.rem(z, 2), i % 2) * 16
        for k in range(4):
            rows = pl.ds(pl.multiple_of(start + k * 32, 16), 16)
            out[k * 16 : (k + 1) * 16, :640] = stage_rows(ways, rows).astype(BF16)
        out[64:, :512] = found
        out[64:, 512:640] = jnp.zeros((16, 128), BF16)
        if i % 2 == 0:
            out[:64, 640:] = stage_rows(late, pl.ds(pl.multiple_of(to * 64, 64), 64)).astype(BF16)
            out[64:, 640:] = jnp.zeros((16, 384), BF16)


def third_kernel(a, b, c, d, *outs):
    z = place()[2] // 2
    found = bias_rows(bias_sum(stage_rows((a, b, c, d), pl.ds(64, 16), slice(0, 512))))
    for e, out in enumerate(outs):
        rows = pl.ds(pl.multiple_of(lax.rem(z + e, 4) * 16, 16), 16)
        out[:16, :640] = stage_rows((a, b, c, d), rows, slice(0, 640)).astype(BF16)
        out[:16, 640:] = stage_rows((a, c), rows, slice(640, 1024)).astype(BF16)
        out[16:, :512] = found
        out[16:, 512:] = jnp.zeros_like(found)


def last_kernel(a, b, c, d, qkv, out, bias):
    parts = (a, b, c, d)
    total = stage_rows(parts, pl.ds(0, 16))
    for m in range(3):
        qkv[m] = total[:, m * WIDTH : (m + 1) * WIDTH]
    out[...] = total[:, 3 * WIDTH :]
    found = bias_sum(stage_rows(parts, pl.ds(16, 16))[:, :512])
    for head in range(HEADS):
        for c in range(16):
            stop = min(c * 48 + 48, NB)
            bias[head : head + 1, c * 48 : stop] = found[head * 16 + c : head * 16 + c + 1, : stop - c * 48]


def load_kernel(*refs):
    sources, targets, arrived = refs[:3], refs[3:6], refs[6]
    copies = [pltpu.make_async_copy(a, b, arrived.at[i]) for i, (a, b) in enumerate(zip(sources, targets))]
    for copy in copies:
        copy.start()
    for copy in copies:
        copy.wait()


def label_rows(labels, first):
    row = lax.broadcasted_iota(jnp.int32, (8, 72), 0)
    col = lax.broadcasted_iota(jnp.int32, (8, 72), 1)
    labels = labels.transpose(0, 2, 1).reshape(1, 72)
    hit = (row % 4 == labels) & ((row >= 4) == (col % 24 < 12))
    return jnp.pad(hit.astype(BF16), ((0, 0), (first, D - 72 - first)))


def shards(tokens, output_grad, region_labels, qkv_weight, out_weight, bias_table, bias_index):
    core = functools.partial(sent, axis="head", to=lambda i: i ^ 1)
    across = functools.partial(sent, axis="head", to=lambda i: i ^ 2)
    back = functools.partial(sent, axis="lat", to=lambda i: (i - 1) % 64)
    onward = functools.partial(sent, axis="lat", to=lambda i: (i + 1) % 64)

    inputs = tokens.transpose(0, 2, 1, 3), output_grad.transpose(0, 2, 1, 3), region_labels
    loaded = pl.pallas_call(
        load_kernel,
        out_shape=[shape(x.shape, x.dtype) for x in inputs],
        in_specs=[pl.BlockSpec(memory_space=pl.ANY)] * 3,
        out_specs=[pl.BlockSpec(memory_space=pltpu.VMEM)] * 3,
        scratch_shapes=[pltpu.SemaphoreType.DMA((3,))],
        compiler_params=pltpu.CompilerParams(vmem_limit_bytes=8 * 2**20),
    )(*inputs)

    def message(r):
        rows = slice(3 - 3 * r, 6 - 3 * r)
        t, g = (x[rows].reshape(72, D) for x in loaded[:2])
        return jnp.concatenate([t, label_rows(loaded[2][rows], 72 * r), g])

    high = message(0)
    high, qkv_weight, out_weight, bias_index = lax.optimization_barrier((high, qkv_weight, out_weight, bias_index))
    low = back(message(1))
    far_high = across(high)

    table = jnp.pad(bias_table.T, ((0, 0), (0, 9)))
    bias, high_rows, low_rows = call(
        bias_kernel,
        (shape((HEADS, WT, WT), F32), shape((88, 16, 256), BF16), shape((88, 48, 256), BF16)),
        (),
        10**8,
        4 * 10**6,
    )(table, bias_index, jnp.asarray(window_order(), BF16))
    low, bias, high_rows, low_rows = lax.optimization_barrier((low, bias, high_rows, low_rows))
    far_low = across(low)
    near = (high, low, core(high), core(low))

    early = call(
        early_kernel,
        shape((4, HALF, WIDTH), BF16),
        [pltpu.VMEM((HALF, D), BF16), pltpu.VMEM((HALF, D), BF16)],
        10**9,
        5 * 10**6,
        8,
    )(*near, qkv_weight, out_weight)
    far_low, early = lax.optimization_barrier((far_low, early))
    far = (far_high, far_low, core(far_high), core(far_low))

    grads, *blocks = call(
        band_kernel,
        (shape((ALL, 3 * WIDTH), BF16),)
        + (shape((272, 640), BF16),) * 4
        + (shape((512, 384), BF16),) * 2,
        [
            pltpu.VMEM((ALL, D), BF16),
            pltpu.VMEM((ALL, D), BF16),
            pltpu.VMEM((3, 4, WT, WIDTH), BF16),
            pltpu.VMEM((ALL, WIDTH), F32),
            pltpu.VMEM((4, WT, WIDTH), F32),
            pltpu.VMEM((4, 4, WT, WIDTH), F32),
            pltpu.VMEM((HEADS, WT, WT), F32),
            pltpu.VMEM((ALL, WIDTH), BF16),
            pltpu.VMEM((4, 8, WIDTH), F32),
            pltpu.VMEM((D, D), BF16),
        ],
        3 * 10**9,
        10**7,
        24,
    )(*near, *far, qkv_weight, out_weight, bias, early, high_rows, low_rows)

    def by_y(parts):
        far = sent(parts[2], "lat", moved(0, 2, 0))
        return [parts[0], sent(parts[1], "lat", moved(0, 1, 0)), far, sent(parts[3], "lat", moved(0, 3, 0))]

    def swapped(parts, dx, dz):
        return [parts[0], sent(parts[1], "lat", paired(dx, dz))]

    pairs = swapped(blocks[4:], 0, 1)
    ways = by_y(blocks[:4])

    near, far, given = call(
        input_kernel, (shape((WT, D), BF16), shape((WT, D), BF16), shape((2 * WT, D), BF16)), (), 10**9, 5 * 10**6
    )(grads, qkv_weight)
    given = core(given)
    far = (far.astype(F32) + given[WT:].astype(F32)).astype(BF16)
    more = across(far)
    parts = call(after_pairs_kernel, (shape((128, 384), BF16),) * 4, (), 10**6, 10**6, 8)(*pairs)
    late = by_y(parts)
    ways, late, more = lax.optimization_barrier((ways, late, more))
    full, part = shape((80, D), BF16), shape((80, 640), BF16)
    *parts, near, low = call(
        second_kernel, (full, part, full, part, shape((72, D), F32), shape((72, D), BF16)), (), 10**6, 4 * 10**6, 8
    )(*ways, *late, near, given[:WT], more)
    parts = [parts[0]] + [sent(parts[i], "lat", paired(i // 2, i % 2)) for i in range(1, 4)]
    parts, low = lax.optimization_barrier((parts, onward(low)))
    input_grad = jnp.concatenate([low.astype(F32), near]).reshape(6, 12, 2, D).transpose(0, 2, 1, 3)
    parts = call(third_kernel, (shape((32, D), BF16),) * 4, (), 10**6, 10**6, 8)(*parts)
    far = sent(parts[2], "lat", moved(0, 0, 4))
    got = [parts[0], sent(parts[1], "lat", moved(0, 0, 2)), far, sent(parts[3], "lat", moved(0, 0, 6))]
    got, input_grad = lax.optimization_barrier((got, input_grad))
    qkv_grad, out_grad, bias_grad = call(
        last_kernel,
        (shape((3, 16, WIDTH), F32), shape((16, WIDTH), F32), shape((HEADS, NB), F32)),
        (),
        10**6,
        10**6,
        8,
    )(*got)
    return input_grad, qkv_grad, out_grad.T, bias_grad.T


def solution(mesh):
    return jax.shard_map(
        shards,
        mesh=mesh,
        in_specs=(
            P("lat", None, "head", None),
            P("lat", None, "head", None),
            P("lat", None, "head"),
            P(None, None, "head"),
            P("head", None),
            P(None, "head"),
            P(),
        ),
        out_specs=(
            P("lat", None, "head", None),
            P(None, "lat", "head"),
            P("head", "lat"),
            P(None, "head"),
        ),
        check_vma=False,
    )
```

```python
import functools

import jax
import jax.numpy as jnp
import numpy as np
from jax import lax
from jax.experimental import pallas as pl
from jax.experimental.pallas import tpu as pltpu
from jax.sharding import PartitionSpec as P

D = 1024
HD = 64
HEADS = 4
WIDTH = 256
WT = 144
NB = 759
ROWS = 80
BLOCKS = 8
ALL = BLOCKS * ROWS
HALF = 320
NY = 4
NZ = 8
F32 = jnp.float32
BF16 = jnp.bfloat16
NT = (((1,), (1,)), ((), ()))
TN = (((0,), (0,)), ((), ()))


def sent(x, axis, to):
    size = lax.axis_size(axis)
    return lax.ppermute(x, axis, [(i, to(i)) for i in range(size)])


def lat_of(x, y, z):
    return (x * NY + y % NY) * NZ + z % NZ


def moved(dx, dy, dz):
    def to(i):
        x, y, z = i // (NY * NZ), i // NZ % NY, i % NZ
        return lat_of(x ^ dx, y + dy, z + dz)

    return to


def paired(dx, dz):
    def to(i):
        x, y, z = i // (NY * NZ), i // NZ % NY, i % NZ
        return lat_of(x ^ dx, y, z ^ dz)

    return to


def call(kernel, out, args, flops, moved_bytes, vmem=16):
    return pl.pallas_call(
        kernel,
        out_shape=out,
        scratch_shapes=args,
        compiler_params=pltpu.CompilerParams(vmem_limit_bytes=vmem * 2**20),
        cost_estimate=pl.CostEstimate(flops=flops, bytes_accessed=moved_bytes, transcendentals=0),
    )


def shape(dims, dtype):
    return jax.ShapeDtypeStruct(dims, dtype)


def window_order():
    order = np.zeros((WT, WT), np.float32)
    for row in range(6):
        for half in range(2):
            for lon in range(6):
                for lev in range(2):
                    n = row * 24 + half * 12 + lon * 2 + lev
                    order[n, row * 24 + (1 - lev) * 12 + (1 - half) * 6 + lon] = 1
    return order


def turned(x, fill):
    x = jnp.concatenate([x[:, 128:], jnp.full((WT, 112), fill, F32)], axis=1)
    x = jnp.concatenate([x, jnp.full((112, 128), fill, F32)], axis=0)
    return jnp.transpose(x)[:16]


def bias_kernel(table, index, order, bias, highs, lows):
    idx = index[...].astype(F32)
    high = jnp.floor(idx * (1.0 / 32.0))
    low = idx - high * 32.0
    perm = order[...]

    def reordered(x):
        y = jnp.dot(perm, x.astype(BF16), preferred_element_type=F32).astype(BF16)
        return lax.dot_general(y, perm, NT, preferred_element_type=F32)

    own_f = reordered(high) * 32.0 + reordered(low)
    own = own_f.astype(jnp.int32)
    ends = turned(own_f, -1.0).astype(jnp.int32)

    def found(head, places):
        chunk = lax.shift_right_logical(places, 7)
        lane = lax.bitwise_and(places, 127)
        total = jnp.zeros(places.shape, F32)
        for c in range(6):
            row = jnp.broadcast_to(table[head : head + 1, c * 128 : (c + 1) * 128], places.shape)
            got = jnp.take_along_axis(row, lane, axis=1, mode="promise_in_bounds")
            total = jnp.where(chunk == c, got, total)
        return total

    for head in range(HEADS):
        bias[head, :, :128] = found(head, own[:, :128])
        rest = jnp.concatenate([found(head, ends[:, :128]), found(head, ends[:, 128:])], axis=1)
        rest = jnp.transpose(jnp.concatenate([rest, jnp.zeros((112, 256), F32)], axis=0))
        bias[head, :, 128:] = rest[:WT, :16]

    high_row = lax.broadcasted_iota(jnp.int32, (16, 256), 0)
    low_row = lax.broadcasted_iota(jnp.int32, (48, 256), 0)
    for n in range(88):
        if n < 72:
            places = jnp.concatenate([own[2 * n : 2 * n + 1, :128], own[2 * n + 1 : 2 * n + 2, :128]], axis=1)
        else:
            places = ends[n - 72 : n - 71]
        upper = jnp.floor(places.astype(F32) * (1.0 / 48.0) + 0.01).astype(jnp.int32)
        highs[n] = (high_row == upper).astype(F32).astype(BF16)
        lows[n] = (low_row == places - upper * 48).astype(F32).astype(BF16)


def eastern(width):
    row = lax.broadcasted_iota(jnp.int32, (72, width), 0)
    return lax.rem(row, 24) < 12


def to_windows(rows, wins, own):
    first = eastern(rows.shape[1])
    for w in range(4):
        near = lax.bitwise_xor(own, w) * 2 * ROWS
        east = lax.bitwise_xor(own, (w + 1) % 4) * 2 * ROWS
        for r in range(2):
            a = rows[pl.ds(pl.multiple_of(near + r * ROWS, 8), 72), :]
            b = rows[pl.ds(pl.multiple_of(east + r * ROWS, 8), 72), :]
            wins[w, r * 72 : (r + 1) * 72, :] = jnp.where(first, b, a)


def from_windows(wins, rows, own):
    first = eastern(rows.shape[1])
    for s in range(4):
        start = lax.bitwise_xor(own, s) * 2 * ROWS
        for r in range(2):
            a = wins[s, r * 72 : (r + 1) * 72, :]
            b = wins[(s + 3) % 4, r * 72 : (r + 1) * 72, :]
            at = pl.multiple_of(start + r * ROWS, 8)
            rows[pl.ds(at, 72), :] = jnp.where(first, b, a)
            rows[pl.ds(pl.multiple_of(at + 72, 8), 8), :] = jnp.zeros((8, rows.shape[1]), F32)


def by_head(x):
    lane = lax.shift_right_logical(lax.broadcasted_iota(jnp.int32, (1, WIDTH), 1), 6)
    return jnp.concatenate([x * (lane == head).astype(F32).astype(BF16) for head in range(HEADS)], axis=0)


def own_columns(x):
    first = lax.broadcasted_iota(jnp.int32, (WT, 128), 1) < HD
    part = [x[head * WT : (head + 1) * WT, head // 2 * 128 : head // 2 * 128 + 128] for head in range(HEADS)]
    return jnp.concatenate([jnp.where(first, part[0], part[1]), jnp.where(first, part[2], part[3])], axis=1)


def stacked(pieces, tall, gall):
    for p, piece in enumerate(pieces):
        tall[p * ROWS : (p + 1) * ROWS, :] = piece[:ROWS, :]
        rows = jnp.concatenate([piece[ROWS:, :].astype(F32), jnp.zeros((8, D), F32)], axis=0)
        gall[p * ROWS : (p + 1) * ROWS, :] = rows.astype(BF16)


def projected(m, tall, gall, weight, wo):
    if m < 3:
        y = jnp.dot(tall[...], weight[m], preferred_element_type=F32)
    else:
        y = lax.dot_general(gall[...], wo[...], NT, preferred_element_type=F32)
    return y.astype(BF16)


def attended(marks, q, k, v, d, bias):
    same = lax.dot_general(marks, marks, TN, preferred_element_type=F32)[:WT, :WT] > 0.5
    same = jnp.where(same, 0.0, -jnp.inf)
    q = by_head(q * jnp.asarray(0.125, BF16))
    d = by_head(d)
    s = lax.dot_general(q, k, NT, preferred_element_type=F32).reshape(HEADS, WT, WT)
    dp = lax.dot_general(d, v, NT, preferred_element_type=F32).reshape(HEADS, WT, WT)
    s = s + bias + same[None]
    e = jnp.exp(s - jnp.max(s, axis=2, keepdims=True))
    pr = e * (1.0 / jnp.sum(e, axis=2, keepdims=True))
    ds = pr * (dp - jnp.sum(pr * dp, axis=2, keepdims=True))
    prb = pr.astype(BF16).reshape(HEADS * WT, WT)
    dsb = ds.astype(BF16).reshape(HEADS * WT, WT)
    dq = own_columns(jnp.dot(dsb, k, preferred_element_type=F32)) * 0.125
    dk = lax.dot_general(dsb, q, TN, preferred_element_type=F32)
    dv = lax.dot_general(prb, d, TN, preferred_element_type=F32)
    return (dq, dk, dv, own_columns(jnp.dot(prb, v, preferred_element_type=F32))), ds


def marked(pieces, p):
    return sum(pieces[2 * p + r][64:80, :WIDTH].astype(F32)[8:16] for r in range(2))


def early_kernel(m0, m1, m2, m3, weight, wo, bias, proj, done, sums, tall, gall, rows, win):
    pieces = (m0, m1, m2, m3)
    stacked(pieces, tall, gall)
    odd = lax.bitwise_and(lax.axis_index("head"), 1)
    first = eastern(WIDTH)
    for m in range(4):
        y = projected(m, tall, gall, weight, wo)
        proj[m] = y
        rows[...] = y.astype(F32)
        for r in range(2):
            a = rows[pl.ds(pl.multiple_of(odd * 160 + r * ROWS, 8), 72), :]
            b = rows[pl.ds(pl.multiple_of(160 - odd * 160 + r * ROWS, 8), 72), :]
            win[m, r * 72 : (r + 1) * 72, :] = jnp.where(first, b, a)
    here, there = marked(pieces, 0), marked(pieces, 1)
    here, there = jnp.where(odd == 1, there, here), jnp.where(odd == 1, here, there)
    row = lax.broadcasted_iota(jnp.int32, (8, WIDTH), 0)
    marks = jnp.where(row < 4, here + pltpu.roll(there, 4, 0), 0.0).astype(BF16)
    results, ds = attended(marks, *(win[m].astype(BF16) for m in range(4)), bias[...])
    for m in range(4):
        done[m] = results[m]
    sums[...] = ds


def segment_sums(sums, highs, lows):
    total = jnp.zeros((64, 48), F32)
    ends = [turned(sums[head], 0.0) for head in range(HEADS)]
    for n in range(88):
        rows = []
        for head in range(HEADS):
            if n < 72:
                row = jnp.concatenate([sums[head, 2 * n : 2 * n + 1, :128], sums[head, 2 * n + 1 : 2 * n + 2, :128]], axis=1)
            else:
                row = ends[head][n - 72 : n - 71]
            rows.append(jnp.broadcast_to(row, (16, 256)).astype(BF16) * highs[n])
        total += lax.dot_general(jnp.concatenate(rows, axis=0), lows[n], NT, preferred_element_type=F32)
    return total


def bias_rows(x):
    top = x.astype(BF16).astype(F32)
    x = top + pltpu.roll(x - top, 64, 1)
    return jnp.concatenate([x[head * 16 : (head + 1) * 16] for head in range(HEADS)], axis=1).astype(BF16)


def bias_sum(s):
    x = jnp.concatenate([s[:, head * 128 : (head + 1) * 128] for head in range(HEADS)], axis=0)
    lane = lax.broadcasted_iota(jnp.int32, x.shape, 1)
    return jnp.where(lane < 64, x + pltpu.roll(x, 64, 1), 0.0)


def band_kernel(*refs):
    pieces = refs[:8]
    weight, wo, bias, early, done, early_sums, high_rows, low_rows, grads = refs[8:17]
    ways, pairs = refs[17:21], refs[21:23]
    tall, gall, qkv, rows, wins, outs, sums, att, labels, full = refs[23:]
    own = lax.axis_index("head")
    labels[...] = jnp.zeros_like(labels)
    row = lax.broadcasted_iota(jnp.int32, (8, WIDTH), 0)
    for p in range(4):
        shard = lax.bitwise_xor(own, p)
        before = lax.rem(shard + 3, 4)
        marks = marked(pieces, p)
        labels[shard] += jnp.where(row < 4, marks, 0.0)
        labels[before] += jnp.where(row < 4, pltpu.roll(marks, 4, 0), 0.0)
    stacked(pieces[:4], tall.at[:HALF, :], gall.at[:HALF, :])
    stacked(pieces[4:], tall.at[HALF:, :], gall.at[HALF:, :])
    for m in range(4):
        rows[:HALF, :] = early[m].astype(F32)
        rows[HALF:, :] = projected(m, tall.at[HALF:, :], gall.at[HALF:, :], weight, wo).astype(F32)
        to_windows(rows, wins, own)
        if m < 3:
            qkv[m] = wins[...].astype(BF16)
    near = lax.bitwise_and(own, 2)
    for m in range(4):
        outs[m, near] = done[m]
    sums[...] = early_sums[...]
    for i in range(1, 4):
        w = lax.rem(near + i, 4)
        marks = labels[w].astype(BF16)
        results, ds = attended(marks, qkv[0, w], qkv[1, w], qkv[2, w], wins[w].astype(BF16), bias[...])
        sums[...] += ds
        for m in range(4):
            outs[m, w] = results[m]
    for m in range(4):
        from_windows(outs.at[m], rows, own)
        if m < 3:
            grads[:, m * WIDTH : (m + 1) * WIDTH] = rows[...].astype(BF16)
    att[...] = rows[...].astype(BF16)

    found = segment_sums(sums, high_rows, low_rows)
    found = bias_rows(jnp.concatenate([found, jnp.zeros((64, 80), F32)], axis=1))

    full[:, : 3 * WIDTH] = lax.dot_general(tall[...], grads[...], TN, preferred_element_type=F32).astype(BF16)
    full[:, 3 * WIDTH :] = lax.dot_general(gall[...], att[...], TN, preferred_element_type=F32).astype(BF16)
    lat = lax.axis_index("lat")
    y, z = lax.rem(lat // NZ, NY), lax.rem(lat, 2)
    for d, out in enumerate(ways):
        out[256:272, :512] = found
        out[256:272, 512:] = jnp.zeros((16, 128), BF16)
        for half in range(2):
            at = pl.ds(pl.multiple_of(half * 512 + lax.rem(y + d, NY) * 128, 128), 128)
            out[half * 128 : (half + 1) * 128, :] = full[at, :640]
    for i, out in enumerate(pairs):
        start = lax.bitwise_xor(z, i) * 16
        for b in range(32):
            at = pl.ds(pl.multiple_of(start + (b // 4) * 128 + (b % 4) * 32, 16), 16)
            out[b * 16 : (b + 1) * 16, :] = full[at, 640:]


def input_kernel(grads, weight, near, far, given):
    total = jnp.zeros((ALL, D), F32)
    for m in range(3):
        total += lax.dot_general(
            grads[:, m * WIDTH : (m + 1) * WIDTH], weight[m], NT, preferred_element_type=F32
        )
    for p, out in enumerate((near.at[...], given.at[:WT, :], far.at[...], given.at[WT:, :])):
        start = p * 2 * ROWS
        both = jnp.concatenate([total[start : start + 72], total[start + ROWS : start + ROWS + 72]], axis=0)
        out[...] = both.astype(BF16)


def stage_rows(parts, rows, columns=slice(None)):
    total = parts[0][rows, columns].astype(F32)
    for part in parts[1:]:
        total += part[rows, columns].astype(F32)
    return total


def place():
    lat = lax.axis_index("lat")
    return lat // (NY * NZ), lax.rem(lat // NZ, NY), lax.rem(lat, NZ)


def after_pairs_kernel(*refs):
    pairs, outs = refs[:2], refs[2:]
    y = place()[1]
    for d, out in enumerate(outs):
        to = lax.rem(y + d, NY) * 64
        for half in range(2):
            rows = pl.ds(pl.multiple_of(half * 256 + to, 64), 64)
            out[half * 64 : (half + 1) * 64, :] = stage_rows(pairs, rows).astype(BF16)


def second_kernel(*refs):
    ways, late, (near, given, more), outs, (high, low) = refs[:4], refs[4:8], refs[8:11], refs[11:15], refs[15:]
    total = near[...].astype(F32) + given[...].astype(F32) + more[...].astype(F32)
    high[...] = total[:72]
    low[...] = total[72:].astype(BF16)
    x, _, z = place()
    found = bias_rows(bias_sum(stage_rows(ways, pl.ds(256, 16), slice(0, 512))))
    for i, out in enumerate(outs):
        to = lax.bitwise_xor(x, i // 2)
        start = to * 128 + lax.bitwise_xor(lax.rem(z, 2), i % 2) * 16
        for k in range(4):
            rows = pl.ds(pl.multiple_of(start + k * 32, 16), 16)
            out[k * 16 : (k + 1) * 16, :640] = stage_rows(ways, rows).astype(BF16)
        out[64:, :512] = found
        out[64:, 512:640] = jnp.zeros((16, 128), BF16)
        if i % 2 == 0:
            out[:64, 640:] = stage_rows(late, pl.ds(pl.multiple_of(to * 64, 64), 64)).astype(BF16)
            out[64:, 640:] = jnp.zeros((16, 384), BF16)


def third_kernel(a, b, c, d, *outs):
    z = place()[2] // 2
    found = bias_rows(bias_sum(stage_rows((a, b, c, d), pl.ds(64, 16), slice(0, 512))))
    for e, out in enumerate(outs):
        rows = pl.ds(pl.multiple_of(lax.rem(z + e, 4) * 16, 16), 16)
        out[:16, :640] = stage_rows((a, b, c, d), rows, slice(0, 640)).astype(BF16)
        out[:16, 640:] = stage_rows((a, c), rows, slice(640, 1024)).astype(BF16)
        out[16:, :512] = found
        out[16:, 512:] = jnp.zeros_like(found)


def last_kernel(a, b, c, d, qkv, out, bias):
    parts = (a, b, c, d)
    total = stage_rows(parts, pl.ds(0, 16))
    for m in range(3):
        qkv[m] = total[:, m * WIDTH : (m + 1) * WIDTH]
    out[...] = total[:, 3 * WIDTH :]
    found = bias_sum(stage_rows(parts, pl.ds(16, 16))[:, :512])
    for head in range(HEADS):
        for c in range(16):
            stop = min(c * 48 + 48, NB)
            bias[head : head + 1, c * 48 : stop] = found[head * 16 + c : head * 16 + c + 1, : stop - c * 48]


def load_kernel(*refs):
    sources, targets, arrived = refs[:3], refs[3:6], refs[6]
    copies = [pltpu.make_async_copy(a, b, arrived.at[i]) for i, (a, b) in enumerate(zip(sources, targets))]
    for copy in copies:
        copy.start()
    for copy in copies:
        copy.wait()


def label_rows(labels, first):
    row = lax.broadcasted_iota(jnp.int32, (8, 72), 0)
    col = lax.broadcasted_iota(jnp.int32, (8, 72), 1)
    labels = labels.transpose(0, 2, 1).reshape(1, 72)
    hit = (row % 4 == labels) & ((row >= 4) == (col % 24 < 12))
    return jnp.pad(hit.astype(BF16), ((0, 0), (first, D - 72 - first)))


def shards(tokens, output_grad, region_labels, qkv_weight, out_weight, bias_table, bias_index):
    core = functools.partial(sent, axis="head", to=lambda i: i ^ 1)
    across = functools.partial(sent, axis="head", to=lambda i: i ^ 2)
    back = functools.partial(sent, axis="lat", to=lambda i: (i - 1) % 64)
    onward = functools.partial(sent, axis="lat", to=lambda i: (i + 1) % 64)

    inputs = tokens.transpose(0, 2, 1, 3), output_grad.transpose(0, 2, 1, 3), region_labels
    loaded = pl.pallas_call(
        load_kernel,
        out_shape=[shape(x.shape, x.dtype) for x in inputs],
        in_specs=[pl.BlockSpec(memory_space=pl.ANY)] * 3,
        out_specs=[pl.BlockSpec(memory_space=pltpu.VMEM)] * 3,
        scratch_shapes=[pltpu.SemaphoreType.DMA((3,))],
        compiler_params=pltpu.CompilerParams(vmem_limit_bytes=56 * 2**20),
    )(*inputs)

    def message(r):
        rows = slice(3 - 3 * r, 6 - 3 * r)
        t, g = (x[rows].reshape(72, D) for x in loaded[:2])
        return jnp.concatenate([t, label_rows(loaded[2][rows], 72 * r), g])

    high = message(0)
    high, qkv_weight, out_weight, bias_index = lax.optimization_barrier((high, qkv_weight, out_weight, bias_index))
    low = back(message(1))
    far_high = across(high)

    table = jnp.pad(bias_table.T, ((0, 0), (0, 9)))
    bias, high_rows, low_rows = call(
        bias_kernel,
        (shape((HEADS, WT, WT), F32), shape((88, 16, 256), BF16), shape((88, 48, 256), BF16)),
        (),
        10**8,
        4 * 10**6,
    )(table, bias_index, jnp.asarray(window_order(), BF16))
    low, bias, high_rows, low_rows = lax.optimization_barrier((low, bias, high_rows, low_rows))
    far_low = across(low)
    near = (high, low, core(high), core(low))

    early, done, sums = call(
        early_kernel,
        (shape((4, HALF, WIDTH), BF16), shape((4, WT, WIDTH), F32), shape((HEADS, WT, WT), F32)),
        [
            pltpu.VMEM((HALF, D), BF16),
            pltpu.VMEM((HALF, D), BF16),
            pltpu.VMEM((HALF, WIDTH), F32),
            pltpu.VMEM((4, WT, WIDTH), F32),
        ],
        10**9,
        5 * 10**6,
        16,
    )(*near, qkv_weight, out_weight, bias)
    far_low, early, done, sums = lax.optimization_barrier((far_low, early, done, sums))
    far = (far_high, far_low, core(far_high), core(far_low))

    grads, *blocks = call(
        band_kernel,
        (shape((ALL, 3 * WIDTH), BF16),)
        + (shape((272, 640), BF16),) * 4
        + (shape((512, 384), BF16),) * 2,
        [
            pltpu.VMEM((ALL, D), BF16),
            pltpu.VMEM((ALL, D), BF16),
            pltpu.VMEM((3, 4, WT, WIDTH), BF16),
            pltpu.VMEM((ALL, WIDTH), F32),
            pltpu.VMEM((4, WT, WIDTH), F32),
            pltpu.VMEM((4, 4, WT, WIDTH), F32),
            pltpu.VMEM((HEADS, WT, WT), F32),
            pltpu.VMEM((ALL, WIDTH), BF16),
            pltpu.VMEM((4, 8, WIDTH), F32),
            pltpu.VMEM((D, D), BF16),
        ],
        3 * 10**9,
        10**7,
        24,
    )(*near, *far, qkv_weight, out_weight, bias, early, done, sums, high_rows, low_rows)

    def by_y(parts):
        far = sent(parts[2], "lat", moved(0, 2, 0))
        return [parts[0], sent(parts[1], "lat", moved(0, 1, 0)), far, sent(parts[3], "lat", moved(0, 3, 0))]

    def swapped(parts, dx, dz):
        return [parts[0], sent(parts[1], "lat", paired(dx, dz))]

    pairs = swapped(blocks[4:], 0, 1)
    ways = by_y(blocks[:4])

    near, far, given = call(
        input_kernel, (shape((WT, D), BF16), shape((WT, D), BF16), shape((2 * WT, D), BF16)), (), 10**9, 5 * 10**6
    )(grads, qkv_weight)
    given = core(given)
    far = (far.astype(F32) + given[WT:].astype(F32)).astype(BF16)
    more = across(far)
    parts = call(after_pairs_kernel, (shape((128, 384), BF16),) * 4, (), 10**6, 10**6, 8)(*pairs)
    late = by_y(parts)
    ways, late, more = lax.optimization_barrier((ways, late, more))
    full, part = shape((80, D), BF16), shape((80, 640), BF16)
    *parts, near, low = call(
        second_kernel, (full, part, full, part, shape((72, D), F32), shape((72, D), BF16)), (), 10**6, 4 * 10**6, 8
    )(*ways, *late, near, given[:WT], more)
    parts = [parts[0]] + [sent(parts[i], "lat", paired(i // 2, i % 2)) for i in range(1, 4)]
    parts, low = lax.optimization_barrier((parts, onward(low)))
    input_grad = jnp.concatenate([low.astype(F32), near]).reshape(6, 12, 2, D).transpose(0, 2, 1, 3)
    parts = call(third_kernel, (shape((32, D), BF16),) * 4, (), 10**6, 10**6, 8)(*parts)
    far = sent(parts[2], "lat", moved(0, 0, 4))
    got = [parts[0], sent(parts[1], "lat", moved(0, 0, 2)), far, sent(parts[3], "lat", moved(0, 0, 6))]
    got, input_grad = lax.optimization_barrier((got, input_grad))
    qkv_grad, out_grad, bias_grad = call(
        last_kernel,
        (shape((3, 16, WIDTH), F32), shape((16, WIDTH), F32), shape((HEADS, NB), F32)),
        (),
        10**6,
        10**6,
        8,
    )(*got)
    return input_grad, qkv_grad, out_grad.T, bias_grad.T


def solution(mesh):
    return jax.shard_map(
        shards,
        mesh=mesh,
        in_specs=(
            P("lat", None, "head", None),
            P("lat", None, "head", None),
            P("lat", None, "head"),
            P(None, None, "head"),
            P("head", None),
            P(None, "head"),
            P(),
        ),
        out_specs=(
            P("lat", None, "head", None),
            P(None, "lat", "head"),
            P("head", "lat"),
            P(None, "head"),
        ),
        check_vma=False,
    )
```

```python
import functools

import jax
import jax.numpy as jnp
import numpy as np
from jax import lax
from jax.experimental import pallas as pl
from jax.experimental.pallas import tpu as pltpu
from jax.sharding import PartitionSpec as P

D = 1024
HD = 64
HEADS = 4
WIDTH = 256
WT = 144
NB = 759
ROWS = 80
BLOCKS = 8
ALL = BLOCKS * ROWS
HALF = 320
NY = 4
NZ = 8
F32 = jnp.float32
BF16 = jnp.bfloat16
NT = (((1,), (1,)), ((), ()))
TN = (((0,), (0,)), ((), ()))


def sent(x, axis, to):
    size = lax.axis_size(axis)
    return lax.ppermute(x, axis, [(i, to(i)) for i in range(size)])


def lat_of(x, y, z):
    return (x * NY + y % NY) * NZ + z % NZ


def moved(dx, dy, dz):
    def to(i):
        x, y, z = i // (NY * NZ), i // NZ % NY, i % NZ
        return lat_of(x ^ dx, y + dy, z + dz)

    return to


def paired(dx, dz):
    def to(i):
        x, y, z = i // (NY * NZ), i // NZ % NY, i % NZ
        return lat_of(x ^ dx, y, z ^ dz)

    return to


def call(kernel, out, args, flops, moved_bytes, vmem=16):
    return pl.pallas_call(
        kernel,
        out_shape=out,
        scratch_shapes=args,
        compiler_params=pltpu.CompilerParams(vmem_limit_bytes=vmem * 2**20),
        cost_estimate=pl.CostEstimate(flops=flops, bytes_accessed=moved_bytes, transcendentals=0),
    )


def shape(dims, dtype):
    return jax.ShapeDtypeStruct(dims, dtype)


def window_order():
    order = np.zeros((WT, WT), np.float32)
    for row in range(6):
        for half in range(2):
            for lon in range(6):
                for lev in range(2):
                    n = row * 24 + half * 12 + lon * 2 + lev
                    order[n, row * 24 + (1 - lev) * 12 + (1 - half) * 6 + lon] = 1
    return order


def turned(x, fill):
    x = jnp.concatenate([x[:, 128:], jnp.full((WT, 112), fill, F32)], axis=1)
    x = jnp.concatenate([x, jnp.full((112, 128), fill, F32)], axis=0)
    return jnp.transpose(x)[:16]


def bias_kernel(table, index, order, bias, highs, lows):
    idx = index[...].astype(F32)
    high = jnp.floor(idx * (1.0 / 32.0))
    low = idx - high * 32.0
    perm = order[...]

    def reordered(x):
        y = jnp.dot(perm, x.astype(BF16), preferred_element_type=F32).astype(BF16)
        return lax.dot_general(y, perm, NT, preferred_element_type=F32)

    own_f = reordered(high) * 32.0 + reordered(low)
    own = own_f.astype(jnp.int32)
    ends = turned(own_f, -1.0).astype(jnp.int32)

    def found(head, places):
        chunk = lax.shift_right_logical(places, 7)
        lane = lax.bitwise_and(places, 127)
        total = jnp.zeros(places.shape, F32)
        for c in range(6):
            row = jnp.broadcast_to(table[head : head + 1, c * 128 : (c + 1) * 128], places.shape)
            got = jnp.take_along_axis(row, lane, axis=1, mode="promise_in_bounds")
            total = jnp.where(chunk == c, got, total)
        return total

    for head in range(HEADS):
        bias[head, :, :128] = found(head, own[:, :128])
        rest = jnp.concatenate([found(head, ends[:, :128]), found(head, ends[:, 128:])], axis=1)
        rest = jnp.transpose(jnp.concatenate([rest, jnp.zeros((112, 256), F32)], axis=0))
        bias[head, :, 128:] = rest[:WT, :16]

    high_row = lax.broadcasted_iota(jnp.int32, (16, 256), 0)
    low_row = lax.broadcasted_iota(jnp.int32, (48, 256), 0)
    for n in range(88):
        if n < 72:
            places = jnp.concatenate([own[2 * n : 2 * n + 1, :128], own[2 * n + 1 : 2 * n + 2, :128]], axis=1)
        else:
            places = ends[n - 72 : n - 71]
        upper = jnp.floor(places.astype(F32) * (1.0 / 48.0) + 0.01).astype(jnp.int32)
        highs[n] = (high_row == upper).astype(F32).astype(BF16)
        lows[n] = (low_row == places - upper * 48).astype(F32).astype(BF16)


def eastern(width):
    row = lax.broadcasted_iota(jnp.int32, (72, width), 0)
    return lax.rem(row, 24) < 12


def to_windows(rows, wins, own):
    first = eastern(rows.shape[1])
    for w in range(4):
        near = lax.bitwise_xor(own, w) * 2 * ROWS
        east = lax.bitwise_xor(own, (w + 1) % 4) * 2 * ROWS
        for r in range(2):
            a = rows[pl.ds(pl.multiple_of(near + r * ROWS, 8), 72), :]
            b = rows[pl.ds(pl.multiple_of(east + r * ROWS, 8), 72), :]
            wins[w, r * 72 : (r + 1) * 72, :] = jnp.where(first, b, a)


def from_windows(wins, rows, own):
    first = eastern(rows.shape[1])
    for s in range(4):
        start = lax.bitwise_xor(own, s) * 2 * ROWS
        for r in range(2):
            a = wins[s, r * 72 : (r + 1) * 72, :]
            b = wins[(s + 3) % 4, r * 72 : (r + 1) * 72, :]
            at = pl.multiple_of(start + r * ROWS, 8)
            rows[pl.ds(at, 72), :] = jnp.where(first, b, a)
            rows[pl.ds(pl.multiple_of(at + 72, 8), 8), :] = jnp.zeros((8, rows.shape[1]), F32)


def by_head(x):
    lane = lax.shift_right_logical(lax.broadcasted_iota(jnp.int32, (1, WIDTH), 1), 6)
    return jnp.concatenate([x * (lane == head).astype(F32).astype(BF16) for head in range(HEADS)], axis=0)


def own_columns(x):
    first = lax.broadcasted_iota(jnp.int32, (WT, 128), 1) < HD
    part = [x[head * WT : (head + 1) * WT, head // 2 * 128 : head // 2 * 128 + 128] for head in range(HEADS)]
    return jnp.concatenate([jnp.where(first, part[0], part[1]), jnp.where(first, part[2], part[3])], axis=1)


def stacked(pieces, tall, gall):
    for p, piece in enumerate(pieces):
        tall[p * ROWS : (p + 1) * ROWS, :] = piece[:ROWS, :]
        rows = jnp.concatenate([piece[ROWS:, :].astype(F32), jnp.zeros((8, D), F32)], axis=0)
        gall[p * ROWS : (p + 1) * ROWS, :] = rows.astype(BF16)


def projected(m, tall, gall, weight, wo):
    if m < 3:
        y = jnp.dot(tall[...], weight[m], preferred_element_type=F32)
    else:
        y = lax.dot_general(gall[...], wo[...], NT, preferred_element_type=F32)
    return y.astype(BF16)


def attended(marks, q, k, v, d, bias):
    same = lax.dot_general(marks, marks, TN, preferred_element_type=F32)[:WT, :WT] > 0.5
    same = jnp.where(same, 0.0, -jnp.inf)
    q = by_head(q * jnp.asarray(0.125, BF16))
    d = by_head(d)
    s = lax.dot_general(q, k, NT, preferred_element_type=F32).reshape(HEADS, WT, WT)
    dp = lax.dot_general(d, v, NT, preferred_element_type=F32).reshape(HEADS, WT, WT)
    s = s + bias + same[None]
    e = jnp.exp(s - jnp.max(s, axis=2, keepdims=True))
    pr = e * (1.0 / jnp.sum(e, axis=2, keepdims=True))
    ds = pr * (dp - jnp.sum(pr * dp, axis=2, keepdims=True))
    prb = pr.astype(BF16).reshape(HEADS * WT, WT)
    dsb = ds.astype(BF16).reshape(HEADS * WT, WT)
    dq = own_columns(jnp.dot(dsb, k, preferred_element_type=F32)) * 0.125
    dk = lax.dot_general(dsb, q, TN, preferred_element_type=F32)
    dv = lax.dot_general(prb, d, TN, preferred_element_type=F32)
    return (dq, dk, dv, own_columns(jnp.dot(prb, v, preferred_element_type=F32))), ds


def marked(pieces, p):
    return sum(pieces[2 * p + r][64:80, :WIDTH].astype(F32)[8:16] for r in range(2))


def early_kernel(m0, m1, m2, m3, weight, wo, bias, proj, done, sums, tall, gall, rows, win):
    pieces = (m0, m1, m2, m3)
    stacked(pieces, tall, gall)
    odd = lax.bitwise_and(lax.axis_index("head"), 1)
    first = eastern(WIDTH)
    for m in range(4):
        y = projected(m, tall, gall, weight, wo)
        proj[m] = y
        rows[...] = y.astype(F32)
        for r in range(2):
            a = rows[pl.ds(pl.multiple_of(odd * 160 + r * ROWS, 8), 72), :]
            b = rows[pl.ds(pl.multiple_of(160 - odd * 160 + r * ROWS, 8), 72), :]
            win[m, r * 72 : (r + 1) * 72, :] = jnp.where(first, b, a)
    here, there = marked(pieces, 0), marked(pieces, 1)
    here, there = jnp.where(odd == 1, there, here), jnp.where(odd == 1, here, there)
    row = lax.broadcasted_iota(jnp.int32, (8, WIDTH), 0)
    marks = jnp.where(row < 4, here + pltpu.roll(there, 4, 0), 0.0).astype(BF16)
    results, ds = attended(marks, *(win[m].astype(BF16) for m in range(4)), bias[...])
    for m in range(4):
        done[m] = results[m]
    sums[...] = ds


def segment_sums(sums, highs, lows):
    total = jnp.zeros((64, 48), F32)
    ends = [turned(sums[head], 0.0) for head in range(HEADS)]
    for n in range(88):
        rows = []
        for head in range(HEADS):
            if n < 72:
                row = jnp.concatenate([sums[head, 2 * n : 2 * n + 1, :128], sums[head, 2 * n + 1 : 2 * n + 2, :128]], axis=1)
            else:
                row = ends[head][n - 72 : n - 71]
            rows.append(jnp.broadcast_to(row, (16, 256)).astype(BF16) * highs[n])
        total += lax.dot_general(jnp.concatenate(rows, axis=0), lows[n], NT, preferred_element_type=F32)
    return total


def bias_rows(x):
    top = x.astype(BF16).astype(F32)
    x = top + pltpu.roll(x - top, 64, 1)
    return jnp.concatenate([x[head * 16 : (head + 1) * 16] for head in range(HEADS)], axis=1).astype(BF16)


def bias_sum(s):
    x = jnp.concatenate([s[:, head * 128 : (head + 1) * 128] for head in range(HEADS)], axis=0)
    lane = lax.broadcasted_iota(jnp.int32, x.shape, 1)
    return jnp.where(lane < 64, x + pltpu.roll(x, 64, 1), 0.0)


def band_kernel(*refs):
    pieces = refs[:8]
    weight, wo, bias, early, done, early_sums, high_rows, low_rows, grads = refs[8:17]
    ways, pairs = refs[17:21], refs[21:23]
    tall, gall, qkv, rows, wins, outs, sums, att, labels, full = refs[23:]
    own = lax.axis_index("head")
    labels[...] = jnp.zeros_like(labels)
    row = lax.broadcasted_iota(jnp.int32, (8, WIDTH), 0)
    for p in range(4):
        shard = lax.bitwise_xor(own, p)
        before = lax.rem(shard + 3, 4)
        marks = marked(pieces, p)
        labels[shard] += jnp.where(row < 4, marks, 0.0)
        labels[before] += jnp.where(row < 4, pltpu.roll(marks, 4, 0), 0.0)
    stacked(pieces[:4], tall.at[:HALF, :], gall.at[:HALF, :])
    stacked(pieces[4:], tall.at[HALF:, :], gall.at[HALF:, :])
    for m in range(4):
        rows[:HALF, :] = early[m].astype(F32)
        rows[HALF:, :] = projected(m, tall.at[HALF:, :], gall.at[HALF:, :], weight, wo).astype(F32)
        to_windows(rows, wins, own)
        if m < 3:
            qkv[m] = wins[...].astype(BF16)
    near = lax.bitwise_and(own, 2)
    for m in range(4):
        outs[m, near] = done[m]
    sums[...] = early_sums[...]
    for i in range(1, 4):
        w = lax.rem(near + i, 4)
        marks = labels[w].astype(BF16)
        results, ds = attended(marks, qkv[0, w], qkv[1, w], qkv[2, w], wins[w].astype(BF16), bias[...])
        sums[...] += ds
        for m in range(4):
            outs[m, w] = results[m]
    for m in range(4):
        from_windows(outs.at[m], rows, own)
        if m < 3:
            grads[:, m * WIDTH : (m + 1) * WIDTH] = rows[...].astype(BF16)
    att[...] = rows[...].astype(BF16)

    found = segment_sums(sums, high_rows, low_rows)
    found = bias_rows(jnp.concatenate([found, jnp.zeros((64, 80), F32)], axis=1))

    full[:, : 3 * WIDTH] = lax.dot_general(tall[...], grads[...], TN, preferred_element_type=F32).astype(BF16)
    full[:, 3 * WIDTH :] = lax.dot_general(gall[...], att[...], TN, preferred_element_type=F32).astype(BF16)
    lat = lax.axis_index("lat")
    y, z = lax.rem(lat // NZ, NY), lax.rem(lat, 2)
    for d, out in enumerate(ways):
        out[256:272, :512] = found
        out[256:272, 512:] = jnp.zeros((16, 128), BF16)
        for half in range(2):
            at = pl.ds(pl.multiple_of(half * 512 + lax.rem(y + d, NY) * 128, 128), 128)
            out[half * 128 : (half + 1) * 128, :] = full[at, :640]
    for i, out in enumerate(pairs):
        start = lax.bitwise_xor(z, i) * 16
        for b in range(32):
            at = pl.ds(pl.multiple_of(start + (b // 4) * 128 + (b % 4) * 32, 16), 16)
            out[b * 16 : (b + 1) * 16, :] = full[at, 640:]


def input_kernel(grads, weight, near, far, given):
    total = jnp.zeros((ALL, D), F32)
    for m in range(3):
        total += lax.dot_general(
            grads[:, m * WIDTH : (m + 1) * WIDTH], weight[m], NT, preferred_element_type=F32
        )
    for p, out in enumerate((near.at[...], given.at[:WT, :], far.at[...], given.at[WT:, :])):
        start = p * 2 * ROWS
        both = jnp.concatenate([total[start : start + 72], total[start + ROWS : start + ROWS + 72]], axis=0)
        out[...] = both.astype(BF16)


def stage_rows(parts, rows, columns=slice(None)):
    total = parts[0][rows, columns].astype(F32)
    for part in parts[1:]:
        total += part[rows, columns].astype(F32)
    return total


def place():
    lat = lax.axis_index("lat")
    return lat // (NY * NZ), lax.rem(lat // NZ, NY), lax.rem(lat, NZ)


def after_pairs_kernel(*refs):
    pairs, outs = refs[:2], refs[2:]
    y = place()[1]
    for d, out in enumerate(outs):
        to = lax.rem(y + d, NY) * 64
        for half in range(2):
            rows = pl.ds(pl.multiple_of(half * 256 + to, 64), 64)
            out[half * 64 : (half + 1) * 64, :] = stage_rows(pairs, rows).astype(BF16)


def second_kernel(*refs):
    ways, late, (near, given, more), outs, (high, low) = refs[:4], refs[4:8], refs[8:11], refs[11:15], refs[15:]
    total = near[...].astype(F32) + given[...].astype(F32) + more[...].astype(F32)
    high[...] = total[:72]
    low[...] = total[72:].astype(BF16)
    x, _, z = place()
    found = bias_rows(bias_sum(stage_rows(ways, pl.ds(256, 16), slice(0, 512))))
    for i, out in enumerate(outs):
        to = lax.bitwise_xor(x, i // 2)
        start = to * 128 + lax.bitwise_xor(lax.rem(z, 2), i % 2) * 16
        for k in range(4):
            rows = pl.ds(pl.multiple_of(start + k * 32, 16), 16)
            out[k * 16 : (k + 1) * 16, :640] = stage_rows(ways, rows).astype(BF16)
        out[64:, :512] = found
        out[64:, 512:640] = jnp.zeros((16, 128), BF16)
        if i % 2 == 0:
            out[:64, 640:] = stage_rows(late, pl.ds(pl.multiple_of(to * 64, 64), 64)).astype(BF16)
            out[64:, 640:] = jnp.zeros((16, 384), BF16)


def third_kernel(a, b, c, d, *outs):
    z = place()[2] // 2
    found = bias_rows(bias_sum(stage_rows((a, b, c, d), pl.ds(64, 16), slice(0, 512))))
    for e, out in enumerate(outs):
        rows = pl.ds(pl.multiple_of(lax.rem(z + e, 4) * 16, 16), 16)
        out[:16, :640] = stage_rows((a, b, c, d), rows, slice(0, 640)).astype(BF16)
        out[:16, 640:] = stage_rows((a, c), rows, slice(640, 1024)).astype(BF16)
        out[16:, :512] = found
        out[16:, 512:] = jnp.zeros_like(found)


def last_kernel(a, b, c, d, qkv, out, bias):
    parts = (a, b, c, d)
    total = stage_rows(parts, pl.ds(0, 16))
    for m in range(3):
        qkv[m] = total[:, m * WIDTH : (m + 1) * WIDTH]
    out[...] = total[:, 3 * WIDTH :]
    found = bias_sum(stage_rows(parts, pl.ds(16, 16))[:, :512])
    for head in range(HEADS):
        for c in range(16):
            stop = min(c * 48 + 48, NB)
            bias[head : head + 1, c * 48 : stop] = found[head * 16 + c : head * 16 + c + 1, : stop - c * 48]


def load_kernel(*refs):
    sources, targets, arrived = refs[:3], refs[3:6], refs[6]
    copies = [pltpu.make_async_copy(a, b, arrived.at[i]) for i, (a, b) in enumerate(zip(sources, targets))]
    for copy in copies:
        copy.start()
    for copy in copies:
        copy.wait()


def label_rows(labels, first):
    row = lax.broadcasted_iota(jnp.int32, (8, 72), 0)
    col = lax.broadcasted_iota(jnp.int32, (8, 72), 1)
    labels = labels.transpose(0, 2, 1).reshape(1, 72)
    hit = (row % 4 == labels) & ((row >= 4) == (col % 24 < 12))
    return jnp.pad(hit.astype(BF16), ((0, 0), (first, D - 72 - first)))


def shards(tokens, output_grad, region_labels, qkv_weight, out_weight, bias_table, bias_index):
    core = functools.partial(sent, axis="head", to=lambda i: i ^ 1)
    across = functools.partial(sent, axis="head", to=lambda i: i ^ 2)
    back = functools.partial(sent, axis="lat", to=lambda i: (i - 1) % 64)
    onward = functools.partial(sent, axis="lat", to=lambda i: (i + 1) % 64)

    inputs = tokens.transpose(0, 2, 1, 3), output_grad.transpose(0, 2, 1, 3), region_labels
    loaded = pl.pallas_call(
        load_kernel,
        out_shape=[shape(x.shape, x.dtype) for x in inputs],
        in_specs=[pl.BlockSpec(memory_space=pl.ANY)] * 3,
        out_specs=[pl.BlockSpec(memory_space=pltpu.VMEM)] * 3,
        scratch_shapes=[pltpu.SemaphoreType.DMA((3,))],
        compiler_params=pltpu.CompilerParams(vmem_limit_bytes=8 * 2**20),
    )(*inputs)

    def message(r):
        rows = slice(3 - 3 * r, 6 - 3 * r)
        t, g = (x[rows].reshape(72, D) for x in loaded[:2])
        return jnp.concatenate([t, label_rows(loaded[2][rows], 72 * r), g])

    high = message(0)
    high, qkv_weight, out_weight, bias_index = lax.optimization_barrier((high, qkv_weight, out_weight, bias_index))
    low = back(message(1))
    far_high = across(high)

    table = jnp.pad(bias_table.T, ((0, 0), (0, 9)))
    bias, high_rows, low_rows = call(
        bias_kernel,
        (shape((HEADS, WT, WT), F32), shape((88, 16, 256), BF16), shape((88, 48, 256), BF16)),
        (),
        10**8,
        4 * 10**6,
    )(table, bias_index, jnp.asarray(window_order(), BF16))
    low, bias, high_rows, low_rows = lax.optimization_barrier((low, bias, high_rows, low_rows))
    far_low = across(low)
    near = (high, low, core(high), core(low))

    early, done, sums = call(
        early_kernel,
        (shape((4, HALF, WIDTH), BF16), shape((4, WT, WIDTH), F32), shape((HEADS, WT, WT), F32)),
        [
            pltpu.VMEM((HALF, D), BF16),
            pltpu.VMEM((HALF, D), BF16),
            pltpu.VMEM((HALF, WIDTH), F32),
            pltpu.VMEM((4, WT, WIDTH), F32),
        ],
        10**9,
        5 * 10**6,
        16,
    )(*near, qkv_weight, out_weight, bias)
    far_low, early, done, sums = lax.optimization_barrier((far_low, early, done, sums))
    far = (far_high, far_low, core(far_high), core(far_low))

    grads, *blocks = call(
        band_kernel,
        (shape((ALL, 3 * WIDTH), BF16),)
        + (shape((272, 640), BF16),) * 4
        + (shape((512, 384), BF16),) * 2,
        [
            pltpu.VMEM((ALL, D), BF16),
            pltpu.VMEM((ALL, D), BF16),
            pltpu.VMEM((3, 4, WT, WIDTH), BF16),
            pltpu.VMEM((ALL, WIDTH), F32),
            pltpu.VMEM((4, WT, WIDTH), F32),
            pltpu.VMEM((4, 4, WT, WIDTH), F32),
            pltpu.VMEM((HEADS, WT, WT), F32),
            pltpu.VMEM((ALL, WIDTH), BF16),
            pltpu.VMEM((4, 8, WIDTH), F32),
            pltpu.VMEM((D, D), BF16),
        ],
        3 * 10**9,
        10**7,
        24,
    )(*near, *far, qkv_weight, out_weight, bias, early, done, sums, high_rows, low_rows)

    def by_y(parts):
        far = sent(parts[2], "lat", moved(0, 2, 0))
        return [parts[0], sent(parts[1], "lat", moved(0, 1, 0)), far, sent(parts[3], "lat", moved(0, 3, 0))]

    def swapped(parts, dx, dz):
        return [parts[0], sent(parts[1], "lat", paired(dx, dz))]

    pairs = swapped(blocks[4:], 0, 1)
    ways = by_y(blocks[:4])

    near, far, given = call(
        input_kernel, (shape((WT, D), BF16), shape((WT, D), BF16), shape((2 * WT, D), BF16)), (), 10**9, 5 * 10**6
    )(grads, qkv_weight)
    given = core(given)
    far = (far.astype(F32) + given[WT:].astype(F32)).astype(BF16)
    more = across(far)
    parts = call(after_pairs_kernel, (shape((128, 384), BF16),) * 4, (), 10**6, 10**6, 8)(*pairs)
    late = by_y(parts)
    ways, late, more = lax.optimization_barrier((ways, late, more))
    full, part = shape((80, D), BF16), shape((80, 640), BF16)
    *parts, near, low = call(
        second_kernel, (full, part, full, part, shape((72, D), F32), shape((72, D), BF16)), (), 10**6, 4 * 10**6, 8
    )(*ways, *late, near, given[:WT], more)
    parts = [parts[0]] + [sent(parts[i], "lat", paired(i // 2, i % 2)) for i in range(1, 4)]
    parts, low = lax.optimization_barrier((parts, onward(low)))
    input_grad = jnp.concatenate([low.astype(F32), near]).reshape(6, 12, 2, D).transpose(0, 2, 1, 3)
    parts = call(third_kernel, (shape((32, D), BF16),) * 4, (), 10**6, 10**6, 8)(*parts)
    far = sent(parts[2], "lat", moved(0, 0, 4))
    got = [parts[0], sent(parts[1], "lat", moved(0, 0, 2)), far, sent(parts[3], "lat", moved(0, 0, 6))]
    got, input_grad = lax.optimization_barrier((got, input_grad))
    qkv_grad, out_grad, bias_grad = call(
        last_kernel,
        (shape((3, 16, WIDTH), F32), shape((16, WIDTH), F32), shape((HEADS, NB), F32)),
        (),
        10**6,
        10**6,
        8,
    )(*got)
    return input_grad, qkv_grad, out_grad.T, bias_grad.T


def solution(mesh):
    return jax.shard_map(
        shards,
        mesh=mesh,
        in_specs=(
            P("lat", None, "head", None),
            P("lat", None, "head", None),
            P("lat", None, "head"),
            P(None, None, "head"),
            P("head", None),
            P(None, "head"),
            P(),
        ),
        out_specs=(
            P("lat", None, "head", None),
            P(None, "lat", "head"),
            P("head", "lat"),
            P(None, "head"),
        ),
        check_vma=False,
    )
```

```python
import functools

import jax
import jax.numpy as jnp
import numpy as np
from jax import lax
from jax.experimental import pallas as pl
from jax.experimental.pallas import tpu as pltpu
from jax.sharding import PartitionSpec as P

D = 1024
HD = 64
HEADS = 4
WIDTH = 256
WT = 144
NB = 759
ROWS = 80
BLOCKS = 8
ALL = BLOCKS * ROWS
HALF = 320
NY = 4
NZ = 8
F32 = jnp.float32
BF16 = jnp.bfloat16
NT = (((1,), (1,)), ((), ()))
TN = (((0,), (0,)), ((), ()))


def sent(x, axis, to):
    size = lax.axis_size(axis)
    return lax.ppermute(x, axis, [(i, to(i)) for i in range(size)])


def lat_of(x, y, z):
    return (x * NY + y % NY) * NZ + z % NZ


def moved(dx, dy, dz):
    def to(i):
        x, y, z = i // (NY * NZ), i // NZ % NY, i % NZ
        return lat_of(x ^ dx, y + dy, z + dz)

    return to


def paired(dx, dz):
    def to(i):
        x, y, z = i // (NY * NZ), i // NZ % NY, i % NZ
        return lat_of(x ^ dx, y, z ^ dz)

    return to


def call(kernel, out, args, flops, moved_bytes, vmem=16):
    return pl.pallas_call(
        kernel,
        out_shape=out,
        scratch_shapes=args,
        compiler_params=pltpu.CompilerParams(vmem_limit_bytes=vmem * 2**20),
        cost_estimate=pl.CostEstimate(flops=flops, bytes_accessed=moved_bytes, transcendentals=0),
    )


def shape(dims, dtype):
    return jax.ShapeDtypeStruct(dims, dtype)


def window_order():
    order = np.zeros((WT, WT), np.float32)
    for row in range(6):
        for half in range(2):
            for lon in range(6):
                for lev in range(2):
                    n = row * 24 + half * 12 + lon * 2 + lev
                    order[n, row * 24 + (1 - lev) * 12 + (1 - half) * 6 + lon] = 1
    return order


def turned(x, fill):
    x = jnp.concatenate([x[:, 128:], jnp.full((WT, 112), fill, F32)], axis=1)
    x = jnp.concatenate([x, jnp.full((112, 128), fill, F32)], axis=0)
    return jnp.transpose(x)[:16]


def bias_kernel(table, index, order, bias, highs, lows):
    idx = index[...].astype(F32)
    high = jnp.floor(idx * (1.0 / 32.0))
    low = idx - high * 32.0
    perm = order[...]

    def reordered(x):
        y = jnp.dot(perm, x.astype(BF16), preferred_element_type=F32).astype(BF16)
        return lax.dot_general(y, perm, NT, preferred_element_type=F32)

    own_f = reordered(high) * 32.0 + reordered(low)
    own = own_f.astype(jnp.int32)
    ends = turned(own_f, -1.0).astype(jnp.int32)

    def found(head, places):
        chunk = lax.shift_right_logical(places, 7)
        lane = lax.bitwise_and(places, 127)
        total = jnp.zeros(places.shape, F32)
        for c in range(6):
            row = jnp.broadcast_to(table[head : head + 1, c * 128 : (c + 1) * 128], places.shape)
            got = jnp.take_along_axis(row, lane, axis=1, mode="promise_in_bounds")
            total = jnp.where(chunk == c, got, total)
        return total

    for head in range(HEADS):
        bias[head, :, :128] = found(head, own[:, :128])
        rest = jnp.concatenate([found(head, ends[:, :128]), found(head, ends[:, 128:])], axis=1)
        rest = jnp.transpose(jnp.concatenate([rest, jnp.zeros((112, 256), F32)], axis=0))
        bias[head, :, 128:] = rest[:WT, :16]

    high_row = lax.broadcasted_iota(jnp.int32, (16, 256), 0)
    low_row = lax.broadcasted_iota(jnp.int32, (48, 256), 0)
    for n in range(88):
        if n < 72:
            places = jnp.concatenate([own[2 * n : 2 * n + 1, :128], own[2 * n + 1 : 2 * n + 2, :128]], axis=1)
        else:
            places = ends[n - 72 : n - 71]
        upper = jnp.floor(places.astype(F32) * (1.0 / 48.0) + 0.01).astype(jnp.int32)
        highs[n] = (high_row == upper).astype(F32).astype(BF16)
        lows[n] = (low_row == places - upper * 48).astype(F32).astype(BF16)


def eastern(width):
    row = lax.broadcasted_iota(jnp.int32, (72, width), 0)
    return lax.rem(row, 24) < 12


def to_windows(rows, wins, own):
    first = eastern(rows.shape[1])
    for w in range(4):
        near = lax.bitwise_xor(own, w) * 2 * ROWS
        east = lax.bitwise_xor(own, (w + 1) % 4) * 2 * ROWS
        for r in range(2):
            a = rows[pl.ds(pl.multiple_of(near + r * ROWS, 8), 72), :]
            b = rows[pl.ds(pl.multiple_of(east + r * ROWS, 8), 72), :]
            wins[w, r * 72 : (r + 1) * 72, :] = jnp.where(first, b, a)


def from_windows(wins, rows, own):
    first = eastern(rows.shape[1])
    for s in range(4):
        start = lax.bitwise_xor(own, s) * 2 * ROWS
        for r in range(2):
            a = wins[s, r * 72 : (r + 1) * 72, :]
            b = wins[(s + 3) % 4, r * 72 : (r + 1) * 72, :]
            at = pl.multiple_of(start + r * ROWS, 8)
            rows[pl.ds(at, 72), :] = jnp.where(first, b, a)
            rows[pl.ds(pl.multiple_of(at + 72, 8), 8), :] = jnp.zeros((8, rows.shape[1]), F32)


def by_head(x):
    lane = lax.shift_right_logical(lax.broadcasted_iota(jnp.int32, (1, WIDTH), 1), 6)
    return jnp.concatenate([x * (lane == head).astype(F32).astype(BF16) for head in range(HEADS)], axis=0)


def own_columns(x):
    first = lax.broadcasted_iota(jnp.int32, (WT, 128), 1) < HD
    part = [x[head * WT : (head + 1) * WT, head // 2 * 128 : head // 2 * 128 + 128] for head in range(HEADS)]
    return jnp.concatenate([jnp.where(first, part[0], part[1]), jnp.where(first, part[2], part[3])], axis=1)


def stacked(pieces, tall, gall):
    for p, piece in enumerate(pieces):
        tall[p * ROWS : (p + 1) * ROWS, :] = piece[:ROWS, :]
        rows = jnp.concatenate([piece[ROWS:, :].astype(F32), jnp.zeros((8, D), F32)], axis=0)
        gall[p * ROWS : (p + 1) * ROWS, :] = rows.astype(BF16)


def projected(m, tall, gall, weight, wo):
    if m < 3:
        y = jnp.dot(tall[...], weight[m], preferred_element_type=F32)
    else:
        y = lax.dot_general(gall[...], wo[...], NT, preferred_element_type=F32)
    return y.astype(BF16)


def attended(marks, q, k, v, d, bias):
    same = lax.dot_general(marks, marks, TN, preferred_element_type=F32)[:WT, :WT] > 0.5
    same = jnp.where(same, 0.0, -jnp.inf)
    q = by_head(q * jnp.asarray(0.125, BF16))
    d = by_head(d)
    s = lax.dot_general(q, k, NT, preferred_element_type=F32).reshape(HEADS, WT, WT)
    dp = lax.dot_general(d, v, NT, preferred_element_type=F32).reshape(HEADS, WT, WT)
    s = s + bias + same[None]
    e = jnp.exp(s - jnp.max(s, axis=2, keepdims=True))
    pr = e * (1.0 / jnp.sum(e, axis=2, keepdims=True))
    ds = pr * (dp - jnp.sum(pr * dp, axis=2, keepdims=True))
    prb = pr.astype(BF16).reshape(HEADS * WT, WT)
    dsb = ds.astype(BF16).reshape(HEADS * WT, WT)
    dq = own_columns(jnp.dot(dsb, k, preferred_element_type=F32)) * 0.125
    dk = lax.dot_general(dsb, q, TN, preferred_element_type=F32)
    dv = lax.dot_general(prb, d, TN, preferred_element_type=F32)
    return (dq, dk, dv, own_columns(jnp.dot(prb, v, preferred_element_type=F32))), ds


def marked(pieces, p):
    return sum(pieces[2 * p + r][64:80, :WIDTH].astype(F32)[8:16] for r in range(2))


def early_kernel(m0, m1, m2, m3, weight, wo, bias, proj, done, sums, tall, gall, rows, win):
    pieces = (m0, m1, m2, m3)
    stacked(pieces, tall, gall)
    odd = lax.bitwise_and(lax.axis_index("head"), 1)
    first = eastern(WIDTH)
    for m in range(4):
        y = projected(m, tall, gall, weight, wo)
        proj[m] = y
        rows[...] = y.astype(F32)
        for r in range(2):
            a = rows[pl.ds(pl.multiple_of(odd * 160 + r * ROWS, 8), 72), :]
            b = rows[pl.ds(pl.multiple_of(160 - odd * 160 + r * ROWS, 8), 72), :]
            win[m, r * 72 : (r + 1) * 72, :] = jnp.where(first, b, a)
    here, there = marked(pieces, 0), marked(pieces, 1)
    here, there = jnp.where(odd == 1, there, here), jnp.where(odd == 1, here, there)
    row = lax.broadcasted_iota(jnp.int32, (8, WIDTH), 0)
    marks = jnp.where(row < 4, here + pltpu.roll(there, 4, 0), 0.0).astype(BF16)
    results, ds = attended(marks, *(win[m].astype(BF16) for m in range(4)), bias[...])
    for m in range(4):
        done[m] = results[m]
    sums[...] = ds


def segment_sums(sums, highs, lows):
    total = jnp.zeros((64, 48), F32)
    ends = [turned(sums[head], 0.0) for head in range(HEADS)]
    for n in range(88):
        rows = []
        for head in range(HEADS):
            if n < 72:
                row = jnp.concatenate([sums[head, 2 * n : 2 * n + 1, :128], sums[head, 2 * n + 1 : 2 * n + 2, :128]], axis=1)
            else:
                row = ends[head][n - 72 : n - 71]
            rows.append(jnp.broadcast_to(row, (16, 256)).astype(BF16) * highs[n])
        total += lax.dot_general(jnp.concatenate(rows, axis=0), lows[n], NT, preferred_element_type=F32)
    return total


def bias_rows(x):
    top = x.astype(BF16).astype(F32)
    x = top + pltpu.roll(x - top, 64, 1)
    return jnp.concatenate([x[head * 16 : (head + 1) * 16] for head in range(HEADS)], axis=1).astype(BF16)


def bias_sum(s):
    x = jnp.concatenate([s[:, head * 128 : (head + 1) * 128] for head in range(HEADS)], axis=0)
    lane = lax.broadcasted_iota(jnp.int32, x.shape, 1)
    return jnp.where(lane < 64, x + pltpu.roll(x, 64, 1), 0.0)


def band_kernel(*refs):
    pieces = refs[:8]
    weight, wo, bias, early, done, early_sums, high_rows, low_rows, grads = refs[8:17]
    ways, pairs = refs[17:21], refs[21:23]
    tall, gall, qkv, rows, wins, outs, sums, att, labels, full = refs[23:]
    own = lax.axis_index("head")
    labels[...] = jnp.zeros_like(labels)
    row = lax.broadcasted_iota(jnp.int32, (8, WIDTH), 0)
    for p in range(4):
        shard = lax.bitwise_xor(own, p)
        before = lax.rem(shard + 3, 4)
        marks = marked(pieces, p)
        labels[shard] += jnp.where(row < 4, marks, 0.0)
        labels[before] += jnp.where(row < 4, pltpu.roll(marks, 4, 0), 0.0)
    stacked(pieces[:4], tall.at[:HALF, :], gall.at[:HALF, :])
    stacked(pieces[4:], tall.at[HALF:, :], gall.at[HALF:, :])
    for m in range(4):
        rows[:HALF, :] = early[m].astype(F32)
        rows[HALF:, :] = projected(m, tall.at[HALF:, :], gall.at[HALF:, :], weight, wo).astype(F32)
        to_windows(rows, wins, own)
        if m < 3:
            qkv[m] = wins[...].astype(BF16)
    near = lax.bitwise_and(own, 2)
    for m in range(4):
        outs[m, near] = done[m]
    sums[...] = early_sums[...]
    for i in range(1, 4):
        w = lax.rem(near + i, 4)
        marks = labels[w].astype(BF16)
        results, ds = attended(marks, qkv[0, w], qkv[1, w], qkv[2, w], wins[w].astype(BF16), bias[...])
        sums[...] += ds
        for m in range(4):
            outs[m, w] = results[m]
    for m in range(4):
        from_windows(outs.at[m], rows, own)
        if m < 3:
            grads[:, m * WIDTH : (m + 1) * WIDTH] = rows[...].astype(BF16)
    att[...] = rows[...].astype(BF16)

    found = segment_sums(sums, high_rows, low_rows)
    found = bias_rows(jnp.concatenate([found, jnp.zeros((64, 80), F32)], axis=1))

    full[:, : 3 * WIDTH] = lax.dot_general(tall[...], grads[...], TN, preferred_element_type=F32).astype(BF16)
    full[:, 3 * WIDTH :] = lax.dot_general(gall[...], att[...], TN, preferred_element_type=F32).astype(BF16)
    lat = lax.axis_index("lat")
    y, z = lax.rem(lat // NZ, NY), lax.rem(lat, 2)
    for d, out in enumerate(ways):
        out[256:272, :512] = found
        out[256:272, 512:] = jnp.zeros((16, 128), BF16)
        for half in range(2):
            at = pl.ds(pl.multiple_of(half * 512 + lax.rem(y + d, NY) * 128, 128), 128)
            out[half * 128 : (half + 1) * 128, :] = full[at, :640]
    for i, out in enumerate(pairs):
        start = lax.bitwise_xor(z, i) * 16
        for b in range(32):
            at = pl.ds(pl.multiple_of(start + (b // 4) * 128 + (b % 4) * 32, 16), 16)
            out[b * 16 : (b + 1) * 16, :] = full[at, 640:]


def input_kernel(grads, weight, near, far, given):
    total = jnp.zeros((ALL, D), F32)
    for m in range(3):
        total += lax.dot_general(
            grads[:, m * WIDTH : (m + 1) * WIDTH], weight[m], NT, preferred_element_type=F32
        )
    for p, out in enumerate((near.at[...], given.at[:WT, :], far.at[...], given.at[WT:, :])):
        start = p * 2 * ROWS
        both = jnp.concatenate([total[start : start + 72], total[start + ROWS : start + ROWS + 72]], axis=0)
        out[...] = both.astype(BF16)


def stage_rows(parts, rows, columns=slice(None)):
    total = parts[0][rows, columns].astype(F32)
    for part in parts[1:]:
        total += part[rows, columns].astype(F32)
    return total


def place():
    lat = lax.axis_index("lat")
    return lat // (NY * NZ), lax.rem(lat // NZ, NY), lax.rem(lat, NZ)


def after_pairs_kernel(*refs):
    pairs, outs = refs[:2], refs[2:]
    y = place()[1]
    for d, out in enumerate(outs):
        to = lax.rem(y + d, NY) * 64
        for half in range(2):
            rows = pl.ds(pl.multiple_of(half * 256 + to, 64), 64)
            out[half * 64 : (half + 1) * 64, :] = stage_rows(pairs, rows).astype(BF16)


def second_kernel(*refs):
    ways, late, outs = refs[:4], refs[4:8], refs[8:]
    x, _, z = place()
    found = bias_rows(bias_sum(stage_rows(ways, pl.ds(256, 16), slice(0, 512))))
    for i, out in enumerate(outs):
        to = lax.bitwise_xor(x, i // 2)
        start = to * 128 + lax.bitwise_xor(lax.rem(z, 2), i % 2) * 16
        for k in range(4):
            rows = pl.ds(pl.multiple_of(start + k * 32, 16), 16)
            out[k * 16 : (k + 1) * 16, :640] = stage_rows(ways, rows).astype(BF16)
        out[64:, :512] = found
        out[64:, 512:640] = jnp.zeros((16, 128), BF16)
        if i % 2 == 0:
            out[:64, 640:] = stage_rows(late, pl.ds(pl.multiple_of(to * 64, 64), 64)).astype(BF16)
            out[64:, 640:] = jnp.zeros((16, 384), BF16)


def third_kernel(a, b, c, d, near, given, more, high, low, *outs):
    total = near[...].astype(F32) + given[...].astype(F32) + more[...].astype(F32)
    high[...] = total[:72]
    low[...] = total[72:].astype(BF16)
    z = place()[2] // 2
    found = bias_rows(bias_sum(stage_rows((a, b, c, d), pl.ds(64, 16), slice(0, 512))))
    for e, out in enumerate(outs):
        rows = pl.ds(pl.multiple_of(lax.rem(z + e, 4) * 16, 16), 16)
        out[:16, :640] = stage_rows((a, b, c, d), rows, slice(0, 640)).astype(BF16)
        out[:16, 640:] = stage_rows((a, c), rows, slice(640, 1024)).astype(BF16)
        out[16:, :512] = found
        out[16:, 512:] = jnp.zeros_like(found)


def last_kernel(a, b, c, d, qkv, out, bias):
    parts = (a, b, c, d)
    total = stage_rows(parts, pl.ds(0, 16))
    for m in range(3):
        qkv[m] = total[:, m * WIDTH : (m + 1) * WIDTH]
    out[...] = total[:, 3 * WIDTH :]
    found = bias_sum(stage_rows(parts, pl.ds(16, 16))[:, :512])
    for head in range(HEADS):
        for c in range(16):
            stop = min(c * 48 + 48, NB)
            bias[head : head + 1, c * 48 : stop] = found[head * 16 + c : head * 16 + c + 1, : stop - c * 48]


def load_kernel(*refs):
    sources, targets, arrived = refs[:3], refs[3:6], refs[6]
    copies = [pltpu.make_async_copy(a, b, arrived.at[i]) for i, (a, b) in enumerate(zip(sources, targets))]
    for copy in copies:
        copy.start()
    for copy in copies:
        copy.wait()


def label_rows(labels, first):
    row = lax.broadcasted_iota(jnp.int32, (8, 72), 0)
    col = lax.broadcasted_iota(jnp.int32, (8, 72), 1)
    labels = labels.transpose(0, 2, 1).reshape(1, 72)
    hit = (row % 4 == labels) & ((row >= 4) == (col % 24 < 12))
    return jnp.pad(hit.astype(BF16), ((0, 0), (first, D - 72 - first)))


def shards(tokens, output_grad, region_labels, qkv_weight, out_weight, bias_table, bias_index):
    core = functools.partial(sent, axis="head", to=lambda i: i ^ 1)
    across = functools.partial(sent, axis="head", to=lambda i: i ^ 2)
    back = functools.partial(sent, axis="lat", to=lambda i: (i - 1) % 64)
    onward = functools.partial(sent, axis="lat", to=lambda i: (i + 1) % 64)

    inputs = tokens.transpose(0, 2, 1, 3), output_grad.transpose(0, 2, 1, 3), region_labels
    loaded = pl.pallas_call(
        load_kernel,
        out_shape=[shape(x.shape, x.dtype) for x in inputs],
        in_specs=[pl.BlockSpec(memory_space=pl.ANY)] * 3,
        out_specs=[pl.BlockSpec(memory_space=pltpu.VMEM)] * 3,
        scratch_shapes=[pltpu.SemaphoreType.DMA((3,))],
        compiler_params=pltpu.CompilerParams(vmem_limit_bytes=8 * 2**20),
    )(*inputs)

    def message(r):
        rows = slice(3 - 3 * r, 6 - 3 * r)
        t, g = (x[rows].reshape(72, D) for x in loaded[:2])
        return jnp.concatenate([t, label_rows(loaded[2][rows], 72 * r), g])

    high = message(0)
    high, qkv_weight, out_weight, bias_index = lax.optimization_barrier((high, qkv_weight, out_weight, bias_index))
    low = back(message(1))
    far_high = across(high)

    table = jnp.pad(bias_table.T, ((0, 0), (0, 9)))
    bias, high_rows, low_rows = call(
        bias_kernel,
        (shape((HEADS, WT, WT), F32), shape((88, 16, 256), BF16), shape((88, 48, 256), BF16)),
        (),
        10**8,
        4 * 10**6,
    )(table, bias_index, jnp.asarray(window_order(), BF16))
    low, bias, high_rows, low_rows = lax.optimization_barrier((low, bias, high_rows, low_rows))
    far_low = across(low)
    near = (high, low, core(high), core(low))

    early, done, sums = call(
        early_kernel,
        (shape((4, HALF, WIDTH), BF16), shape((4, WT, WIDTH), F32), shape((HEADS, WT, WT), F32)),
        [
            pltpu.VMEM((HALF, D), BF16),
            pltpu.VMEM((HALF, D), BF16),
            pltpu.VMEM((HALF, WIDTH), F32),
            pltpu.VMEM((4, WT, WIDTH), F32),
        ],
        10**9,
        5 * 10**6,
        16,
    )(*near, qkv_weight, out_weight, bias)
    far_low, early, done, sums = lax.optimization_barrier((far_low, early, done, sums))
    far = (far_high, far_low, core(far_high), core(far_low))

    grads, *blocks = call(
        band_kernel,
        (shape((ALL, 3 * WIDTH), BF16),)
        + (shape((272, 640), BF16),) * 4
        + (shape((512, 384), BF16),) * 2,
        [
            pltpu.VMEM((ALL, D), BF16),
            pltpu.VMEM((ALL, D), BF16),
            pltpu.VMEM((3, 4, WT, WIDTH), BF16),
            pltpu.VMEM((ALL, WIDTH), F32),
            pltpu.VMEM((4, WT, WIDTH), F32),
            pltpu.VMEM((4, 4, WT, WIDTH), F32),
            pltpu.VMEM((HEADS, WT, WT), F32),
            pltpu.VMEM((ALL, WIDTH), BF16),
            pltpu.VMEM((4, 8, WIDTH), F32),
            pltpu.VMEM((D, D), BF16),
        ],
        3 * 10**9,
        10**7,
        24,
    )(*near, *far, qkv_weight, out_weight, bias, early, done, sums, high_rows, low_rows)

    def by_y(parts):
        far = sent(parts[2], "lat", moved(0, 2, 0))
        return [parts[0], sent(parts[1], "lat", moved(0, 1, 0)), far, sent(parts[3], "lat", moved(0, 3, 0))]

    def swapped(parts, dx, dz):
        return [parts[0], sent(parts[1], "lat", paired(dx, dz))]

    pairs = swapped(blocks[4:], 0, 1)
    ways = by_y(blocks[:4])

    near, far, given = call(
        input_kernel, (shape((WT, D), BF16), shape((WT, D), BF16), shape((2 * WT, D), BF16)), (), 10**9, 5 * 10**6
    )(grads, qkv_weight)
    given = core(given)
    far = (far.astype(F32) + given[WT:].astype(F32)).astype(BF16)
    more = across(far)
    parts = call(after_pairs_kernel, (shape((128, 384), BF16),) * 4, (), 10**6, 10**6, 8)(*pairs)
    late = by_y(parts)
    full, part = shape((80, D), BF16), shape((80, 640), BF16)
    parts = call(second_kernel, (full, part, full, part), (), 10**6, 4 * 10**6, 8)(*ways, *late)
    parts = [parts[0]] + [sent(parts[i], "lat", paired(i // 2, i % 2)) for i in range(1, 4)]
    near, low, *parts = call(
        third_kernel,
        (shape((72, D), F32), shape((72, D), BF16)) + (shape((32, D), BF16),) * 4,
        (),
        10**6,
        2 * 10**6,
        8,
    )(*parts, near, given[:WT], more)
    low = onward(low)
    input_grad = jnp.concatenate([low.astype(F32), near]).reshape(6, 12, 2, D).transpose(0, 2, 1, 3)
    far = sent(parts[2], "lat", moved(0, 0, 4))
    got = [parts[0], sent(parts[1], "lat", moved(0, 0, 2)), far, sent(parts[3], "lat", moved(0, 0, 6))]
    got, input_grad = lax.optimization_barrier((got, input_grad))
    qkv_grad, out_grad, bias_grad = call(
        last_kernel,
        (shape((3, 16, WIDTH), F32), shape((16, WIDTH), F32), shape((HEADS, NB), F32)),
        (),
        10**6,
        10**6,
        8,
    )(*got)
    return input_grad, qkv_grad, out_grad.T, bias_grad.T


def solution(mesh):
    return jax.shard_map(
        shards,
        mesh=mesh,
        in_specs=(
            P("lat", None, "head", None),
            P("lat", None, "head", None),
            P("lat", None, "head"),
            P(None, None, "head"),
            P("head", None),
            P(None, "head"),
            P(),
        ),
        out_specs=(
            P("lat", None, "head", None),
            P(None, "lat", "head"),
            P("head", "lat"),
            P(None, "head"),
        ),
        check_vma=False,
    )
```
